128 devices in a mesh: dp: 32 (over z, x, core), row: 2 (over y_hi), col: 2 (over y_lo).
Axes of the slice: x: 4, y: 4 (y_hi: 2, y_lo: 2; y = y_hi * 2 + y_lo), z: 4, core: 2. Of those that a mesh axis runs over, the one named last changes fastest.
Arguments:
- hidden_in: bfloat16 [10240, 1024], P(('dp', 'col'), 'row'), may hold values from -8 to 8
- cotangent: bfloat16 [10240, 1024], P(('dp', 'col'), 'row'), may hold values from -6 to 6
- seq_ids: int32 [10240], P('dp'), may hold values from 0 to 3, as said below
- qkv_weight: float32 [2, 1024, 3072], P(None, ('row', 'dp'), 'col'), may hold values from -0.1875 to 0.1875
- qkv_first: float32 [2, 1024, 3072], P(None, ('row', 'dp'), 'col'), may hold values from -96 to 96
- qkv_second: float32 [2, 1024, 3072], P(None, ('row', 'dp'), 'col'), may hold values from 604.16 to 9728
- out_weight: float32 [2, 1024, 1024], P(None, ('col', 'dp'), 'row'), may hold values from -0.75 to 0.75
- out_first: float32 [2, 1024, 1024], P(None, ('col', 'dp'), 'row'), may hold values from -10 to 10
- out_second: float32 [2, 1024, 1024], P(None, ('col', 'dp'), 'row'), may hold values from 6.144 to 97.28
- up_weight: float32 [2, 1024, 4096], P(None, ('row', 'dp'), 'col'), may hold values from -0.1875 to 0.1875
- up_first: float32 [2, 1024, 4096], P(None, ('row', 'dp'), 'col'), may hold values from -16 to 16
- up_second: float32 [2, 1024, 4096], P(None, ('row', 'dp'), 'col'), may hold values from 16.384 to 266.24
- down_weight: float32 [2, 4096, 1024], P(None, ('col', 'dp'), 'row'), may hold values from -0.09375 to 0.09375
- down_first: float32 [2, 4096, 1024], P(None, ('col', 'dp'), 'row'), may hold values from -32 to 32
- down_second: float32 [2, 4096, 1024], P(None, ('col', 'dp'), 'row'), may hold values from 67.584 to 1075.2
- qkv_bias: float32 [2, 3072], P(None, ('col', 'row', 'dp')), may hold values from -1.25 to 1.25
- qkv_bias_first: float32 [2, 3072], P(None, ('col', 'row', 'dp')), may hold values from -96 to 96
- qkv_bias_second: float32 [2, 3072], P(None, ('col', 'row', 'dp')), may hold values from 604.16 to 9728
- up_bias: float32 [2, 4096], P(None, ('col', 'row', 'dp')), may hold values from -1.25 to 1.25
- up_bias_first: float32 [2, 4096], P(None, ('col', 'row', 'dp')), may hold values from -16 to 16
- up_bias_second: float32 [2, 4096], P(None, ('col', 'row', 'dp')), may hold values from 16.384 to 266.24
- row_vectors: float32 [2, 6, 1024], P(None, None, 'row'), may hold values from -0.6 to 1.45
- row_first: float32 [2, 6, 1024], P(None, None, 'row'), may hold values from -64 to 64
- row_second: float32 [2, 6, 1024], P(None, None, 'row'), may hold values from 266.24 to 4300.8
Outputs:
- hidden_out: bfloat16 [10240, 1024], P(('dp', 'col'), 'row')
- input_grad: float32 [10240, 1024], P(('dp', 'col'), 'row')
- qkv_weight_new: float32 [2, 1024, 3072], P(None, ('row', 'dp'), 'col')
- qkv_first_new: float32 [2, 1024, 3072], P(None, ('row', 'dp'), 'col')
- qkv_second_new: float32 [2, 1024, 3072], P(None, ('row', 'dp'), 'col')
- out_weight_new: float32 [2, 1024, 1024], P(None, ('col', 'dp'), 'row')
- out_first_new: float32 [2, 1024, 1024], P(None, ('col', 'dp'), 'row')
- out_second_new: float32 [2, 1024, 1024], P(None, ('col', 'dp'), 'row')
- up_weight_new: float32 [2, 1024, 4096], P(None, ('row', 'dp'), 'col')
- up_first_new: float32 [2, 1024, 4096], P(None, ('row', 'dp'), 'col')
- up_second_new: float32 [2, 1024, 4096], P(None, ('row', 'dp'), 'col')
- down_weight_new: float32 [2, 4096, 1024], P(None, ('col', 'dp'), 'row')
- down_first_new: float32 [2, 4096, 1024], P(None, ('col', 'dp'), 'row')
- down_second_new: float32 [2, 4096, 1024], P(None, ('col', 'dp'), 'row')
- qkv_bias_new: float32 [2, 3072], P(None, ('col', 'row', 'dp'))
- qkv_bias_first_new: float32 [2, 3072], P(None, ('col', 'row', 'dp'))
- qkv_bias_second_new: float32 [2, 3072], P(None, ('col', 'row', 'dp'))
- up_bias_new: float32 [2, 4096], P(None, ('col', 'row', 'dp'))
- up_bias_first_new: float32 [2, 4096], P(None, ('col', 'row', 'dp'))
- up_bias_second_new: float32 [2, 4096], P(None, ('col', 'row', 'dp'))
- row_vectors_new: float32 [2, 6, 1024], P(None, None, 'row')
- row_first_new: float32 [2, 6, 1024], P(None, None, 'row')
- row_second_new: float32 [2, 6, 1024], P(None, None, 'row')
The draws below stay inside these ranges and needn't reach their ends.
Inputs may be any that keep to these rules, and one draw needn't show every extreme that they name: `seq_ids`: within each data group of 320 slots the numbers never fall; the value 3 marks padding, which stands after all live slots and occurs in some group; one sequence of every group covers the group's two middle slots; in every draw one group holds a single sequence of 320 slots.
All inputs are finite; a program needn't handle non-finite values.
Results may differ from the reference program's by a relative error of at most 0.012.
Values may be sent and summed in bfloat16 or wider, within the bound.
A program may use at most 128 MiB of HBM per device.

```python
import math
import jax
import jax.numpy as jnp
from jax import lax

D = 1024
FF = 4096
HEADS = 16
HEAD = 64
ROT = 16
LAYERS = 2
CAP = 320
SEQS = 3
STEP = 10
TOKENS = 10240


def draw_hidden_in(key, part):
    key = jax.random.fold_in(key, 5)
    keys = jax.random.split(key, 3)
    place = jnp.arange(D, dtype=jnp.float32) / D
    column_scale = 0.6 * 2.0 ** place * jnp.exp(jax.random.uniform(keys[0], (D,), minval=-0.69, maxval=0.69))
    offset = 0.8 * place - 0.1
    noise = jax.random.normal(keys[1], (TOKENS, D))
    row_scale = jnp.exp(jax.random.uniform(keys[2], (TOKENS, 1), minval=-0.5, maxval=0.5))
    values = jnp.clip(noise * column_scale[None, :] * row_scale + offset[None, :], -8.0, 8.0)
    return values.astype(jnp.bfloat16)


def draw_row_vectors(key, part):
    key = jax.random.fold_in(key, 7)
    base = jnp.clip(jax.random.normal(key, (LAYERS, 6, D)), -3.0, 3.0)
    kinds = jnp.array([1.0, 0.0, 1.0, 0.0, 0.0, 0.0], dtype=jnp.float32)[None, :, None]
    return kinds * (1.0 + 0.15 * base) + (1.0 - kinds) * 0.2 * base


def draw_seq_ids(key, part):
    key = jax.random.fold_in(key, 11)
    groups = TOKENS // CAP
    group_key, full_key = jax.random.split(key)
    full_group = jax.random.randint(full_key, (), 0, groups)
    keys = jax.random.split(group_key, 3)
    live_count = jax.random.randint(keys[0], (groups,), CAP // 2 + 1, CAP)
    first_cut = jax.random.randint(keys[1], (groups,), 1, CAP // 4 + 1)
    second_cut = jnp.minimum(jax.random.randint(keys[2], (groups,), CAP // 2 + 1, CAP + 1), live_count)
    place = jnp.arange(CAP, dtype=jnp.int32)[None, :]
    labels = (place >= first_cut[:, None]).astype(jnp.int32) + (place >= second_cut[:, None]).astype(jnp.int32) + (place >= live_count[:, None]).astype(jnp.int32)
    chosen = (jnp.arange(groups, dtype=jnp.int32) == full_group)[:, None]
    labels = jnp.where(chosen, jnp.zeros_like(labels), labels)
    return labels.reshape(TOKENS).astype(jnp.int32)


def level_of(key, dims, shards, least, high):
    factor_of, own = 1.0, jax.random.fold_in(key, 6)
    for axis_at, shards_of in shards:
        heights = jnp.exp(jax.random.uniform(jax.random.fold_in(own, axis_at), (shards_of,), jnp.float32, least / len(shards), high / len(shards)))
        factor_of = factor_of * jnp.repeat(heights, dims[axis_at] // shards_of).reshape([-1 if axis == axis_at else 1 for axis in range(len(dims))])
    return factor_of


def gaussian(key, shape, scale, reach, cuts=(), kind=jnp.bfloat16):
    factor_of = level_of(key, shape, cuts, -0.22, 0.18) if cuts else 1.0
    values = jax.random.normal(key, shape, jnp.float32) * scale * factor_of
    return jnp.minimum(jnp.maximum(values, -reach), reach).astype(kind)


def setup_inputs(seed: int = 0) -> dict:
    arg_keys = jax.random.split(jax.random.key(seed), 25)
    return {
        "hidden_in": draw_hidden_in(jax.random.fold_in(arg_keys[24], 71), 0),
        "cotangent": gaussian(arg_keys[1], (TOKENS, D), 1.0, 6.0, ((0, 64), (1, 2))),
        "seq_ids": draw_seq_ids(jax.random.fold_in(arg_keys[24], 71), 0),
        "qkv_weight": gaussian(arg_keys[3], (LAYERS, D, 3 * D), D ** -0.5, 0.1875, ((1, 64), (2, 2)), jnp.float32),
        "qkv_first": gaussian(arg_keys[4], (LAYERS, D, 3 * D), (0.17 * TOKENS ** 0.5), 96.0, ((1, 64), (2, 2)), jnp.float32),
        "qkv_second": jnp.clip(jnp.exp(math.log(9728.0) - 2.7789246 * jax.random.uniform(arg_keys[5], (LAYERS, D, 3 * D), jnp.float32) ** level_of(arg_keys[5], (LAYERS, D, 3 * D), ((1, 64), (2, 2)), -0.2, 0.2)), 604.16, 9728.0),
        "out_weight": gaussian(arg_keys[6], (LAYERS, D, D), (D // 16) ** -0.5, 0.75, ((1, 64), (2, 2)), jnp.float32),
        "out_first": gaussian(arg_keys[7], (LAYERS, D, D), (0.017 * TOKENS ** 0.5), 10.0, ((1, 64), (2, 2)), jnp.float32),
        "out_second": jnp.clip(jnp.exp(math.log(97.28) - 2.7621174 * jax.random.uniform(arg_keys[8], (LAYERS, D, D), jnp.float32) ** level_of(arg_keys[8], (LAYERS, D, D), ((1, 64), (2, 2)), -0.2, 0.2)), 6.144, 97.28),
        "up_weight": gaussian(arg_keys[9], (LAYERS, D, FF), D ** -0.5, 0.1875, ((1, 64), (2, 2)), jnp.float32),
        "up_first": gaussian(arg_keys[10], (LAYERS, D, FF), (0.028 * TOKENS ** 0.5), 16.0, ((1, 64), (2, 2)), jnp.float32),
        "up_second": jnp.clip(jnp.exp(math.log(266.24) - 2.7880928 * jax.random.uniform(arg_keys[11], (LAYERS, D, FF), jnp.float32) ** level_of(arg_keys[11], (LAYERS, D, FF), ((1, 64), (2, 2)), -0.2, 0.2)), 16.384, 266.24),
        "down_weight": gaussian(arg_keys[12], (LAYERS, FF, D), FF ** -0.5, 0.09375, ((1, 64), (2, 2)), jnp.float32),
        "down_first": gaussian(arg_keys[13], (LAYERS, FF, D), (0.056 * TOKENS ** 0.5), 32.0, ((1, 64), (2, 2)), jnp.float32),
        "down_second": jnp.clip(jnp.exp(math.log(1075.2) - 2.7668907 * jax.random.uniform(arg_keys[14], (LAYERS, FF, D), jnp.float32) ** level_of(arg_keys[14], (LAYERS, FF, D), ((1, 64), (2, 2)), -0.2, 0.2)), 67.584, 1075.2),
        "qkv_bias": gaussian(arg_keys[15], (LAYERS, 3 * D), 0.2, 1.25, ((1, 128),), jnp.float32),
        "qkv_bias_first": gaussian(arg_keys[16], (LAYERS, 3 * D), (0.17 * TOKENS ** 0.5), 96.0, ((1, 128),), jnp.float32),
        "qkv_bias_second": jnp.clip(jnp.exp(math.log(9728.0) - 2.7789246 * jax.random.uniform(arg_keys[17], (LAYERS, 3 * D), jnp.float32) ** level_of(arg_keys[17], (LAYERS, 3 * D), ((1, 128),), -0.2, 0.2)), 604.16, 9728.0),
        "up_bias": gaussian(arg_keys[18], (LAYERS, FF), 0.2, 1.25, ((1, 128),), jnp.float32),
        "up_bias_first": gaussian(arg_keys[19], (LAYERS, FF), (0.028 * TOKENS ** 0.5), 16.0, ((1, 128),), jnp.float32),
        "up_bias_second": jnp.clip(jnp.exp(math.log(266.24) - 2.7880928 * jax.random.uniform(arg_keys[20], (LAYERS, FF), jnp.float32) ** level_of(arg_keys[20], (LAYERS, FF), ((1, 128),), -0.2, 0.2)), 16.384, 266.24),
        "row_vectors": draw_row_vectors(jax.random.fold_in(arg_keys[24], 71), 0),
        "row_first": gaussian(arg_keys[22], (LAYERS, 6, D), (0.11 * TOKENS ** 0.5), 64.0, ((2, 2),), jnp.float32),
        "row_second": jnp.clip(jnp.exp(math.log(4300.8) - 2.7821582 * jax.random.uniform(arg_keys[23], (LAYERS, 6, D), jnp.float32) ** level_of(arg_keys[23], (LAYERS, 6, D), ((2, 2),), -0.2, 0.2)), 266.24, 4300.8),
    }


EPS_NORM = 1e-05
EPS_ADAM = 1e-08
BETA_ONE = 0.9
BETA_TWO = 0.95
RATE_MATRIX = 0.06
RATE_VECTOR = 0.6
DECAY_MATRIX = 0.01
ROPE_BASE = 10000.0
MASK_VALUE = -1e+30

@jax.custom_vjp
def low(v):
    return lax.optimization_barrier(v.astype(jnp.bfloat16)).astype(jnp.float32)

@jax.custom_vjp
def low_back(v):
    return v

def low_keep(v):
    return (low(v), None)

def low_pass(kept, grad):
    return (grad,)

def back_keep(v):
    return (v, None)

def back_low(kept, grad):
    return (low(grad),)
low.defvjp(low_keep, low_pass)
low_back.defvjp(back_keep, back_low)

def product(left_side, right_side):
    return jnp.dot(left_side, right_side, precision=lax.Precision.HIGHEST, preferred_element_type=jnp.float32)

def sequence_layout(group_ids):
    length = group_ids.shape[0]
    labels = jnp.arange(SEQS + 1, dtype=jnp.int32)
    member = (group_ids[:, None] == labels[None, :]).astype(jnp.int32)
    counts = lax.optimization_barrier(jnp.sum(member, 0, dtype=jnp.int32))
    lower_ids = (labels[None, :] < group_ids[:, None]).astype(jnp.int32)
    starts = lax.optimization_barrier(jnp.sum(lower_ids * counts[None, :], 1, dtype=jnp.int32))
    places = jnp.arange(length, dtype=jnp.int32)
    positions = places - starts
    allowed = (group_ids[:, None] == group_ids[None, :]) & (places[None, :] <= places[:, None])
    live_rows = (group_ids < SEQS).astype(jnp.float32)
    return (positions, allowed, live_rows)

def rope_tables(positions):
    steps_half = jnp.arange(ROT // 2, dtype=jnp.float32)
    frequency = ROPE_BASE ** (-2.0 * steps_half / ROT)
    angles = positions.astype(jnp.float32)[:, None] * frequency[None, :]
    angles = jnp.concatenate([angles, angles], 1)
    return (jnp.cos(angles), jnp.sin(angles))

def rotate_fwd(values, cosine, sine):
    half_rot = ROT // 2
    head_part = values[..., :ROT]
    turned = jnp.concatenate([-head_part[..., half_rot:], head_part[..., :half_rot]], -1)
    rotated = head_part * cosine[:, None, :] + turned * sine[:, None, :]
    return jnp.concatenate([rotated, values[..., ROT:]], -1)

def forward_group(state, params, positions, allowed):
    qkv_weight, out_weight, up_weight, down_weight, qkv_bias, up_bias, row_vectors = params
    cosine, sine = rope_tables(positions)
    score_scale = HEAD ** (-0.5)
    group_len = state.shape[0]
    for layer_index in range(LAYERS):
        vectors = row_vectors[layer_index]
        average = lax.optimization_barrier(jnp.mean(state, 1, keepdims=True))
        spread = lax.optimization_barrier(jnp.mean(state * state, 1, keepdims=True)) - average * average
        normal_hat = (state - average) * lax.rsqrt(spread + EPS_NORM)
        attn_in = low(normal_hat * vectors[0] + vectors[1])
        mlp_in = low(normal_hat * vectors[2] + vectors[3])
        joined = low_back(product(attn_in, low(qkv_weight[layer_index])) + low(qkv_bias[layer_index]))
        joined = joined.reshape(group_len, HEADS, 3 * HEAD)
        query = low(rotate_fwd(joined[..., :HEAD], cosine, sine))
        key_rows = low(rotate_fwd(joined[..., HEAD:2 * HEAD], cosine, sine))
        value_rows = low(joined[..., 2 * HEAD:])
        raw = low_back(jnp.einsum('qhd,khd->hqk', query, key_rows, precision=lax.Precision.HIGHEST))
        scores = jnp.where(allowed[None], raw * score_scale, MASK_VALUE)
        peak = lax.optimization_barrier(jnp.max(scores, -1, keepdims=True))
        expo = jnp.exp(scores - peak)
        probs = expo / lax.optimization_barrier(jnp.sum(expo, -1, keepdims=True))
        attended = jnp.einsum('hqk,khd->qhd', low(probs), value_rows, precision=lax.Precision.HIGHEST)
        attended = low(low_back(attended.reshape(group_len, D)))
        hidden_pre = low_back(product(mlp_in, low(up_weight[layer_index])) + low(up_bias[layer_index]))
        activated = low(jax.nn.gelu(hidden_pre, approximate=False))
        attn_out = low_back(product(attended, low(out_weight[layer_index])) + vectors[4])
        mlp_out = low_back(product(activated, low(down_weight[layer_index])) + vectors[5])
        state = state + attn_out + mlp_out
    return state

def adamw(master, moment_one, moment_two, gradient, step_rate, step_decay):
    one_new = BETA_ONE * moment_one + (1.0 - BETA_ONE) * gradient
    two_new = BETA_TWO * moment_two + (1.0 - BETA_TWO) * gradient * gradient
    one_hat = one_new / (1.0 - BETA_ONE ** STEP)
    two_hat = two_new / (1.0 - BETA_TWO ** STEP)
    master_new = master - step_rate * (one_hat / (jnp.sqrt(two_hat) + EPS_ADAM) + step_decay * master)
    return (master_new, one_new, two_new)

def reference(hidden_in, cotangent, seq_ids, qkv_weight, qkv_first, qkv_second, out_weight, out_first, out_second, up_weight, up_first, up_second, down_weight, down_first, down_second, qkv_bias, qkv_bias_first, qkv_bias_second, up_bias, up_bias_first, up_bias_second, row_vectors, row_first, row_second):
    groups = TOKENS // CAP
    params = (qkv_weight, out_weight, up_weight, down_weight, qkv_bias, up_bias, row_vectors)
    states = hidden_in.astype(jnp.float32).reshape(groups, CAP, D)
    pulls = cotangent.astype(jnp.float32).reshape(groups, CAP, D)
    labels = seq_ids.reshape(groups, CAP)

    def one_group(totals, inputs):
        state, pull, group_ids = inputs
        positions, allowed, live_rows = sequence_layout(group_ids)
        result, backward = jax.vjp(lambda source, weights: forward_group(source, weights, positions, allowed), state, params)
        grad_state, grad_params = backward(pull * live_rows[:, None])
        totals = jax.tree.map(lambda left_side, right_side: left_side + right_side, totals, grad_params)
        return (totals, (result, grad_state))
    zeros = jax.tree.map(jnp.zeros_like, params)
    totals, (results, grad_states) = lax.scan(one_group, zeros, (states, pulls, labels))
    grad_qkv, grad_out, grad_up, grad_down, grad_qkv_bias, grad_up_bias, grad_rows = totals
    qkv_new = adamw(qkv_weight, qkv_first, qkv_second, grad_qkv, RATE_MATRIX, DECAY_MATRIX)
    out_new = adamw(out_weight, out_first, out_second, grad_out, RATE_MATRIX, DECAY_MATRIX)
    up_new = adamw(up_weight, up_first, up_second, grad_up, RATE_MATRIX, DECAY_MATRIX)
    down_new = adamw(down_weight, down_first, down_second, grad_down, RATE_MATRIX, DECAY_MATRIX)
    qkv_bias_new = adamw(qkv_bias, qkv_bias_first, qkv_bias_second, grad_qkv_bias, RATE_MATRIX, 0.0)
    up_bias_new = adamw(up_bias, up_bias_first, up_bias_second, grad_up_bias, RATE_MATRIX, 0.0)
    row_new = adamw(row_vectors, row_first, row_second, grad_rows, RATE_VECTOR, 0.0)
    hidden_out = results.reshape(TOKENS, D).astype(jnp.bfloat16)
    input_grad = grad_states.reshape(TOKENS, D)
    return (hidden_out, input_grad, qkv_new[0], qkv_new[1], qkv_new[2], out_new[0], out_new[1], out_new[2], up_new[0], up_new[1], up_new[2], down_new[0], down_new[1], down_new[2], qkv_bias_new[0], qkv_bias_new[1], qkv_bias_new[2], up_bias_new[0], up_bias_new[1], up_bias_new[2], row_new[0], row_new[1], row_new[2])
```

```python
import math
from functools import partial

import jax
import jax.numpy as jnp
from jax import lax
from jax.experimental import pallas as pl
from jax.experimental.pallas import tpu as pltpu
from jax.sharding import PartitionSpec as P

D = 1024
HEAD = 64
ROT = 16
LAYERS = 2
SEQS = 3
STEP = 10


EPS_NORM = 1e-05
EPS_ADAM = 1e-08
BETA_ONE = 0.9
BETA_TWO = 0.95
RATE_MATRIX = 0.06
RATE_VECTOR = 0.6
DECAY_MATRIX = 0.01
ROPE_BASE = 10000.0
MASK_VALUE = -1e30
CONTRACT_ROWS = (((0,), (0,)), ((), ()))
CONTRACT_COLS = (((1,), (1,)), ((), ()))

BF = jnp.bfloat16
F32 = jnp.float32
MESH = pl.DeviceIdType.MESH
GRIDS = {32: (4, 4, 2), 8: (2, 2, 2)}
VEC_ROWS = 8
VMEM_SPEC = pl.BlockSpec(memory_space=pltpu.VMEM)


def params(collective_id, mib):
    return pltpu.CompilerParams(
        collective_id=collective_id, has_side_effects=True, vmem_limit_bytes=mib << 20
    )


def remote(src, dst, sends, recvs, at, device):
    return pltpu.make_async_remote_copy(
        src_ref=src,
        dst_ref=dst,
        send_sem=sends.at[at],
        recv_sem=recvs.at[at],
        device_id=device,
        device_id_type=MESH,
    )


def greet(device):
    pl.semaphore_signal(
        pltpu.get_barrier_semaphore(), inc=1, device_id=device, device_id_type=MESH
    )


def greeted(count):
    pl.semaphore_wait(pltpu.get_barrier_semaphore(), count)


def group_place():
    return lax.axis_index("row") * 2 + lax.axis_index("col")


def group_peer(place, step):
    other = lax.rem(place + step, 4)
    return {"row": other // 2, "col": lax.rem(other, 2)}


def over(lengths, body):
    total = math.prod(lengths)

    def one(index, carry):
        place, rest = [], index
        for length in reversed(lengths):
            place.append(lax.rem(rest, length))
            rest = rest // length
        body(*reversed(place))
        return carry

    lax.fori_loop(0, total, one, 0)


def sequence_layout(group_ids):
    length = group_ids.shape[0]
    labels = jnp.arange(SEQS + 1, dtype=jnp.int32)
    member = (group_ids[:, None] == labels[None, :]).astype(jnp.int32)
    counts = jnp.sum(member, 0, dtype=jnp.int32)
    lower_ids = (labels[None, :] < group_ids[:, None]).astype(jnp.int32)
    starts = jnp.sum(lower_ids * counts[None, :], 1, dtype=jnp.int32)
    places = jnp.arange(length, dtype=jnp.int32)
    positions = places - starts
    allowed = (group_ids[:, None] == group_ids[None, :]) & (places[None, :] <= places[:, None])
    live_rows = (group_ids < SEQS).astype(jnp.float32)
    return (positions, allowed, live_rows)


def rope_tables(positions):
    steps_half = jnp.arange(ROT // 2, dtype=jnp.float32)
    frequency = ROPE_BASE ** (-2.0 * steps_half / ROT)
    angles = positions.astype(jnp.float32)[:, None] * frequency[None, :]
    angles = jnp.concatenate([angles, angles], 1)
    return (jnp.cos(angles), jnp.sin(angles))


def rotate_fwd(values, cosine, sine):
    half_rot = ROT // 2
    head_part = values[..., :ROT]
    turned = jnp.concatenate([-head_part[..., half_rot:], head_part[..., :half_rot]], -1)
    rotated = head_part * cosine[:, None, :] + turned * sine[:, None, :]
    return jnp.concatenate([rotated, values[..., ROT:]], -1)


def rotate_back(gradient, cosine, sine):
    half_rot = ROT // 2
    head_part = gradient[..., :ROT]
    scaled = head_part * sine[:, None, :]
    turned = jnp.concatenate([scaled[..., half_rot:], -scaled[..., :half_rot]], -1)
    return jnp.concatenate([head_part * cosine[:, None, :] + turned, gradient[..., ROT:]], -1)


def masked_scores(query, key_rows, allowed):
    score_scale = HEAD ** (-0.5)
    scores = (
        jnp.einsum("qhd,khd->hqk", query, key_rows, preferred_element_type=jnp.float32)
        * score_scale
    )
    return jnp.where(allowed[None], scores, MASK_VALUE)


def attend(query, key_rows, value_rows, allowed):
    scores = masked_scores(query, key_rows, allowed)
    peak = jnp.max(scores, -1, keepdims=True)
    expo = jnp.exp(scores - peak)
    row_total = jnp.sum(expo, -1, keepdims=True)
    probs = expo / row_total
    log_total = peak + jnp.log(row_total)
    attended = jnp.einsum(
        "hqk,khd->qhd", probs.astype(jnp.bfloat16), value_rows, preferred_element_type=jnp.float32
    )
    return (attended, log_total)


def attend_back(query, key_rows, value_rows, allowed, log_total, grad_attended):
    score_scale = HEAD ** (-0.5)
    probs = jnp.exp(masked_scores(query, key_rows, allowed) - log_total)
    grad_value = jnp.einsum(
        "hqk,qhd->khd",
        probs.astype(jnp.bfloat16),
        grad_attended,
        preferred_element_type=jnp.float32,
    )
    grad_probs = jnp.einsum(
        "qhd,khd->hqk", grad_attended, value_rows, preferred_element_type=jnp.float32
    )
    inner = jnp.sum(grad_probs * probs, -1, keepdims=True)
    grad_raw = (probs * (grad_probs - inner) * score_scale).astype(jnp.bfloat16)
    grad_query = jnp.einsum("hqk,khd->qhd", grad_raw, key_rows, preferred_element_type=jnp.float32)
    grad_key = jnp.einsum("hqk,qhd->khd", grad_raw, query, preferred_element_type=jnp.float32)
    return (grad_query, grad_key, grad_value)


def adamw(master, moment_one, moment_two, gradient, step_rate, step_decay):
    one_new = BETA_ONE * moment_one + (1.0 - BETA_ONE) * gradient
    two_new = BETA_TWO * moment_two + (1.0 - BETA_TWO) * gradient * gradient
    one_hat = one_new / (1.0 - BETA_ONE**STEP)
    two_hat = two_new / (1.0 - BETA_TWO**STEP)
    master_new = master - step_rate * (
        one_hat / (jnp.sqrt(two_hat) + EPS_ADAM) + step_decay * master
    )
    return (master_new, one_new, two_new)


def start_kernel(
    n_dp, hid, cot, vec, wa, wb, hid_all, cot_all, vec_all, wa_own, wb_own, sends, recvs, local
):
    half = n_dp // 2
    d, r, c = lax.axis_index("dp"), lax.axis_index("row"), lax.axis_index("col")
    place = group_place()
    rows, lanes = hid.shape
    dh, dl = d // half, lax.rem(d, half)
    swap_needed = dh != r
    swap_to = {"dp": r * half + dl, "row": dh}
    a_target = r * half + d // 2
    slot = lax.rem(d, 2)
    a_selfs = [(r == k) & (a_target == d) for k in range(2)]
    a_from = [2 * dl + k for k in range(2)]
    from_selfs = [(dh == r) & (a_from[k] == d) for k in range(2)]

    for step in range(1, 4):
        greet(group_peer(place, step))
    for k in range(2):

        @pl.when(jnp.logical_not(from_selfs[k]))
        def _():
            greet({"dp": a_from[k], "row": dh})

    @pl.when(swap_needed)
    def _():
        greet(swap_to)

    greeted(5 + swap_needed.astype(jnp.int32) - sum(k.astype(jnp.int32) for k in a_selfs))

    tokens = pl.ds(pl.multiple_of(c * rows, rows), rows)
    features = pl.ds(pl.multiple_of(r * lanes, lanes), lanes)

    def swap_copy():
        return remote(wb, wb_own, sends.at[6], recvs.at[6], 0, swap_to)

    for k in range(2):

        @pl.when(jnp.logical_not(a_selfs[k]))
        def _():
            remote(
                wa.at[k],
                wa_own.at[:, slot],
                sends.at[7 + k],
                recvs.at[7],
                slot,
                {"dp": a_target, "row": k},
            ).start()

        @pl.when(a_selfs[k])
        def _():
            pltpu.make_async_copy(wa.at[k], wa_own.at[:, slot], local.at[0]).start()

    @pl.when(swap_needed)
    def _():
        swap_copy().start()

    @pl.when(jnp.logical_not(swap_needed))
    def _():
        pltpu.make_async_copy(wb, wb_own, local.at[1]).start()

    copies = []
    for step in range(1, 4):
        peer = group_peer(place, step)
        copies.append(
            remote(hid, hid_all.at[tokens, features], sends.at[0], recvs.at[0], step, peer)
        )
        copies.append(
            remote(cot, cot_all.at[tokens, features], sends.at[1], recvs.at[1], step, peer)
        )
    copies.append(
        remote(
            vec, vec_all.at[:, features], sends.at[2], recvs.at[2], 0, {"row": 1 - r}
        )
    )
    for copy in copies:
        copy.start()
    own = [
        pltpu.make_async_copy(hid, hid_all.at[tokens, features], local.at[2]),
        pltpu.make_async_copy(cot, cot_all.at[tokens, features], local.at[3]),
        pltpu.make_async_copy(vec, vec_all.at[:, features], local.at[4]),
    ]
    for copy in own:
        copy.start()
    for copy in own:
        copy.wait()
    for copy in copies:
        copy.wait()

    for k in range(2):

        @pl.when(jnp.logical_not(a_selfs[k]))
        def _():
            remote(
                wa.at[k],
                wa_own.at[:, slot],
                sends.at[7 + k],
                recvs.at[7],
                slot,
                {"dp": a_target, "row": k},
            ).wait_send()

        @pl.when(a_selfs[k])
        def _():
            pltpu.make_async_copy(wa.at[k], wa_own.at[:, slot], local.at[0]).wait()

        @pl.when(jnp.logical_not(from_selfs[k]))
        def _():
            remote(
                wa.at[k],
                wa_own.at[:, k],
                sends.at[7],
                recvs.at[7],
                k,
                {"dp": a_from[k], "row": dh},
            ).wait_recv()

    @pl.when(swap_needed)
    def _():
        swap_copy().wait()

    @pl.when(jnp.logical_not(swap_needed))
    def _():
        pltpu.make_async_copy(wb, wb_own, local.at[1]).wait()


def start_exchange(n_dp, hid, cot, vec, wa, wb):
    rows, lanes = hid.shape
    _, layers, depth, width = wa.shape
    return pl.pallas_call(
        partial(start_kernel, n_dp),
        out_shape=(
            jax.ShapeDtypeStruct((2 * rows, 2 * lanes), BF),
            jax.ShapeDtypeStruct((2 * rows, 2 * lanes), BF),
            jax.ShapeDtypeStruct((vec.shape[0], 2 * lanes), F32),
            jax.ShapeDtypeStruct((layers, 2, depth, width), BF),
            jax.ShapeDtypeStruct(wb.shape, BF),
        ),
        in_specs=[VMEM_SPEC] * 5,
        out_specs=(VMEM_SPEC,) * 5,
        scratch_shapes=[
            pltpu.SemaphoreType.DMA((9, 4)),
            pltpu.SemaphoreType.DMA((9, 4)),
            pltpu.SemaphoreType.DMA((5,)),
        ],
        compiler_params=params(0, 16),
        name="start_exchange",
    )(hid, cot, vec, wa, wb)


def place_in(grid):
    nz, nx, nc = grid
    d = lax.axis_index("dp")
    return (d // (nx * nc), lax.rem(d // nc, nx), lax.rem(d, nc))


def dp_at(grid, z, x, core):
    _, nx, nc = grid
    return {"dp": (z * nx + x) * nc + core}


def weights_kernel(grid, cut, wa, wb, wc, full_a, full_b, full_c, sends, recvs, local):
    nz, nx, nc = grid
    z, x, core = place_in(grid)
    zls = nz // 2
    zh, zl = z // zls, lax.rem(z, zls)
    lanes = wb.shape[-1]
    a_rows, b_rows = wa.shape[1], wb.shape[1]
    a_cut = (pl.ds(0, a_rows // 2), pl.ds(a_rows // 2, a_rows // 2))
    b_cut = (pl.ds(0, cut), pl.ds(cut, b_rows - cut))
    steps = (nz, nx)

    def z_peer(step):
        return dp_at(grid, lax.rem(z + step, nz), x, core)

    def x_peer(step):
        return dp_at(grid, z, lax.rem(x + step, nx), core)

    partner = dp_at(grid, z, x, 1 - core)

    for step in range(1, nz):
        greet(z_peer(step))
    for step in range(1, nx):
        greet(x_peer(step))
    greet(partner)
    greeted(nz + nx - 1)

    def b_lanes(zz):
        return pl.ds(pl.multiple_of((zz // zls) * lanes, lanes), lanes)

    def own_pieces(order):
        got = [
            (wa.at[:, a_cut[order]], full_a.at[:, z, x, core, a_cut[order]]),
            (wb.at[:, b_cut[order]], full_b.at[:, zl, x, core, b_cut[order], b_lanes(z)]),
        ]
        if order == 0:
            got.append((wc, full_c.at[z, x, core]))
        return got

    def line_pieces(order, along, cc):
        if order == 0:
            return [
                full_a.at[:, :, along, cc, a_cut[0]],
                full_b.at[:, :, along, cc, b_cut[0]],
                full_c.at[:, along, cc],
            ]
        return [
            full_a.at[:, along, :, cc, a_cut[1]],
            full_b.at[:, lax.rem(along, zls), :, cc, b_cut[1], b_lanes(along)],
        ]

    own = []
    for order in range(2):
        for k, (src, dst) in enumerate(own_pieces(order)):
            own.append(pltpu.make_async_copy(src, dst, local.at[order, k]))
    for copy in own:
        copy.start()

    first = [[], []]
    for order in range(2):
        peer = (z_peer, x_peer)[order]
        for step in range(1, steps[order]):
            for k, (src, dst) in enumerate(own_pieces(order)):
                first[order].append(
                    remote(src, dst, sends.at[order, 0, k], recvs.at[order, 0, k], step, peer(step))
                )
        for copy in first[order]:
            copy.start()
    for copy in own:
        copy.wait()

    second, forward = [[], []], [[], []]
    for order in range(2):
        for copy in first[order]:
            copy.wait_recv()
        peer, along = ((x_peer, x), (z_peer, z))[order]
        for step in range(1, steps[1 - order]):
            for k, ref in enumerate(line_pieces(order, along, core)):
                second[order].append(
                    remote(ref, ref, sends.at[order, 1, k], recvs.at[order, 1, k], step, peer(step))
                )
        for copy in second[order]:
            copy.start()
        for k, ref in enumerate(line_pieces(order, along, core)):
            forward[order].append(
                remote(ref, ref, sends.at[order, 2, k], recvs.at[order, 2, k], 0, partner)
            )
        for copy in forward[order]:
            copy.start()

    for step in range(1, max(nz, nx)):
        for order in range(2):
            count, along = ((nx, x), (nz, z))[order]
            if step >= count:
                continue
            pieces = len(line_pieces(order, along, core))
            for copy in second[order][(step - 1) * pieces : step * pieces]:
                copy.wait_recv()
            source = lax.rem(along + count - step, count)
            for k, ref in enumerate(line_pieces(order, source, core)):
                copy = remote(
                    ref, ref, sends.at[order, 2, k], recvs.at[order, 2, k], step, partner
                )
                copy.start()
                forward[order].append(copy)

    for order in range(2):
        for copy in first[order] + second[order] + forward[order]:
            copy.wait_send()
        count, along = ((nx, x), (nz, z))[order]
        for step in range(count):
            source = lax.rem(along + count - step, count)
            for k, ref in enumerate(line_pieces(order, source, 1 - core)):
                remote(
                    ref, ref, sends.at[order, 2, k], recvs.at[order, 2, k], step, partner
                ).wait_recv()


def gather_weights(grid, cut, wa, wb, wc):
    nz, nx, nc = grid
    layers, a_rows, width = wa.shape
    _, b_rows, lanes = wb.shape
    return pl.pallas_call(
        partial(weights_kernel, grid, cut),
        out_shape=(
            jax.ShapeDtypeStruct((layers, nz, nx, nc, a_rows, width), BF),
            jax.ShapeDtypeStruct((layers, nz // 2, nx, nc, b_rows, 2 * lanes), BF),
            jax.ShapeDtypeStruct((nz, nx, nc, *wc.shape), BF),
        ),
        in_specs=[VMEM_SPEC] * 3,
        out_specs=(VMEM_SPEC,) * 3,
        scratch_shapes=[
            pltpu.SemaphoreType.DMA((2, 3, 3, 4)),
            pltpu.SemaphoreType.DMA((2, 3, 3, 4)),
            pltpu.SemaphoreType.DMA((2, 3)),
        ],
        compiler_params=params(1, 40),
        name="gather_weights",
    )(wa, wb, wc)


def greet_group():
    place = group_place()
    for step in range(1, 4):
        greet(group_peer(place, step))
    greeted(3)
    return place


def spread_rows(place, whole, rows, sends, recvs):
    mine = whole.at[pl.ds(pl.multiple_of(place * rows, rows), rows)]
    copies = [
        remote(mine, mine, sends, recvs, step, group_peer(place, step)) for step in range(1, 4)
    ]
    for copy in copies:
        copy.start()
    return copies


def sum_rows(place, part, landed, rows, sends, recvs):
    copies = []
    for step in range(1, 4):
        other = lax.rem(place + step, 4)
        copies.append(
            remote(
                part.at[pl.ds(pl.multiple_of(other * rows, rows), rows)],
                landed.at[step - 1],
                sends,
                recvs,
                step,
                group_peer(place, step),
            )
        )
    for copy in copies:
        copy.start()
    total = part[pl.ds(pl.multiple_of(place * rows, rows), rows), :].astype(F32)
    for copy in copies:
        copy.wait()
    for step in range(3):
        total = total + landed[step].astype(F32)
    return total


def norm_stats(state):
    width = state.shape[1]
    average = jnp.sum(state, 1, keepdims=True) / width
    spread = jnp.sum(state * state, 1, keepdims=True) / width - average * average
    inv_std = lax.rsqrt(spread + EPS_NORM)
    return ((state - average) * inv_std, inv_std)


def forward_mid_kernel(part, state, state_new, inv_std, hat_all, landed, sends, recvs):
    rows = state.shape[0]
    place = greet_group()
    total = state[...] + sum_rows(place, part, landed, rows, sends.at[0], recvs.at[0])
    state_new[...] = total
    hat, inverse = norm_stats(total)
    inv_std[...] = jnp.broadcast_to(inverse, inv_std.shape)
    hat_all[pl.ds(pl.multiple_of(place * rows, rows), rows), :] = hat.astype(BF)
    for copy in spread_rows(place, hat_all, rows, sends.at[1], recvs.at[1]):
        copy.wait()


def forward_mid(part, state):
    tokens, width = part.shape
    rows = tokens // 4
    return pl.pallas_call(
        forward_mid_kernel,
        out_shape=(
            jax.ShapeDtypeStruct((rows, width), F32),
            jax.ShapeDtypeStruct((rows, 128), F32),
            jax.ShapeDtypeStruct((tokens, width), BF),
        ),
        in_specs=[VMEM_SPEC] * 2,
        out_specs=(VMEM_SPEC,) * 3,
        scratch_shapes=[
            pltpu.VMEM((3, rows, width), BF),
            pltpu.SemaphoreType.DMA((2, 4)),
            pltpu.SemaphoreType.DMA((2, 4)),
        ],
        compiler_params=params(2, 16),
        name="forward_mid",
    )(part, state)


def backward_mid_kernel(part, grad, inv_std, grad_new, grad_all, landed, sends, recvs):
    rows = grad.shape[0]
    place = greet_group()
    total = sum_rows(place, part, landed, rows, sends.at[0], recvs.at[0])
    total = grad[...] + inv_std[:, :1] * total
    grad_new[...] = total
    grad_all[pl.ds(pl.multiple_of(place * rows, rows), rows), :] = total.astype(BF)
    for copy in spread_rows(place, grad_all, rows, sends.at[1], recvs.at[1]):
        copy.wait()


def backward_mid(part, grad, inv_std):
    tokens, width = part.shape
    rows = tokens // 4
    return pl.pallas_call(
        backward_mid_kernel,
        out_shape=(
            jax.ShapeDtypeStruct((rows, width), F32),
            jax.ShapeDtypeStruct((tokens, width), BF),
        ),
        in_specs=[VMEM_SPEC] * 3,
        out_specs=(VMEM_SPEC,) * 2,
        scratch_shapes=[
            pltpu.VMEM((3, rows, width), BF),
            pltpu.SemaphoreType.DMA((2, 4)),
            pltpu.SemaphoreType.DMA((2, 4)),
        ],
        compiler_params=params(3, 16),
        name="backward_mid",
    )(part, grad, inv_std)


def sum_blocks_kernel(part, out, landed, sends, recvs):
    rows, lanes = out.shape
    place = greet_group()

    def block(at):
        return (
            pl.ds(pl.multiple_of(lax.rem(at, 2) * rows, rows), rows),
            pl.ds(pl.multiple_of((at // 2) * lanes, lanes), lanes),
        )

    copies = [
        remote(
            part.at[block(lax.rem(place + step, 4))],
            landed.at[step - 1],
            sends,
            recvs,
            step,
            group_peer(place, step),
        )
        for step in range(1, 4)
    ]
    for copy in copies:
        copy.start()
    total = part[block(place)].astype(F32)
    for copy in copies:
        copy.wait()
    for step in range(3):
        total = total + landed[step].astype(F32)
    out[...] = total


def sum_blocks(part):
    tokens, width = part.shape
    return pl.pallas_call(
        sum_blocks_kernel,
        out_shape=jax.ShapeDtypeStruct((tokens // 2, width // 2), F32),
        in_specs=[VMEM_SPEC],
        out_specs=VMEM_SPEC,
        scratch_shapes=[
            pltpu.VMEM((3, tokens // 2, width // 2), BF),
            pltpu.SemaphoreType.DMA((4,)),
            pltpu.SemaphoreType.DMA((4,)),
        ],
        compiler_params=params(4, 16),
        name="sum_blocks",
    )(part)


def grads_kernel(
    grid,
    cut,
    ga,
    gb,
    gv,
    out_a,
    out_b,
    out_v,
    own_v,
    sa,
    sb,
    sv,
    line_a0,
    line_a1,
    line_b0,
    line_b1,
    line_v,
    mid_a0,
    mid_a1,
    mid_b0,
    mid_b1,
    last_a0,
    last_a1,
    last_b0,
    last_b1,
    last_v,
    fin_a,
    fin_b,
    group_v,
    sends,
    recvs,
    local,
):
    nz, nx, nc = grid
    n_dp = nz * nx * nc
    half = n_dp // 2
    z, x, core = place_in(grid)
    d, r = lax.axis_index("dp"), lax.axis_index("row")
    place = group_place()
    zls = nz // 2
    layers, a_rows = ga.shape[0], ga.shape[4]
    b_rows, lanes = gb.shape[4], gb.shape[5] // 2
    a_half = a_rows // 2
    a_cut = (pl.ds(0, a_half), pl.ds(a_half, a_half))
    b_cut = (pl.ds(0, cut), pl.ds(cut, b_rows - cut))
    partner = dp_at(grid, z, x, 1 - core)

    def z_at(step):
        return lax.rem(z + step, nz)

    def x_at(step):
        return lax.rem(x + step, nx)

    def b_lanes(zz):
        return pl.ds(pl.multiple_of((zz // zls) * lanes, lanes), lanes)

    dh, dl = d // half, lax.rem(d, half)
    swap_needed = dh != r
    swap_to = {"dp": r * half + dl, "row": dh}
    a_target = [{"dp": 2 * dl + s, "row": dh} for s in range(2)]
    to_self = [(dh == r) & (2 * dl + s == d) for s in range(2)]
    a_slot = lax.rem(d, 2)
    a_source = r * half + d // 2
    from_self = [(r == k) & (a_source == d) for k in range(2)]

    for step in range(1, nz):
        greet(dp_at(grid, z_at(step), x, core))
    for step in range(1, nx):
        greet(dp_at(grid, z, x_at(step), core))
    greet(partner)
    for step in range(1, 4):
        greet(group_peer(place, step))
    for k in range(2):

        @pl.when(jnp.logical_not(from_self[k]))
        def _():
            greet({"dp": a_source, "row": k})

    @pl.when(swap_needed)
    def _():
        greet(swap_to)

    greeted(nz + nx + 4 + swap_needed.astype(jnp.int32) - sum(s.astype(jnp.int32) for s in to_self))

    core_copies = []
    for order in range(2):
        pair = [
            remote(
                ga.at[:, :, :, 1 - core, a_cut[order]],
                sa.at[:, :, :, a_cut[order]],
                sends.at[0, order],
                recvs.at[0, order],
                0,
                partner,
            ),
            remote(
                gb.at[:, :, :, 1 - core, b_cut[order]],
                sb.at[:, :, :, b_cut[order]],
                sends.at[1, order],
                recvs.at[1, order],
                0,
                partner,
            ),
        ]
        if order == 0:
            pair.append(remote(gv, sv, sends.at[2, 0], recvs.at[2, 0], 0, partner))
        for copy in pair:
            copy.start()
        core_copies.append(pair)

    lines = [(line_a0, line_b0), (line_a1, line_b1)]
    mids = [(mid_a0, mid_b0), (mid_a1, mid_b1)]
    lasts = [(last_a0, last_b0), (last_a1, last_b1)]

    line_copies = [[], []]
    for order in range(2):
        for copy in core_copies[order]:
            copy.wait()
        a_at, b_at = a_cut[order], b_cut[order]

        def add_a(layer, zz, xx):
            sa[layer, zz, xx, a_at] = (
                sa[layer, zz, xx, a_at].astype(F32) + ga[layer, zz, xx, core, a_at].astype(F32)
            ).astype(BF)

        def add_b(layer, zz, xx):
            sb[layer, zz, xx, b_at] = (
                sb[layer, zz, xx, b_at].astype(F32) + gb[layer, zz, xx, core, b_at].astype(F32)
            ).astype(BF)

        over((layers, nz, nx), add_a)
        over((layers, zls, nx), add_b)
        line_a, line_b = lines[order]
        if order == 0:
            line_v[x] = sv[...] + gv[...]
            for step in range(1, nx):
                to = x_at(step)
                device = dp_at(grid, z, to, core)
                line_copies[0] += [
                    remote(
                        sa.at[:, :, to, a_at], line_a.at[x], sends.at[3, 0], recvs.at[3, 0], step, device
                    ),
                    remote(
                        sb.at[:, :, to, b_at], line_b.at[x], sends.at[4, 0], recvs.at[4, 0], step, device
                    ),
                    remote(
                        line_v.at[x], line_v.at[x], sends.at[5, 0], recvs.at[5, 0], step, device
                    ),
                ]
        else:
            for step in range(1, nz):
                to = z_at(step)
                device = dp_at(grid, to, x, core)
                line_copies[1] += [
                    remote(
                        sa.at[:, to, :, a_at], line_a.at[z], sends.at[3, 1], recvs.at[3, 1], step, device
                    ),
                    remote(
                        sb.at[:, lax.rem(to, zls), :, b_at, b_lanes(to)],
                        line_b.at[z],
                        sends.at[4, 1],
                        recvs.at[4, 1],
                        step,
                        device,
                    ),
                ]
        for copy in line_copies[order]:
            copy.start()

    last_copies = [[], []]
    for order in range(2):
        for copy in line_copies[order]:
            copy.wait()
        a_at, b_at = a_cut[order], b_cut[order]
        (line_a, line_b), (mid_a, mid_b), (last_a, last_b) = lines[order], mids[order], lasts[order]
        if order == 0:

            def add_a(layer, zz):
                total = sa[layer, zz, x, a_at].astype(F32)
                for step in range(1, nx):
                    total = total + line_a[x_at(step), layer, zz].astype(F32)
                mid_a[layer, zz] = total.astype(BF)

            def add_b(layer, zz):
                total = sb[layer, zz, x, b_at].astype(F32)
                for step in range(1, nx):
                    total = total + line_b[x_at(step), layer, zz].astype(F32)
                mid_b[layer, zz] = total.astype(BF)

            over((layers, nz), add_a)
            over((layers, zls), add_b)
            total = line_v[0]
            for xx in range(1, nx):
                total = total + line_v[xx]
            last_v[z] = total
            for step in range(1, nz):
                to = z_at(step)
                device = dp_at(grid, to, x, core)
                last_copies[0] += [
                    remote(
                        mid_a.at[:, to], last_a.at[z], sends.at[6, 0], recvs.at[6, 0], step, device
                    ),
                    remote(
                        mid_b.at[:, lax.rem(to, zls), :, b_lanes(to)],
                        last_b.at[z],
                        sends.at[7, 0],
                        recvs.at[7, 0],
                        step,
                        device,
                    ),
                    remote(
                        last_v.at[z], last_v.at[z], sends.at[8, 0], recvs.at[8, 0], step, device
                    ),
                ]
        else:

            def add_a(layer, xx):
                total = sa[layer, z, xx, a_at].astype(F32)
                for step in range(1, nz):
                    total = total + line_a[z_at(step), layer, xx].astype(F32)
                mid_a[layer, xx] = total.astype(BF)

            def add_b(layer, xx):
                total = sb[layer, lax.rem(z, zls), xx, b_at, b_lanes(z)].astype(F32)
                for step in range(1, nz):
                    total = total + line_b[z_at(step), layer, xx].astype(F32)
                mid_b[layer, xx] = total.astype(BF)

            over((layers, nx), add_a)
            over((layers, nx), add_b)
            for step in range(1, nx):
                to = x_at(step)
                device = dp_at(grid, z, to, core)
                last_copies[1] += [
                    remote(
                        mid_a.at[:, to], last_a.at[x], sends.at[6, 1], recvs.at[6, 1], step, device
                    ),
                    remote(
                        mid_b.at[:, to], last_b.at[x], sends.at[7, 1], recvs.at[7, 1], step, device
                    ),
                ]
        for copy in last_copies[order]:
            copy.start()

    group_copies = []
    for order in range(2):
        for copy in last_copies[order]:
            copy.wait()
        a_at, b_at = a_cut[order], b_cut[order]
        (mid_a, mid_b), (last_a, last_b) = mids[order], lasts[order]
        if order == 0:
            total = last_v[0]
            for zz in range(1, nz):
                total = total + last_v[zz]
            group_v[place] = total
            for step in range(1, 4):
                group_copies.append(
                    remote(
                        group_v.at[place],
                        group_v.at[place],
                        sends.at[9, 0],
                        recvs.at[9, 0],
                        step,
                        group_peer(place, step),
                    )
                )
            for copy in group_copies:
                copy.start()

        def add_a(layer):
            total = mid_a[layer, (z, x)[order]].astype(F32)
            for step in range(1, (nz, nx)[order]):
                total = total + last_a[(z_at, x_at)[order](step), layer].astype(F32)
            fin_a[order, layer] = total.astype(BF)

        def add_b(layer):
            if order == 0:
                total = mid_b[layer, lax.rem(z, zls), :, b_lanes(z)].astype(F32)
            else:
                total = mid_b[layer, x].astype(F32)
            for step in range(1, (nz, nx)[order]):
                total = total + last_b[(z_at, x_at)[order](step), layer].astype(F32)
            fin_b[layer, b_at] = total.astype(BF)

        over((layers,), add_a)
        over((layers,), add_b)

        @pl.when(jnp.logical_not(to_self[order]))
        def _():
            pltpu.make_async_remote_copy(
                src_ref=fin_a.at[order],
                dst_ref=out_a.at[r],
                send_sem=sends.at[9, 1, order],
                recv_sem=recvs.at[10, 1, r],
                device_id=a_target[order],
                device_id_type=MESH,
            ).start()

        @pl.when(to_self[order])
        def _():
            pltpu.make_async_copy(fin_a.at[order], out_a.at[r], local.at[0]).start()

    def swap_copy():
        return remote(fin_b, out_b, sends.at[10, 0], recvs.at[10, 0], 0, swap_to)

    @pl.when(swap_needed)
    def _():
        swap_copy().start()
        swap_copy().wait()

    @pl.when(jnp.logical_not(swap_needed))
    def _():
        copy = pltpu.make_async_copy(fin_b, out_b, local.at[1])
        copy.start()
        copy.wait()

    for copy in group_copies:
        copy.wait()
    total = group_v[0]
    for other in range(1, 4):
        total = total + group_v[other]
    out_v[...] = total
    own_v[...] = group_v[place]

    for k in range(2):

        @pl.when(jnp.logical_not(to_self[k]))
        def _():
            pltpu.make_async_remote_copy(
                src_ref=fin_a.at[k],
                dst_ref=out_a.at[r],
                send_sem=sends.at[9, 1, k],
                recv_sem=recvs.at[10, 1, r],
                device_id=a_target[k],
                device_id_type=MESH,
            ).wait_send()

        @pl.when(to_self[k])
        def _():
            pltpu.make_async_copy(fin_a.at[k], out_a.at[r], local.at[0]).wait()

        @pl.when(jnp.logical_not(from_self[k]))
        def _():
            pltpu.make_async_remote_copy(
                src_ref=fin_a.at[k],
                dst_ref=out_a.at[k],
                send_sem=sends.at[9, 1, k],
                recv_sem=recvs.at[10, 1, k],
                device_id={"dp": a_source, "row": k},
                device_id_type=MESH,
            ).wait_recv()


def sum_grads(grid, cut, ga, gb, gv):
    nz, nx, _ = grid
    layers, a_rows, width = ga.shape[0], ga.shape[4], ga.shape[5]
    b_rows, lanes = gb.shape[4], gb.shape[5] // 2
    a_half, zls, rest = a_rows // 2, nz // 2, b_rows - cut
    low = partial(pltpu.VMEM, dtype=BF)

    def vecs(count):
        return pltpu.VMEM((count, *gv.shape), F32)

    return pl.pallas_call(
        partial(grads_kernel, grid, cut),
        out_shape=(
            jax.ShapeDtypeStruct((2, layers, a_half, width), BF),
            jax.ShapeDtypeStruct((layers, b_rows, lanes), BF),
            jax.ShapeDtypeStruct(gv.shape, F32),
            jax.ShapeDtypeStruct(gv.shape, F32),
        ),
        in_specs=[VMEM_SPEC] * 3,
        out_specs=(VMEM_SPEC,) * 4,
        scratch_shapes=[
            low((layers, nz, nx, a_rows, width)),
            low((layers, zls, nx, b_rows, 2 * lanes)),
            pltpu.VMEM(gv.shape, F32),
            low((nx, layers, nz, a_half, width)),
            low((nz, layers, nx, a_half, width)),
            low((nx, layers, zls, cut, 2 * lanes)),
            low((nz, layers, nx, rest, lanes)),
            vecs(nx),
            low((layers, nz, a_half, width)),
            low((layers, nx, a_half, width)),
            low((layers, zls, cut, 2 * lanes)),
            low((layers, nx, rest, lanes)),
            low((nz, layers, a_half, width)),
            low((nx, layers, a_half, width)),
            low((nz, layers, cut, lanes)),
            low((nx, layers, rest, lanes)),
            vecs(nz),
            low((2, layers, a_half, width)),
            low((layers, b_rows, lanes)),
            vecs(4),
            pltpu.SemaphoreType.DMA((11, 2, 4)),
            pltpu.SemaphoreType.DMA((11, 2, 4)),
            pltpu.SemaphoreType.DMA((2,)),
        ],
        compiler_params=params(5, 56),
        name="sum_grads",
    )(ga, gb, gv)


def columns_for(array, row, width):
    return lax.dynamic_slice_in_dim(array, row * width, width, axis=2)


def layer_forward(rows_attn, rows_mlp, mats, layout):
    qkv_mat, up_mat, out_mat, down_mat, qkv_shift, up_shift = mats
    cosine, sine, allowed = layout
    group_len = rows_attn.shape[0]
    heads_here = qkv_mat.shape[1] // (3 * HEAD)
    joined = jnp.dot(rows_attn, qkv_mat, preferred_element_type=F32) + qkv_shift.astype(F32)
    joined = joined.reshape(group_len, heads_here, 3 * HEAD)
    query = rotate_fwd(joined[..., :HEAD], cosine, sine).astype(BF)
    key_rows = rotate_fwd(joined[..., HEAD : 2 * HEAD], cosine, sine).astype(BF)
    value_rows = joined[..., 2 * HEAD :].astype(BF)
    attended, log_total = attend(query, key_rows, value_rows, allowed)
    rows_heads = attended.reshape(group_len, heads_here * HEAD).astype(BF)
    hidden_pre = jnp.dot(rows_mlp, up_mat, preferred_element_type=F32) + up_shift.astype(F32)
    rows_units = jax.nn.gelu(hidden_pre, approximate=False).astype(BF)
    part = jnp.dot(rows_heads, out_mat, preferred_element_type=F32)
    part = part + jnp.dot(rows_units, down_mat, preferred_element_type=F32)
    return part, (query, key_rows, value_rows, log_total, hidden_pre, rows_heads, rows_units)


def layer_backward(rows_grad, rows_attn, rows_mlp, mats, layout, cache):
    qkv_mat, up_mat, out_mat, down_mat, _, _ = mats
    cosine, sine, allowed = layout
    query, key_rows, value_rows, log_total, hidden_pre, rows_heads, rows_units = cache
    group_len, heads_here, _ = query.shape

    def weight_grad(left, right):
        return lax.dot_general(left, right, CONTRACT_ROWS, preferred_element_type=F32).astype(BF)

    def input_grad(left, right):
        return lax.dot_general(left, right, CONTRACT_COLS, preferred_element_type=F32)

    grad_out_mat = weight_grad(rows_heads, rows_grad)
    grad_down_mat = weight_grad(rows_units, rows_grad)
    grad_heads = input_grad(rows_grad, out_mat)
    grad_units = input_grad(rows_grad, down_mat)
    _, gelu_pull = jax.vjp(partial(jax.nn.gelu, approximate=False), hidden_pre)
    grad_pre = gelu_pull(grad_units)[0].astype(BF)
    grad_attended = grad_heads.reshape(group_len, heads_here, HEAD).astype(BF)
    grad_query, grad_key, grad_value = attend_back(
        query, key_rows, value_rows, allowed, log_total, grad_attended
    )
    grad_joined = jnp.concatenate(
        [rotate_back(grad_query, cosine, sine), rotate_back(grad_key, cosine, sine), grad_value],
        -1,
    )
    grad_joined = grad_joined.reshape(group_len, heads_here * 3 * HEAD).astype(BF)
    grad_a = jnp.concatenate(
        [weight_grad(rows_attn, grad_joined), weight_grad(rows_mlp, grad_pre)], 1
    )
    shifts = (jnp.sum(grad_joined.astype(F32), 0), jnp.sum(grad_pre.astype(F32), 0))
    grad_attn_in = input_grad(grad_joined, qkv_mat)
    grad_mlp_in = input_grad(grad_pre, up_mat)
    return grad_attn_in, grad_mlp_in, grad_a, (grad_out_mat, grad_down_mat), shifts


def norm_back(grad_hat, hat):
    first = jnp.mean(grad_hat, 1, keepdims=True)
    second = jnp.mean(grad_hat * hat, 1, keepdims=True)
    return grad_hat - first - hat * second


def vector_sums(grad_attn_in, grad_mlp_in, hat, rows_grad, shifts):
    def padded(row):
        return jnp.pad(row, (0, D - row.shape[0]))

    return jnp.stack(
        [
            jnp.sum(grad_attn_in * hat, 0),
            jnp.sum(grad_attn_in, 0),
            jnp.sum(grad_mlp_in * hat, 0),
            jnp.sum(grad_mlp_in, 0),
            jnp.sum(rows_grad.astype(F32), 0) * 0.25,
            padded(shifts[0]),
            padded(shifts[1]),
            jnp.zeros((D,), F32),
        ]
    )


def on_device(
    hidden_in,
    cotangent,
    seq_ids,
    qkv_weight,
    qkv_first,
    qkv_second,
    out_weight,
    out_first,
    out_second,
    up_weight,
    up_first,
    up_second,
    down_weight,
    down_first,
    down_second,
    qkv_bias,
    qkv_bias_first,
    qkv_bias_second,
    up_bias,
    up_bias_first,
    up_bias_second,
    row_vectors,
    row_first,
    row_second,
):
    n_dp = lax.axis_size("dp")
    grid = GRIDS[n_dp]
    nz, nx, nc = grid
    d, r, c = lax.axis_index("dp"), lax.axis_index("row"), lax.axis_index("col")
    place = r * 2 + c
    group_len = seq_ids.shape[0]
    slot_rows = qkv_weight.shape[1]
    qkv_width, up_width = qkv_weight.shape[2] // 2, up_weight.shape[2] // 2
    out_rows, down_rows = out_weight.shape[1], down_weight.shape[1]
    bias_widths = qkv_bias.shape[1], up_bias.shape[1]
    cut = out_rows + down_rows // 2

    wa = jnp.stack(
        [
            jnp.concatenate(
                [
                    qkv_weight[:, :, k * qkv_width : (k + 1) * qkv_width],
                    up_weight[:, :, k * up_width : (k + 1) * up_width],
                ],
                2,
            )
            for k in range(2)
        ]
    ).astype(BF)
    wb = jnp.concatenate([out_weight, down_weight], 1).astype(BF)
    wc = jnp.pad(
        jnp.concatenate([qkv_bias, up_bias], 1), ((0, 14), (0, 128 - sum(bias_widths)))
    ).astype(BF)
    vec = jnp.pad(row_vectors, ((0, 0), (0, 2), (0, 0))).reshape(LAYERS * 8, -1)
    hid_all, cot_all, vec_all, wa_own, wb_own = start_exchange(
        n_dp, hidden_in, cotangent, vec, wa, wb
    )
    wa_own = wa_own.reshape(LAYERS, 2 * slot_rows, qkv_width + up_width)
    full_a, full_b, full_c = gather_weights(grid, cut, wa_own, wb_own, wc)
    full_a = full_a.reshape(LAYERS, D, qkv_width + up_width)
    full_b = full_b.reshape(LAYERS, n_dp // 2, out_rows + down_rows, D)
    full_c = full_c.reshape(n_dp, 16, 128)
    vectors = vec_all.reshape(LAYERS, 8, D)
    mats = [
        (
            full_a[k, :, :qkv_width],
            full_a[k, :, qkv_width:],
            full_b[k, :, :out_rows].reshape(-1, D),
            full_b[k, :, out_rows:].reshape(-1, D),
            full_c[:, k, : bias_widths[0]].reshape(-1),
            full_c[:, k, bias_widths[0] : sum(bias_widths)].reshape(-1),
        )
        for k in range(LAYERS)
    ]

    positions, allowed, live_rows = sequence_layout(seq_ids)
    cosine, sine = rope_tables(positions)
    layout = (cosine, sine, allowed)
    quarter = group_len // 4

    def own_rows(array):
        return lax.dynamic_slice_in_dim(array, place * quarter, quarter)

    def add_own(part, rows):
        return lax.dynamic_update_slice_in_dim(
            part, own_rows(part) + rows, place * quarter, axis=0
        ).astype(BF)

    def normed(hat, layer):
        rows = [
            (hat * vectors[layer, 2 * k] + vectors[layer, 2 * k + 1]).astype(BF) for k in range(2)
        ]
        return rows[0], rows[1]

    state_all = hid_all.astype(F32)
    hat_zero, inv_zero = norm_stats(state_all)
    inputs_zero = normed(hat_zero, 0)
    part, cache_zero = layer_forward(*inputs_zero, mats[0], layout)
    state_one, inv_one, hat_low = forward_mid(
        part.astype(BF), own_rows(state_all) + (vectors[0, 4] + vectors[0, 5])
    )
    hat_one = hat_low.astype(F32)
    inputs_one = normed(hat_one, 1)
    part, cache_one = layer_forward(*inputs_one, mats[1], layout)
    bias_one = row_vectors[1, 4] + row_vectors[1, 5]
    hidden_out = (sum_blocks(add_own(part, state_one)) + bias_one).astype(BF)

    rows_grad = (cot_all.astype(F32) * live_rows[:, None]).astype(BF)
    grad_attn_in, grad_mlp_in, ga_one, gb_one, shifts = layer_backward(
        rows_grad, *inputs_one, mats[1], layout, cache_one
    )
    sums_one = vector_sums(grad_attn_in, grad_mlp_in, hat_one, rows_grad, shifts)
    grad_hat = grad_attn_in * vectors[1, 0] + grad_mlp_in * vectors[1, 2]
    grad_one, rows_grad = backward_mid(
        norm_back(grad_hat, hat_one).astype(BF), own_rows(rows_grad).astype(F32), inv_one
    )
    grad_attn_in, grad_mlp_in, ga_zero, gb_zero, shifts = layer_backward(
        rows_grad, *inputs_zero, mats[0], layout, cache_zero
    )
    sums_zero = vector_sums(grad_attn_in, grad_mlp_in, hat_zero, rows_grad, shifts)
    grad_hat = grad_attn_in * vectors[0, 0] + grad_mlp_in * vectors[0, 2]
    grad_state = sum_blocks(add_own(inv_zero * norm_back(grad_hat, hat_zero), grad_one))

    ga = jnp.stack([ga_zero, ga_one]).reshape(LAYERS, nz, nx, nc, 2 * slot_rows, -1)
    gb = jnp.stack(
        [
            jnp.concatenate(
                [pair[0].reshape(-1, out_rows, D), pair[1].reshape(-1, down_rows, D)], 1
            )
            for pair in (gb_zero, gb_one)
        ]
    ).reshape(LAYERS, nz // 2, nx, nc, out_rows + down_rows, D)
    gv = jnp.concatenate([sums_zero, sums_one], 0)
    own_a, own_b, all_v, group_v = sum_grads(grid, cut, ga, gb, gv)
    grad_qkv = jnp.concatenate([own_a[0, ..., :qkv_width], own_a[1, ..., :qkv_width]], 2)
    grad_up = jnp.concatenate([own_a[0, ..., qkv_width:], own_a[1, ..., qkv_width:]], 2)
    group_v = group_v.reshape(LAYERS, VEC_ROWS, D)
    all_v = lax.dynamic_slice_in_dim(
        all_v.reshape(LAYERS, VEC_ROWS, D), r * hidden_in.shape[1], hidden_in.shape[1], axis=2
    )
    vector_grad = jnp.concatenate([all_v[:, :5], all_v[:, 4:5]], 1)
    grad_qkv_bias = lax.dynamic_slice_in_dim(
        group_v[:, 5], d * bias_widths[0], bias_widths[0], axis=1
    )
    grad_up_bias = lax.dynamic_slice_in_dim(
        group_v[:, 6], d * bias_widths[1], bias_widths[1], axis=1
    )
    stacked = (
        grad_qkv.astype(F32),
        own_b[:, :out_rows].astype(F32),
        grad_up.astype(F32),
        own_b[:, out_rows:].astype(F32),
        grad_qkv_bias,
        grad_up_bias,
    )
    qkv_new = adamw(qkv_weight, qkv_first, qkv_second, stacked[0], RATE_MATRIX, DECAY_MATRIX)
    out_new = adamw(out_weight, out_first, out_second, stacked[1], RATE_MATRIX, DECAY_MATRIX)
    up_new = adamw(up_weight, up_first, up_second, stacked[2], RATE_MATRIX, DECAY_MATRIX)
    down_new = adamw(down_weight, down_first, down_second, stacked[3], RATE_MATRIX, DECAY_MATRIX)
    qkv_bias_new = adamw(qkv_bias, qkv_bias_first, qkv_bias_second, stacked[4], RATE_MATRIX, 0.0)
    up_bias_new = adamw(up_bias, up_bias_first, up_bias_second, stacked[5], RATE_MATRIX, 0.0)
    row_new = adamw(row_vectors, row_first, row_second, vector_grad, RATE_VECTOR, 0.0)
    return (
        hidden_out,
        grad_state,
        qkv_new[0],
        qkv_new[1],
        qkv_new[2],
        out_new[0],
        out_new[1],
        out_new[2],
        up_new[0],
        up_new[1],
        up_new[2],
        down_new[0],
        down_new[1],
        down_new[2],
        qkv_bias_new[0],
        qkv_bias_new[1],
        qkv_bias_new[2],
        up_bias_new[0],
        up_bias_new[1],
        up_bias_new[2],
        row_new[0],
        row_new[1],
        row_new[2],
    )


def solution(mesh):
    placed = (
        P(("dp", "col"), "row"),
        P(("dp", "col"), "row"),
        P("dp"),
        P(None, ("row", "dp"), "col"),
        P(None, ("row", "dp"), "col"),
        P(None, ("row", "dp"), "col"),
        P(None, ("col", "dp"), "row"),
        P(None, ("col", "dp"), "row"),
        P(None, ("col", "dp"), "row"),
        P(None, ("row", "dp"), "col"),
        P(None, ("row", "dp"), "col"),
        P(None, ("row", "dp"), "col"),
        P(None, ("col", "dp"), "row"),
        P(None, ("col", "dp"), "row"),
        P(None, ("col", "dp"), "row"),
        P(None, ("col", "row", "dp")),
        P(None, ("col", "row", "dp")),
        P(None, ("col", "row", "dp")),
        P(None, ("col", "row", "dp")),
        P(None, ("col", "row", "dp")),
        P(None, ("col", "row", "dp")),
        P(None, None, "row"),
        P(None, None, "row"),
        P(None, None, "row"),
    )
    return jax.shard_map(
        on_device,
        mesh=mesh,
        in_specs=placed,
        out_specs=(
            P(("dp", "col"), "row"),
            P(("dp", "col"), "row"),
            P(None, ("row", "dp"), "col"),
            P(None, ("row", "dp"), "col"),
            P(None, ("row", "dp"), "col"),
            P(None, ("col", "dp"), "row"),
            P(None, ("col", "dp"), "row"),
            P(None, ("col", "dp"), "row"),
            P(None, ("row", "dp"), "col"),
            P(None, ("row", "dp"), "col"),
            P(None, ("row", "dp"), "col"),
            P(None, ("col", "dp"), "row"),
            P(None, ("col", "dp"), "row"),
            P(None, ("col", "dp"), "row"),
            P(None, ("col", "row", "dp")),
            P(None, ("col", "row", "dp")),
            P(None, ("col", "row", "dp")),
            P(None, ("col", "row", "dp")),
            P(None, ("col", "row", "dp")),
            P(None, ("col", "row", "dp")),
            P(None, None, "row"),
            P(None, None, "row"),
            P(None, None, "row"),
        ),
        check_vma=False,
    )
```

```python
import math
from functools import partial

import jax
import jax.numpy as jnp
from jax import lax
from jax.experimental import pallas as pl
from jax.experimental.pallas import tpu as pltpu
from jax.sharding import PartitionSpec as P

D = 1024
HEAD = 64
ROT = 16
LAYERS = 2
SEQS = 3
STEP = 10


EPS_NORM = 1e-05
EPS_ADAM = 1e-08
BETA_ONE = 0.9
BETA_TWO = 0.95
RATE_MATRIX = 0.06
RATE_VECTOR = 0.6
DECAY_MATRIX = 0.01
ROPE_BASE = 10000.0
MASK_VALUE = -1e30
CONTRACT_ROWS = (((0,), (0,)), ((), ()))
CONTRACT_COLS = (((1,), (1,)), ((), ()))

BF = jnp.bfloat16
F32 = jnp.float32
MESH = pl.DeviceIdType.MESH
GRIDS = {32: (4, 4, 2), 8: (2, 2, 2)}
VEC_ROWS = 8
VMEM_SPEC = pl.BlockSpec(memory_space=pltpu.VMEM)


def params(collective_id, mib):
    return pltpu.CompilerParams(
        collective_id=collective_id, has_side_effects=True, vmem_limit_bytes=mib << 20
    )


def remote(src, dst, sends, recvs, at, device):
    return pltpu.make_async_remote_copy(
        src_ref=src,
        dst_ref=dst,
        send_sem=sends.at[at],
        recv_sem=recvs.at[at],
        device_id=device,
        device_id_type=MESH,
    )


def greet(device):
    pl.semaphore_signal(
        pltpu.get_barrier_semaphore(), inc=1, device_id=device, device_id_type=MESH
    )


def greeted(count):
    pl.semaphore_wait(pltpu.get_barrier_semaphore(), count)


def group_place():
    return lax.axis_index("row") * 2 + lax.axis_index("col")


def group_peer(place, step):
    other = lax.rem(place + step, 4)
    return {"row": other // 2, "col": lax.rem(other, 2)}


def over(lengths, body):
    total = math.prod(lengths)

    def one(index, carry):
        place, rest = [], index
        for length in reversed(lengths):
            place.append(lax.rem(rest, length))
            rest = rest // length
        body(*reversed(place))
        return carry

    lax.fori_loop(0, total, one, 0)


def sequence_layout(group_ids):
    length = group_ids.shape[0]
    labels = jnp.arange(SEQS + 1, dtype=jnp.int32)
    member = (group_ids[:, None] == labels[None, :]).astype(jnp.int32)
    counts = jnp.sum(member, 0, dtype=jnp.int32)
    lower_ids = (labels[None, :] < group_ids[:, None]).astype(jnp.int32)
    starts = jnp.sum(lower_ids * counts[None, :], 1, dtype=jnp.int32)
    places = jnp.arange(length, dtype=jnp.int32)
    positions = places - starts
    allowed = (group_ids[:, None] == group_ids[None, :]) & (places[None, :] <= places[:, None])
    live_rows = (group_ids < SEQS).astype(jnp.float32)
    return (positions, allowed, live_rows)


def rope_tables(positions):
    steps_half = jnp.arange(ROT // 2, dtype=jnp.float32)
    frequency = ROPE_BASE ** (-2.0 * steps_half / ROT)
    angles = positions.astype(jnp.float32)[:, None] * frequency[None, :]
    angles = jnp.concatenate([angles, angles], 1)
    return (jnp.cos(angles), jnp.sin(angles))


def adamw(master, moment_one, moment_two, gradient, step_rate, step_decay):
    one_new = BETA_ONE * moment_one + (1.0 - BETA_ONE) * gradient
    two_new = BETA_TWO * moment_two + (1.0 - BETA_TWO) * gradient * gradient
    one_hat = one_new / (1.0 - BETA_ONE**STEP)
    two_hat = two_new / (1.0 - BETA_TWO**STEP)
    master_new = master - step_rate * (
        one_hat / (jnp.sqrt(two_hat) + EPS_ADAM) + step_decay * master
    )
    return (master_new, one_new, two_new)


class Copies:
    def __init__(self, sends, recvs):
        self.sends, self.recvs, self.count = sends, recvs, 0

    def to(self, src, dst, device):
        copy = remote(src, dst, self.sends, self.recvs, self.count, device)
        self.count += 1
        return copy


class Ring:
    def __init__(self, length, place, device_at):
        self.length, self.place, self.device_at = length, place, device_at
        self.ways = ((0, 1), (1, -1)) if length > 2 else ((0, 1),)

    def at(self, step):
        return lax.rem(self.place + step + self.length, self.length)

    def device(self, step):
        return self.device_at(self.at(step))


class RingGather:
    def __init__(self, copies, ring, views, sources=None, arrived=None):
        self.copies, self.ring, self.views = copies, ring, views
        self.sources, self.arrived = sources, arrived
        self.near, self.far = [[], []], [[], []]

    def start(self):
        for way, step in self.ring.ways:
            for k, view in enumerate(self.views):
                own = view(self.ring.place, None)
                src = self.sources[k] if self.sources else own
                copy = self.copies.to(src, own, self.ring.device(step))
                copy.start()
                self.near[way].append(copy)

    def middle(self):
        for way, step in self.ring.ways:
            for copy in self.near[way]:
                copy.wait_recv()
            came_from = self.ring.at(-step)
            if self.ring.length > 2:
                for view in self.views:
                    ref = view(came_from, way)
                    if ref is not None:
                        copy = self.copies.to(ref, ref, self.ring.device(step))
                        copy.start()
                        self.far[way].append(copy)
            if self.arrived:
                self.arrived(came_from)

    def end(self):
        for copy in self.far[0] + self.far[1]:
            copy.wait_recv()
        if self.arrived and self.ring.length > 2:
            self.arrived(self.ring.at(2))

    def finish(self):
        for copy in self.near[0] + self.near[1] + self.far[0] + self.far[1]:
            copy.wait_send()


class Summand:
    def __init__(self, ref, index, count, width, near, far):
        self.ref, self.index, self.count, self.width = ref, index, count, width
        self.near, self.far = near, far

    def view(self, target, start, width):
        return self.ref.at[self.index(slice(None), target, start, width)]

    def add(self, target, start, width, other):
        def one(lead):
            at = self.index(lead, target, start, width)
            more = other[...] if self.count is None else other[lead]
            self.ref[at] = (self.ref[at].astype(F32) + more.astype(F32)).astype(BF)

        if self.count is None:
            one(None)
        else:
            over((self.count,), one)

    def total(self, lead, target, ways):
        value = self.ref[self.index(lead, target, 0, self.width)].astype(F32)
        for way in range(ways):
            more = self.far[way][...] if self.count is None else self.far[way][lead]
            value = value + more.astype(F32)
        return value


class RingSum:
    def __init__(self, copies, ring, summands):
        self.copies, self.ring, self.summands = copies, ring, summands
        self.near, self.far = [[], []], [[], []]

    def start(self):
        if self.ring.length == 2:
            return
        for way, step in self.ring.ways:
            for s in self.summands:
                half = s.width // 2
                copy = self.copies.to(
                    s.view(self.ring.at(2), way * half, half), s.near[way], self.ring.device(step)
                )
                copy.start()
                self.near[way].append(copy)

    def middle(self):
        for way, step in self.ring.ways:
            target = self.ring.at(step)
            for k, s in enumerate(self.summands):
                if self.ring.length > 2:
                    self.near[way][k].wait_recv()
                    s.add(target, way * (s.width // 2), s.width // 2, s.near[way])
                copy = self.copies.to(
                    s.view(target, 0, s.width), s.far[way], self.ring.device(step)
                )
                copy.start()
                self.far[way].append(copy)

    def end(self):
        for copy in self.far[0] + self.far[1]:
            copy.wait_recv()

    def total(self, k, lead=None):
        return self.summands[k].total(lead, self.ring.place, len(self.ring.ways))

    def finish(self):
        for copy in self.near[0] + self.near[1] + self.far[0] + self.far[1]:
            copy.wait_send()


def lanes_at(start, width):
    if not isinstance(start, int):
        start = pl.multiple_of(start, 128)
    return pl.ds(start, width)


class Slice:
    def __init__(self, grid):
        self.grid = grid
        nz, nx, nc = grid
        d = lax.axis_index("dp")
        self.d, self.z, self.x, self.core = d, d // (nx * nc), lax.rem(d // nc, nx), lax.rem(d, nc)
        self.row, self.col = lax.axis_index("row"), lax.axis_index("col")
        self.half = nz * nx * nc // 2
        self.place = group_place()
        self.zls = nz // 2
        self.partner = self.dp(self.z, self.x, 1 - self.core)
        self.z_ring = Ring(nz, self.z, lambda z: self.dp(z, self.x, self.core))
        self.x_ring = Ring(nx, self.x, lambda x: self.dp(self.z, x, self.core))
        self.y_ring = Ring(4, self.place, lambda q: {"row": q // 2, "col": lax.rem(q, 2)})

    def dp(self, z, x, core):
        _, nx, nc = self.grid
        return {"dp": (z * nx + x) * nc + core}

    def greet_rings(self, rings, whole=False):
        count = 0
        for ring in rings:
            steps = range(1, ring.length) if whole else [step for _, step in ring.ways]
            for step in steps:
                greet(ring.device(step))
                count += 1
        return count


class WeightGather:
    def __init__(self, here, cut, copies, local, wa, wb, wc, full_a, full_b, full_c):
        self.here, self.copies, self.core_copies = here, copies, []
        grid = here.grid
        lanes = wb.shape[-1]
        a_rows, a_lanes, b_rows = wa.shape[0], wa.shape[1], wb.shape[0]
        a_cut = (pl.ds(0, a_rows // 2), pl.ds(a_rows // 2, a_rows // 2))
        b_cut = (pl.ds(0, cut), pl.ds(cut, b_rows - cut))
        z, x, core, zls = here.z, here.x, here.core, here.zls

        def part(width, half):
            return (0, width) if half is None else (half * (width // 2), width // 2)

        def chunk(order, kind, along, half):
            zz, xx = (along, x) if order == 0 else (z, along)
            if kind == "a":
                return full_a.at[zz, xx, core, a_cut[order], pl.ds(*part(a_lanes, half))]
            if kind == "b":
                start, width = part(lanes, half)
                at = lanes_at((zz // zls) * lanes + start, width)
                return full_b.at[lax.rem(zz, zls), xx, core, b_cut[order], at]
            return None if half == 1 else full_c.at[zz, xx, core]

        def line(order, kind, along, half):
            if kind == "a":
                at = pl.ds(*part(a_lanes, half))
                if order == 0:
                    return full_a.at[:, along, core, a_cut[0], at]
                return full_a.at[along, :, core, a_cut[1], at]
            if kind == "b":
                if order == 0:
                    return full_b.at[:, along, core, b_cut[0], pl.ds(*part(2 * lanes, half))]
                start, width = part(lanes, half)
                at = lanes_at((along // zls) * lanes + start, width)
                return full_b.at[lax.rem(along, zls), :, core, b_cut[1], at]
            return None if half == 1 else full_c.at[:, along, core]

        rings = ((here.z_ring, here.x_ring), (here.x_ring, here.z_ring))
        self.first, self.second, self.lines, self.own = [], [], [], []
        for order in range(2):
            kinds = ["a", "b", "c"] if order == 0 and wc is not None else ["a", "b"]
            sources = [wa.at[a_cut[order]], wb.at[b_cut[order]], wc][: len(kinds)]
            chunks = [partial(chunk, order, kind) for kind in kinds]
            lines = [partial(line, order, kind) for kind in kinds]
            for k, view in enumerate(chunks):
                self.own.append(
                    pltpu.make_async_copy(
                        sources[k], view(rings[order][0].place, None), local.at[order * 3 + k]
                    )
                )
            self.first.append(RingGather(copies, rings[order][0], chunks, sources))
            self.second.append(
                RingGather(copies, rings[order][1], lines, None, partial(self.forward, order))
            )
            self.lines.append(lines)

    def forward(self, order, along):
        for view in self.lines[order]:
            ref = view(along, None)
            copy = self.copies.to(ref, ref, self.here.partner)
            copy.start()
            self.core_copies.append(copy)

    def start(self):
        for ring in self.first:
            ring.start()
        for copy in self.own:
            copy.start()

    def first_middle(self):
        for ring in self.first:
            ring.middle()

    def turn(self):
        for copy in self.own:
            copy.wait()
        for order in range(2):
            self.first[order].end()
            self.second[order].start()
            self.forward(order, self.second[order].ring.place)

    def second_middle(self):
        for ring in self.second:
            ring.middle()

    def end(self):
        for ring in self.second:
            ring.end()

    def finish(self):
        for ring in self.first + self.second:
            ring.finish()
        for copy in self.core_copies:
            copy.wait()


def start_kernel(
    grid,
    cut,
    hid,
    cot,
    vec,
    wa,
    wb,
    wc,
    hid_all,
    cot_all,
    vec_all,
    wa_one,
    wb_one,
    full_a,
    full_b,
    full_c,
    wa_zero,
    wb_zero,
    sends,
    recvs,
    local,
):
    here = Slice(grid)
    d, r, c, half = here.d, here.row, here.col, here.half
    rows, lanes = hid.shape
    slot_rows = wa.shape[2]
    dh, dl = d // half, lax.rem(d, half)
    swap_needed = dh != r
    swap_to = {"dp": r * half + dl, "row": dh}
    a_target = r * half + d // 2
    slot = pl.ds(pl.multiple_of(lax.rem(d, 2) * slot_rows, slot_rows), slot_rows)
    a_selfs = [(r == k) & (a_target == d) for k in range(2)]
    a_from = [2 * dl + k for k in range(2)]
    from_selfs = [(dh == r) & (a_from[k] == d) for k in range(2)]

    count = here.greet_rings([here.z_ring, here.x_ring])
    count += here.greet_rings([here.y_ring], whole=True)
    greet(here.partner)
    for k in range(2):

        @pl.when(jnp.logical_not(from_selfs[k]))
        def _():
            greet({"dp": a_from[k], "row": dh})

    @pl.when(swap_needed)
    def _():
        greet(swap_to)

    greeted(
        count + 3 + swap_needed.astype(jnp.int32) - sum(k.astype(jnp.int32) for k in a_selfs)
    )

    copies = Copies(sends, recvs)
    copies.count = 16
    a_own, b_own = (wa_zero, wa_one), (wb_zero, wb_one)

    def a_copy(layer, k):
        return pltpu.make_async_remote_copy(
            src_ref=wa.at[layer, k],
            dst_ref=a_own[layer].at[slot],
            send_sem=sends.at[layer * 8 + k],
            recv_sem=recvs.at[layer * 8 + lax.rem(d, 2)],
            device_id={"dp": a_target, "row": k},
            device_id_type=MESH,
        )

    def a_arrival(layer, k):
        return pltpu.make_async_remote_copy(
            src_ref=wa.at[layer, 0],
            dst_ref=a_own[layer].at[pl.ds(k * slot_rows, slot_rows)],
            send_sem=sends.at[layer * 8],
            recv_sem=recvs.at[layer * 8 + k],
            device_id={"dp": a_from[k], "row": dh},
            device_id_type=MESH,
        )

    def a_local(layer, k):
        return pltpu.make_async_copy(wa.at[layer, k], a_own[layer].at[slot], local.at[8 + layer])

    def swap_copy(layer):
        return remote(wb.at[layer], b_own[layer], sends, recvs, layer * 8 + 2, swap_to)

    def swap_local(layer):
        return pltpu.make_async_copy(wb.at[layer], b_own[layer], local.at[10 + layer])

    def begin(layer):
        for k in range(2):

            @pl.when(jnp.logical_not(a_selfs[k]))
            def _():
                a_copy(layer, k).start()

            @pl.when(a_selfs[k])
            def _():
                a_local(layer, k).start()

        @pl.when(swap_needed)
        def _():
            swap_copy(layer).start()

        @pl.when(jnp.logical_not(swap_needed))
        def _():
            swap_local(layer).start()

    def complete(layer):
        for k in range(2):

            @pl.when(jnp.logical_not(a_selfs[k]))
            def _():
                a_copy(layer, k).wait_send()

            @pl.when(a_selfs[k])
            def _():
                a_local(layer, k).wait()

            @pl.when(jnp.logical_not(from_selfs[k]))
            def _():
                a_arrival(layer, k).wait_recv()

        @pl.when(swap_needed)
        def _():
            swap_copy(layer).wait()

        @pl.when(jnp.logical_not(swap_needed))
        def _():
            swap_local(layer).wait()

    begin(0)
    tokens = pl.ds(pl.multiple_of(c * rows, rows), rows)
    features = pl.ds(pl.multiple_of(r * lanes, lanes), lanes)
    small = []
    for ref, dst in (
        (hid, hid_all.at[tokens, features]),
        (cot, cot_all.at[tokens, features]),
    ):
        for step in range(1, 4):
            small.append(copies.to(ref, dst, here.y_ring.device(step)))
    small.append(copies.to(vec, vec_all.at[:, features], {"row": 1 - r}))
    for copy in small[:3] + small[6:]:
        copy.start()
    own = [
        pltpu.make_async_copy(hid, hid_all.at[tokens, features], local.at[12]),
        pltpu.make_async_copy(cot, cot_all.at[tokens, features], local.at[13]),
        pltpu.make_async_copy(vec, vec_all.at[:, features], local.at[14]),
    ]
    for copy in own:
        copy.start()
    complete(0)
    weights = WeightGather(
        here, cut, copies, local, wa_zero, wb_zero, wc, full_a, full_b, full_c
    )
    weights.start()
    begin(1)
    for copy in small[3:6]:
        copy.start()
    weights.first_middle()
    weights.turn()
    weights.second_middle()
    weights.end()
    for copy in small + own:
        copy.wait()
    complete(1)
    weights.finish()


def full_shapes(grid, a_shape, b_shape):
    nz, nx, nc = grid
    return (
        jax.ShapeDtypeStruct((nz, nx, nc, *a_shape), BF),
        jax.ShapeDtypeStruct((nz // 2, nx, nc, b_shape[0], 2 * b_shape[1]), BF),
    )


def start_exchange(grid, cut, hid, cot, vec, wa, wb, wc):
    rows, lanes = hid.shape
    a_shape, b_shape = (2 * wa.shape[2], wa.shape[3]), wb.shape[1:]
    token_rows = jax.ShapeDtypeStruct((2 * rows, 2 * lanes), BF)
    return pl.pallas_call(
        partial(start_kernel, grid, cut),
        out_shape=(
            token_rows,
            token_rows,
            jax.ShapeDtypeStruct((vec.shape[0], 2 * lanes), F32),
            jax.ShapeDtypeStruct(a_shape, BF),
            jax.ShapeDtypeStruct(b_shape, BF),
            *full_shapes(grid, a_shape, b_shape),
            jax.ShapeDtypeStruct((*grid, *wc.shape), BF),
        ),
        in_specs=[VMEM_SPEC] * 6,
        out_specs=(VMEM_SPEC,) * 8,
        scratch_shapes=[
            pltpu.VMEM(a_shape, BF),
            pltpu.VMEM(b_shape, BF),
            pltpu.SemaphoreType.DMA((96,)),
            pltpu.SemaphoreType.DMA((96,)),
            pltpu.SemaphoreType.DMA((16,)),
        ],
        compiler_params=params(0, 40),
        name="start_exchange",
    )(hid, cot, vec, wa, wb, wc)


def dot(left, right):
    return jnp.dot(left, right, preferred_element_type=F32)


def dot_rows(left, right):
    return lax.dot_general(left, right, CONTRACT_ROWS, preferred_element_type=F32)


def dot_cols(left, right):
    return lax.dot_general(left, right, CONTRACT_COLS, preferred_element_type=F32)


def norm_stats(state):
    width = state.shape[1]
    average = jnp.sum(state, 1, keepdims=True) / width
    spread = jnp.sum(state * state, 1, keepdims=True) / width - average * average
    inv_std = lax.rsqrt(spread + EPS_NORM)
    return ((state - average) * inv_std, inv_std)


def norm_back(grad_hat, hat):
    width = hat.shape[1]
    first = jnp.sum(grad_hat, 1, keepdims=True) / width
    second = jnp.sum(grad_hat * hat, 1, keepdims=True) / width
    return grad_hat - first - hat * second


class Layer:
    def __init__(self, layer, vec, tables, mask, bias, full_a, full_b, sizes):
        self.vec, self.tables, self.mask, self.bias = vec, tables, mask, bias
        self.layer, self.full_a, self.full_b = layer, full_a, full_b
        self.qkv_width, self.up_width, self.out_rows = sizes
        self.heads_here = self.qkv_width // (3 * HEAD)

    def vector(self, k):
        at = self.layer * VEC_ROWS + k
        return self.vec[at : at + 1, :]

    def a_matrix(self, start, width):
        value = self.full_a[:, :, :, :, start : start + width]
        return value.reshape(-1, width)

    def b_matrix(self, low, high, start, width):
        value = self.full_b[:, :, :, low:high, start : start + width]
        return value.reshape(-1, width)

    def out_matrix(self, start, width):
        return self.b_matrix(0, self.out_rows, start, width)

    def down_matrix(self, start, width):
        return self.b_matrix(self.out_rows, self.full_b.shape[3], start, width)

    def inputs(self, hat, attn_in, mlp_in):
        attn_in[...] = (hat * self.vector(0) + self.vector(1)).astype(BF)
        mlp_in[...] = (hat * self.vector(2) + self.vector(3)).astype(BF)

    def project(self, attn_in, joined):
        pair = 6 * HEAD
        cosine, left, right = self.tables
        for start in range(0, self.qkv_width, pair):
            value = dot(attn_in[...], self.a_matrix(start, pair))
            value = value + self.bias[0:1, start : start + pair]
            value = (
                value * cosine[...]
                + pltpu.roll(value, pair - ROT // 2, 1) * left[...]
                + pltpu.roll(value, ROT // 2, 1) * right[...]
            )
            joined[:, start : start + pair] = value.astype(BF)

    def head(self, joined, h):
        start = h * 3 * HEAD
        return [joined[:, start + k * HEAD : start + (k + 1) * HEAD] for k in range(3)]

    def attend(self, joined, probs, heads):
        for h in range(self.heads_here):
            query, key_rows, value_rows = self.head(joined, h)
            scores = dot_cols(query, key_rows) * HEAD**-0.5 + self.mask[...]
            expo = jnp.exp(scores - jnp.max(scores, 1, keepdims=True))
            low = (expo / jnp.sum(expo, 1, keepdims=True)).astype(BF)
            probs[h] = low
            heads[:, h * HEAD : (h + 1) * HEAD] = dot(low, value_rows).astype(BF)

    def units(self, mlp_in, pre, units):
        width = 256
        for start in range(0, self.up_width, width):
            at = slice(start, start + width)
            value = dot(mlp_in[...], self.a_matrix(self.qkv_width + start, width))
            value = value + self.bias[1:2, at]
            pre[:, at] = value
            units[:, at] = (0.5 * value * (1.0 + lax.erf(value * 0.5**0.5))).astype(BF)

    def outputs(self, heads, units, start, width):
        return dot(heads[...], self.out_matrix(start, width)) + dot(
            units[...], self.down_matrix(start, width)
        )

    def branch_back(self, grad, pre, grad_heads, grad_pre):
        grad_heads[...] = dot_cols(grad[...], self.out_matrix(0, D)).astype(BF)
        zls, nx, nc = self.full_b.shape[:3]
        depth = self.full_b.shape[3] - self.out_rows
        count = nx * nc
        for zl in range(zls):
            matrix = self.full_b[zl, :, :, self.out_rows :, :].reshape(-1, D)
            width = depth * count
            for start in range(0, width, 256):
                at = slice(zl * width + start, zl * width + start + 256)
                value = pre[:, at]
                slope = 0.5 * (1.0 + lax.erf(value * 0.5**0.5)) + value * jnp.exp(
                    value * value * -0.5
                ) * ((2.0 * math.pi) ** -0.5)
                pull = dot_cols(grad[...], matrix[start : start + 256])
                grad_pre[:, at] = (pull * slope).astype(BF)

    def attend_back(self, joined, probs, grad_heads, raw, grad_joined):
        for h in range(self.heads_here):
            query, key_rows, value_rows = self.head(joined, h)
            grad = grad_heads[:, h * HEAD : (h + 1) * HEAD]
            low = probs[h]
            high = low.astype(F32)
            grad_probs = dot_cols(grad, value_rows)
            inner = jnp.sum(grad_probs * high, 1, keepdims=True)
            grad_raw = (high * (grad_probs - inner) * HEAD**-0.5).astype(BF)
            start = h * 3 * HEAD
            raw[:, start : start + HEAD] = dot(grad_raw, key_rows)
            raw[:, start + HEAD : start + 2 * HEAD] = dot_rows(grad_raw, query)
            raw[:, start + 2 * HEAD : start + 3 * HEAD] = dot_rows(low, grad)
        pair = 6 * HEAD
        cosine, left, right = self.tables
        for start in range(0, self.qkv_width, pair):
            value = raw[:, start : start + pair]
            value = (
                value * cosine[...]
                + pltpu.roll(value * left[...], ROT // 2, 1)
                + pltpu.roll(value * right[...], pair - ROT // 2, 1)
            )
            grad_joined[:, start : start + pair] = value.astype(BF)

    def inputs_back(self, grad_joined, grad_pre, hat, grad, sums):
        grad_attn_in = dot_cols(grad_joined[...], self.a_matrix(0, self.qkv_width))
        rows = [
            jnp.sum(grad_attn_in * hat, 0, keepdims=True),
            jnp.sum(grad_attn_in, 0, keepdims=True),
        ]
        grad_hat = grad_attn_in * self.vector(0)
        grad_mlp_in = dot_cols(grad_pre[...], self.a_matrix(self.qkv_width, self.up_width))
        rows += [
            jnp.sum(grad_mlp_in * hat, 0, keepdims=True),
            jnp.sum(grad_mlp_in, 0, keepdims=True),
            jnp.sum(grad[...].astype(F32), 0, keepdims=True) * 0.25,
        ]
        for k, row in enumerate(rows):
            sums[k : k + 1, :] = row
        for k, (ref, width) in enumerate(
            ((grad_joined, self.qkv_width), (grad_pre, self.up_width))
        ):
            sums[5 + k : 6 + k, :] = jnp.zeros((1, D), F32)
            sums[5 + k : 6 + k, :width] = jnp.sum(ref[...].astype(F32), 0, keepdims=True)
        sums[7:8, :] = jnp.zeros((1, D), F32)
        return norm_back(grad_hat + grad_mlp_in * self.vector(2), hat)


def grads_a(left, right, out, start):
    width = right.shape[1]
    nz = out.shape[0]
    block = left.shape[1] // nz
    for k in range(nz):
        value = dot_rows(left[:, k * block : (k + 1) * block], right[...]).astype(BF)
        out[k, :, :, :, start : start + width] = value.reshape(*out.shape[1:4], width)


def grads_b(left, right, out, low, high):
    zls = out.shape[0]
    block = left.shape[1] // zls
    for k in range(zls):
        value = dot_rows(left[:, k * block : (k + 1) * block], right[...]).astype(BF)
        out[k, :, :, low:high, :] = value.reshape(*out.shape[1:3], high - low, D)


def rows_index(rows):
    def index(lead, target, start, width):
        return (
            pl.ds(pl.multiple_of(target * rows, rows), rows),
            lanes_at(start, width),
        )

    return index


def blocks_index(rows, lanes):
    def index(lead, target, start, width):
        return (
            pl.ds(pl.multiple_of(lax.rem(target, 2) * rows, rows), rows),
            lanes_at((target // 2) * lanes + start, width),
        )

    return index


def group_sum(here, copies, part, index, width, near, far):
    summand = Summand(part, index, None, width, (near.at[0], near.at[1]), (far.at[0], far.at[1]))
    return RingSum(copies, here.y_ring, [summand])


def group_gather(here, copies, whole, rows):
    def view(target, half):
        width = whole.shape[1]
        start, width = (0, width) if half is None else (half * (width // 2), width // 2)
        return whole.at[pl.ds(pl.multiple_of(target * rows, rows), rows), pl.ds(start, width)]

    return RingGather(copies, here.y_ring, [view])


def own_rows(here, rows):
    return pl.ds(pl.multiple_of(here.place * rows, rows), rows)


def ring_scratch(rows, width):
    return [pltpu.VMEM((2, rows, width // 2), BF), pltpu.VMEM((2, rows, width), BF)]


def first_kernel(
    grid,
    cut,
    sizes,
    hid_all,
    vec,
    cosine,
    left,
    right,
    mask,
    bias,
    full_a,
    full_b,
    wa,
    wb,
    state_new,
    inv_std,
    hat_all,
    joined,
    probs,
    heads,
    pre,
    units,
    next_a,
    next_b,
    attn_in,
    mlp_in,
    part,
    near,
    far,
    sends,
    recvs,
    local,
):
    here = Slice(grid)
    copies = Copies(sends, recvs)
    rows = state_new.shape[0]
    count = here.greet_rings([here.z_ring, here.x_ring, here.y_ring])
    greet(here.partner)
    greeted(count + 1)
    weights = WeightGather(here, cut, copies, local, wa, wb, None, next_a, next_b, None)
    weights.start()
    layer = Layer(0, vec, (cosine, left, right), mask, bias, full_a, full_b, sizes)
    hat, _ = norm_stats(hid_all[...].astype(F32))
    layer.inputs(hat, attn_in, mlp_in)
    layer.project(attn_in, joined)
    weights.first_middle()
    layer.attend(joined, probs, heads)
    weights.turn()
    layer.units(mlp_in, pre, units)
    weights.second_middle()
    for start in (0, D // 2):
        part[:, start : start + D // 2] = layer.outputs(heads, units, start, D // 2).astype(BF)
    summed = group_sum(here, copies, part, rows_index(rows), D, near, far)
    summed.start()
    weights.end()
    summed.middle()
    mine = own_rows(here, rows)
    state = hid_all[mine, :].astype(F32) + layer.vector(4) + layer.vector(5)
    summed.end()
    state = state + summed.total(0)
    state_new[...] = state
    hat, inverse = norm_stats(state)
    inv_std[...] = jnp.broadcast_to(inverse, inv_std.shape)
    hat_all[mine, :] = hat.astype(BF)
    spread = group_gather(here, copies, hat_all, rows)
    spread.start()
    spread.middle()
    spread.end()
    summed.finish()
    spread.finish()
    weights.finish()


def first_layer(grid, cut, sizes, hid_all, vec, tables, mask, bias, full_a, full_b, wa, wb):
    tokens = hid_all.shape[0]
    rows = tokens // 4
    qkv_width, up_width, _ = sizes
    heads_here = qkv_width // (3 * HEAD)
    shape = jax.ShapeDtypeStruct
    return pl.pallas_call(
        partial(first_kernel, grid, cut, sizes),
        out_shape=(
            shape((rows, D), F32),
            shape((rows, 128), F32),
            shape((tokens, D), BF),
            shape((tokens, qkv_width), BF),
            shape((heads_here, tokens, tokens), BF),
            shape((tokens, heads_here * HEAD), BF),
            shape((tokens, up_width), F32),
            shape((tokens, up_width), BF),
            *full_shapes(grid, wa.shape, wb.shape),
        ),
        in_specs=[VMEM_SPEC] * 11,
        out_specs=(VMEM_SPEC,) * 10,
        scratch_shapes=[
            pltpu.VMEM((tokens, D), BF),
            pltpu.VMEM((tokens, D), BF),
            pltpu.VMEM((tokens, D), BF),
            *ring_scratch(rows, D),
            pltpu.SemaphoreType.DMA((64,)),
            pltpu.SemaphoreType.DMA((64,)),
            pltpu.SemaphoreType.DMA((6,)),
        ],
        compiler_params=params(1, 56),
        name="first_layer",
    )(hid_all, vec, *tables, mask, bias, full_a, full_b, wa, wb)


def last_kernel(
    grid,
    sizes,
    hat_all,
    vec,
    cosine,
    left,
    right,
    mask,
    bias,
    full_a,
    full_b,
    state,
    inv_std,
    cot,
    live,
    hidden,
    grad_new,
    grad_all,
    ga,
    gb,
    sums,
    attn_in,
    mlp_in,
    joined,
    probs,
    heads,
    pre,
    units,
    part,
    back,
    grad,
    grad_heads,
    grad_pre,
    raw,
    grad_joined,
    near,
    far,
    near_back,
    far_back,
    sends,
    recvs,
):
    here = Slice(grid)
    copies = Copies(sends, recvs)
    rows = state.shape[0]
    greeted(here.greet_rings([here.y_ring]))
    layer = Layer(1, vec, (cosine, left, right), mask, bias, full_a, full_b, sizes)
    layer.inputs(hat_all[...].astype(F32), attn_in, mlp_in)
    layer.project(attn_in, joined)
    layer.attend(joined, probs, heads)
    layer.units(mlp_in, pre, units)
    mine = own_rows(here, rows)
    for start in (0, D // 2):
        part[:, start : start + D // 2] = layer.outputs(heads, units, start, D // 2).astype(BF)
    part[mine, :] = (part[mine, :].astype(F32) + state[...]).astype(BF)
    summed = group_sum(
        here, copies, part, blocks_index(2 * rows, D // 2), D // 2, near, far
    )
    summed.start()
    grad[...] = (cot[...].astype(F32) * live[:, :1]).astype(BF)
    layer.branch_back(grad, pre, grad_heads, grad_pre)
    summed.middle()
    layer.attend_back(joined, probs, grad_heads, raw, grad_joined)
    back[...] = layer.inputs_back(
        grad_joined, grad_pre, hat_all[...].astype(F32), grad, sums
    ).astype(BF)
    summed_back = group_sum(here, copies, back, rows_index(rows), D, near_back, far_back)
    summed_back.start()
    summed.end()
    features = pl.ds(pl.multiple_of(here.row * (D // 2), D // 2), D // 2)
    bias_sum = vec[VEC_ROWS + 4 : VEC_ROWS + 5, features] + vec[VEC_ROWS + 5 : VEC_ROWS + 6, features]
    hidden[...] = (summed.total(0) + bias_sum).astype(BF)
    grads_a(attn_in, grad_joined, ga, 0)
    summed_back.middle()
    grads_a(mlp_in, grad_pre, ga, grad_joined.shape[1])
    summed_back.end()
    total = grad[mine, :].astype(F32) + inv_std[:, :1] * summed_back.total(0)
    grad_new[...] = total
    grad_all[mine, :] = total.astype(BF)
    spread = group_gather(here, copies, grad_all, rows)
    spread.start()
    grads_b(heads, grad, gb, 0, sizes[2])
    spread.middle()
    grads_b(units, grad, gb, sizes[2], gb.shape[3])
    spread.end()
    for ring in (summed, summed_back, spread):
        ring.finish()


def last_layer(
    grid, sizes, hat_all, vec, tables, mask, bias, full_a, full_b, state, inv_std, cot, live
):
    tokens = hat_all.shape[0]
    rows = tokens // 4
    qkv_width, up_width, _ = sizes
    heads_here = qkv_width // (3 * HEAD)
    shape = jax.ShapeDtypeStruct

    def low(*dims):
        return pltpu.VMEM(dims, BF)

    return pl.pallas_call(
        partial(last_kernel, grid, sizes),
        out_shape=(
            shape((2 * rows, D // 2), BF),
            shape((rows, D), F32),
            shape((tokens, D), BF),
            shape(full_a.shape, BF),
            shape(full_b.shape, BF),
            shape((VEC_ROWS, D), F32),
        ),
        in_specs=[VMEM_SPEC] * 13,
        out_specs=(VMEM_SPEC,) * 6,
        scratch_shapes=[
            low(tokens, D),
            low(tokens, D),
            low(tokens, qkv_width),
            low(heads_here, tokens, tokens),
            low(tokens, heads_here * HEAD),
            pltpu.VMEM((tokens, up_width), F32),
            low(tokens, up_width),
            low(tokens, D),
            low(tokens, D),
            low(tokens, D),
            low(tokens, heads_here * HEAD),
            low(tokens, up_width),
            pltpu.VMEM((tokens, qkv_width), F32),
            low(tokens, qkv_width),
            *ring_scratch(2 * rows, D // 2),
            *ring_scratch(rows, D),
            pltpu.SemaphoreType.DMA((32,)),
            pltpu.SemaphoreType.DMA((32,)),
        ],
        compiler_params=params(2, 56),
        name="last_layer",
    )(hat_all, vec, *tables, mask, bias, full_a, full_b, state, inv_std, cot, live)


class GradSum:
    def __init__(self, here, cut, copies, kind, g, s, buffers):
        self.here, self.copies, self.kind, self.g, self.s = here, copies, kind, g, s
        self.near, self.far, self.mid, self.near_two, self.far_two, self.fin = buffers
        rows = g.shape[3]
        first = rows // 2 if kind == "a" else cut
        self.cuts = (pl.ds(0, first), pl.ds(first, rows - first))
        self.full = g.shape[4]
        self.lanes = self.full // 2
        self.lines, self.turns = [None, None], [None, None]

    def start(self):
        self.core = []
        for order in range(2):
            copy = self.copies.to(
                self.g.at[:, :, 1 - self.here.core, self.cuts[order]],
                self.s.at[:, :, self.cuts[order]],
                self.here.partner,
            )
            copy.start()
            self.core.append(copy)

    def line(self, order):
        here, at, zls = self.here, self.cuts[order], self.here.zls
        self.core[order].wait_recv()

        def add(zz, xx):
            self.s[zz, xx, at] = (
                self.s[zz, xx, at].astype(F32) + self.g[zz, xx, here.core, at].astype(F32)
            ).astype(BF)

        over(self.s.shape[:2], add)
        nx = self.s.shape[1]
        if order == 0:
            ring, count, width = here.x_ring, self.s.shape[0], self.full

            def index(lead, target, start, width):
                return (lead, target, at, lanes_at(start, width))

        elif self.kind == "a":
            ring, count, width = here.z_ring, nx, self.full

            def index(lead, target, start, width):
                return (target, lead, at, lanes_at(start, width))

        else:
            ring, count, width = here.z_ring, nx, self.lanes

            def index(lead, target, start, width):
                return (
                    lax.rem(target, zls),
                    lead,
                    at,
                    lanes_at((target // zls) * self.lanes + start, width),
                )

        summand = Summand(
            self.s,
            index,
            count,
            width,
            (self.near[order].at[0], self.near[order].at[1]),
            (self.far[order].at[0], self.far[order].at[1]),
        )
        self.lines[order] = RingSum(self.copies, ring, [summand])
        self.lines[order].start()

    def line_middle(self, order):
        self.lines[order].middle()

    def turn(self, order):
        here, zls, mid = self.here, self.here.zls, self.mid[order]
        line = self.lines[order]
        line.end()

        def put(lead):
            mid[lead] = line.total(0, lead).astype(BF)

        over(mid.shape[:1], put)
        ring = here.z_ring if order == 0 else here.x_ring
        if self.kind == "b" and order == 0:

            def index(lead, target, start, width):
                return (
                    lax.rem(target, zls),
                    slice(None),
                    lanes_at((target // zls) * self.lanes + start, width),
                )

        else:

            def index(lead, target, start, width):
                return (target, slice(None), lanes_at(start, width))

        summand = Summand(
            mid,
            index,
            None,
            self.full if self.kind == "a" else self.lanes,
            (self.near_two[order].at[0], self.near_two[order].at[1]),
            (self.far_two[order].at[0], self.far_two[order].at[1]),
        )
        self.turns[order] = RingSum(self.copies, ring, [summand])
        self.turns[order].start()

    def turn_middle(self, order):
        self.turns[order].middle()

    def end(self, order):
        self.turns[order].end()
        value = self.turns[order].total(0).astype(BF)
        if self.kind == "a":
            self.fin[order] = value
        else:
            self.fin[self.cuts[order]] = value

    def finish(self):
        for copy in self.core:
            copy.wait_send()
        for order in range(2):
            self.lines[order].finish()
            self.turns[order].finish()


def grad_buffers(grid, cut, g_shape, kind):
    nz, nx, _ = grid
    rows, full = g_shape[3:]
    zls = g_shape[0]
    first = rows // 2 if kind == "a" else cut
    lanes = full if kind == "a" else full // 2
    cuts = (first, rows - first)

    def low(*dims):
        return pltpu.VMEM(dims, BF)

    counts = (zls, nx)
    widths = (full, lanes)
    fin = low(2, first, full) if kind == "a" else low(rows, lanes)
    return [
        low(zls, nx, rows, full),
        *[low(2, counts[o], cuts[o], widths[o] // 2) for o in range(2)],
        *[low(2, counts[o], cuts[o], widths[o]) for o in range(2)],
        *[low(counts[o], cuts[o], widths[o]) for o in range(2)],
        *[low(2, cuts[o], lanes // 2) for o in range(2)],
        *[low(2, cuts[o], lanes) for o in range(2)],
        fin,
    ]


def grad_sum(here, cut, copies, kind, g, refs):
    s, near0, near1, far0, far1, mid0, mid1, low0, low1, top0, top1, fin = refs
    return GradSum(
        here,
        cut,
        copies,
        kind,
        g,
        s,
        ((near0, near1), (far0, far1), (mid0, mid1), (low0, low1), (top0, top1), fin),
    )


def final_kernel(grid, cut, sizes, *refs):
    (
        hid_all,
        vec,
        cosine,
        left,
        right,
        mask,
        bias,
        full_a,
        full_b,
        joined,
        probs,
        heads,
        pre,
        units,
        grad,
        grad_one,
        ga_one,
        gb_one,
        sums_one,
    ) = refs[:19]
    grad_out, out_a, out_b, out_v = refs[19:23]
    (
        ga,
        gb,
        sums,
        hat_ref,
        attn_in,
        mlp_in,
        back,
        grad_heads,
        grad_pre,
        raw,
        grad_joined,
        near,
        far,
        v_core,
        v_line,
        v_last,
        v_group,
    ) = refs[23:40]
    buffers = refs[40:88]
    sends, recvs, local = refs[88:]
    here = Slice(grid)
    nz, nx, _ = grid
    copies = Copies(sends, recvs)
    rows = grad_one.shape[0]
    d, r, half = here.d, here.row, here.half
    dh, dl = d // half, lax.rem(d, half)
    swap_needed = dh != r
    swap_to = {"dp": r * half + dl, "row": dh}
    a_target = [{"dp": 2 * dl + s, "row": dh} for s in range(2)]
    to_self = [(dh == r) & (2 * dl + s == d) for s in range(2)]
    a_source = r * half + d // 2
    from_self = [(r == k) & (a_source == d) for k in range(2)]

    count = here.greet_rings([here.z_ring, here.x_ring, here.y_ring], whole=True)
    greet(here.partner)
    for k in range(2):

        @pl.when(jnp.logical_not(from_self[k]))
        def _():
            greet({"dp": a_source, "row": k})

    @pl.when(swap_needed)
    def _():
        greet(swap_to)

    greeted(
        count + 3 + swap_needed.astype(jnp.int32) - sum(s.astype(jnp.int32) for s in to_self)
    )
    copies.count = 24

    sum_a_one = grad_sum(here, cut, copies, "a", ga_one, buffers[0:12])
    sum_b_one = grad_sum(here, cut, copies, "b", gb_one, buffers[12:24])
    sum_a = grad_sum(here, cut, copies, "a", ga, buffers[24:36])
    sum_b = grad_sum(here, cut, copies, "b", gb, buffers[36:48])

    def owner_copy(layer, fin, order):
        return pltpu.make_async_remote_copy(
            src_ref=fin.at[order],
            dst_ref=out_a.at[layer, r],
            send_sem=sends.at[layer * 8 + order],
            recv_sem=recvs.at[layer * 8 + r],
            device_id=a_target[order],
            device_id_type=MESH,
        )

    def owner_arrival(layer, fin, k):
        return pltpu.make_async_remote_copy(
            src_ref=fin.at[0],
            dst_ref=out_a.at[layer, k],
            send_sem=sends.at[layer * 8],
            recv_sem=recvs.at[layer * 8 + k],
            device_id={"dp": a_source, "row": k},
            device_id_type=MESH,
        )

    def owner_local(layer, fin, order):
        return pltpu.make_async_copy(fin.at[order], out_a.at[layer, r], local.at[layer])

    def swap_copy(layer, fin):
        return remote(fin, out_b.at[layer], sends, recvs, layer * 8 + 2, swap_to)

    def swap_local(layer, fin):
        return pltpu.make_async_copy(fin, out_b.at[layer], local.at[2 + layer])

    def hand_a(layer, fin, order):
        @pl.when(jnp.logical_not(to_self[order]))
        def _():
            owner_copy(layer, fin, order).start()

        @pl.when(to_self[order])
        def _():
            owner_local(layer, fin, order).start()

    def hand_b(layer, fin):
        @pl.when(swap_needed)
        def _():
            swap_copy(layer, fin).start()

        @pl.when(jnp.logical_not(swap_needed))
        def _():
            swap_local(layer, fin).start()

    def handed(layer, fin_a, fin_b):
        for k in range(2):

            @pl.when(jnp.logical_not(to_self[k]))
            def _():
                owner_copy(layer, fin_a, k).wait_send()

            @pl.when(to_self[k])
            def _():
                owner_local(layer, fin_a, k).wait()

            @pl.when(jnp.logical_not(from_self[k]))
            def _():
                owner_arrival(layer, fin_a, k).wait_recv()

        @pl.when(swap_needed)
        def _():
            swap_copy(layer, fin_b).wait()

        @pl.when(jnp.logical_not(swap_needed))
        def _():
            swap_local(layer, fin_b).wait()

    def phase(name, which):
        for order in range(2):
            for one in which:
                getattr(one, name)(order)

    ones = [sum_a_one, sum_b_one]
    for one in ones:
        one.start()
    layer = Layer(0, vec, (cosine, left, right), mask, bias, full_a, full_b, sizes)
    grads_b(heads, grad, gb, 0, sizes[2])
    grads_b(units, grad, gb, sizes[2], gb.shape[3])
    phase("line", ones)
    sum_b.start()
    hat, inverse = norm_stats(hid_all[...].astype(F32))
    hat_ref[...] = hat
    layer.inputs(hat, attn_in, mlp_in)
    layer.branch_back(grad, pre, grad_heads, grad_pre)
    phase("line_middle", ones)
    layer.attend_back(joined, probs, grad_heads, raw, grad_joined)
    phase("turn", ones)
    phase("line", [sum_b])
    grads_a(attn_in, grad_joined, ga, 0)
    grads_a(mlp_in, grad_pre, ga, grad_joined.shape[1])
    phase("turn_middle", ones)
    sum_a.start()
    phase("line_middle", [sum_b])
    value = layer.inputs_back(grad_joined, grad_pre, hat_ref[...], grad, sums)
    _, inverse = norm_stats(hid_all[...].astype(F32))
    back[...] = (inverse * value).astype(BF)
    mine = own_rows(here, rows)
    back[mine, :] = (back[mine, :].astype(F32) + grad_one[...]).astype(BF)
    summed = group_sum(
        here, copies, back, blocks_index(2 * rows, D // 2), D // 2, near, far
    )
    summed.start()
    v_lanes = D // 2
    v_mine = pl.ds(pl.multiple_of(here.core * v_lanes, v_lanes), v_lanes)
    v_other = pl.ds(pl.multiple_of((1 - here.core) * v_lanes, v_lanes), v_lanes)
    v_copies = [
        copies.to(sums.at[:, v_other], v_core.at[0], here.partner),
        copies.to(sums_one.at[:, v_other], v_core.at[1], here.partner),
    ]
    for copy in v_copies:
        copy.start()
    phase("line", [sum_a])
    for order in range(2):
        sum_a_one.end(order)
        sum_b_one.end(order)
        hand_a(1, sum_a_one.fin, order)
    hand_b(1, sum_b_one.fin)
    for copy in v_copies:
        copy.wait()
    v_line[here.x, 0:VEC_ROWS] = v_core[0] + sums[:, v_mine]
    v_line[here.x, VEC_ROWS:] = v_core[1] + sums_one[:, v_mine]
    v_x = [copies.to(v_line.at[here.x], v_line.at[here.x], here.x_ring.device(k)) for k in range(1, nx)]
    for copy in v_x:
        copy.start()
    phase("turn", [sum_b])
    summed.middle()
    phase("line_middle", [sum_a])
    for copy in v_x:
        copy.wait()
    total = v_line[0]
    for k in range(1, nx):
        total = total + v_line[k]
    v_last[here.z] = total
    v_z = [copies.to(v_last.at[here.z], v_last.at[here.z], here.z_ring.device(k)) for k in range(1, nz)]
    for copy in v_z:
        copy.start()
    phase("turn_middle", [sum_b])
    summed.end()
    grad_out[...] = summed.total(0)
    phase("turn", [sum_a])
    for copy in v_z:
        copy.wait()
    total = v_last[0]
    for k in range(1, nz):
        total = total + v_last[k]
    v_group[here.place] = total
    v_y = [
        copies.to(v_group.at[here.place], v_group.at[here.place], here.y_ring.device(k))
        for k in range(1, 4)
    ]
    for copy in v_y:
        copy.start()
    for order in range(2):
        sum_b.end(order)
    hand_b(0, sum_b.fin)
    phase("turn_middle", [sum_a])
    for copy in v_y:
        copy.wait()
    total = v_group[0]
    for k in range(1, 4):
        total = total + v_group[k]
    out_v[0, :, v_mine] = total
    out_v[1, :, v_mine] = v_group[here.place]
    v_swap = copies.to(out_v.at[:, :, v_mine], out_v.at[:, :, v_mine], here.partner)
    v_swap.start()
    for order in range(2):
        sum_a.end(order)
        hand_a(0, sum_a.fin, order)
    v_swap.wait()
    handed(1, sum_a_one.fin, sum_b_one.fin)
    handed(0, sum_a.fin, sum_b.fin)
    summed.finish()
    for one in (sum_a_one, sum_b_one, sum_a, sum_b):
        one.finish()


def final_layer(
    grid,
    cut,
    sizes,
    hid_all,
    vec,
    tables,
    mask,
    bias,
    full_a,
    full_b,
    cache,
    grad_all,
    grad_one,
    ga_one,
    gb_one,
    sums_one,
):
    nz, nx, _ = grid
    tokens = hid_all.shape[0]
    rows = tokens // 4
    qkv_width, up_width, _ = sizes
    heads_here = qkv_width // (3 * HEAD)
    shape = jax.ShapeDtypeStruct
    a_rows, a_lanes = full_a.shape[3:]
    b_rows, b_lanes = full_b.shape[3:]

    def low(*dims):
        return pltpu.VMEM(dims, BF)

    def high(*dims):
        return pltpu.VMEM(dims, F32)

    buffers_a = grad_buffers(grid, cut, full_a.shape, "a")
    buffers_b = grad_buffers(grid, cut, full_b.shape, "b")
    return pl.pallas_call(
        partial(final_kernel, grid, cut, sizes),
        out_shape=(
            shape((2 * rows, D // 2), F32),
            shape((LAYERS, 2, a_rows // 2, a_lanes), BF),
            shape((LAYERS, b_rows, b_lanes // 2), BF),
            shape((2, LAYERS * VEC_ROWS, D), F32),
        ),
        in_specs=[VMEM_SPEC] * 19,
        out_specs=(VMEM_SPEC,) * 4,
        scratch_shapes=[
            low(*full_a.shape),
            low(*full_b.shape),
            high(VEC_ROWS, D),
            high(tokens, D),
            low(tokens, D),
            low(tokens, D),
            low(tokens, D),
            low(tokens, heads_here * HEAD),
            low(tokens, up_width),
            high(tokens, qkv_width),
            low(tokens, qkv_width),
            *ring_scratch(2 * rows, D // 2),
            high(2, VEC_ROWS, D // 2),
            high(nx, LAYERS * VEC_ROWS, D // 2),
            high(nz, LAYERS * VEC_ROWS, D // 2),
            high(4, LAYERS * VEC_ROWS, D // 2),
            *buffers_a,
            *buffers_b,
            *buffers_a,
            *buffers_b,
            pltpu.SemaphoreType.DMA((128,)),
            pltpu.SemaphoreType.DMA((128,)),
            pltpu.SemaphoreType.DMA((4,)),
        ],
        compiler_params=params(3, 60),
        name="final_layer",
    )(
        hid_all,
        vec,
        *tables,
        mask,
        bias,
        full_a,
        full_b,
        *cache,
        grad_all,
        grad_one,
        ga_one,
        gb_one,
        sums_one,
    )


def rope_lanes(cosine, sine):
    half = ROT // 2
    length = cosine.shape[0]
    ones = jnp.ones((length, HEAD), F32)
    zeros = jnp.zeros((length, HEAD), F32)

    def pair(rotated, rest):
        block = jnp.concatenate([rotated, rest[:, ROT:]], 1)
        return jnp.concatenate([block, block, rest] * 2, 1)

    return (
        pair(cosine, ones),
        pair(jnp.concatenate([-sine[:, :half], zeros[:, :half]], 1), zeros),
        pair(jnp.concatenate([zeros[:, :half], sine[:, half:]], 1), zeros),
    )


def on_device(
    hidden_in,
    cotangent,
    seq_ids,
    qkv_weight,
    qkv_first,
    qkv_second,
    out_weight,
    out_first,
    out_second,
    up_weight,
    up_first,
    up_second,
    down_weight,
    down_first,
    down_second,
    qkv_bias,
    qkv_bias_first,
    qkv_bias_second,
    up_bias,
    up_bias_first,
    up_bias_second,
    row_vectors,
    row_first,
    row_second,
):
    n_dp = lax.axis_size("dp")
    grid = GRIDS[n_dp]
    d, r = lax.axis_index("dp"), lax.axis_index("row")
    group_len = seq_ids.shape[0]
    qkv_width, up_width = qkv_weight.shape[2] // 2, up_weight.shape[2] // 2
    out_rows, down_rows = out_weight.shape[1], down_weight.shape[1]
    bias_widths = qkv_bias.shape[1], up_bias.shape[1]
    cut = out_rows + down_rows // 2
    sizes = (qkv_width, up_width, out_rows)

    wa = jnp.stack(
        [
            jnp.concatenate(
                [
                    qkv_weight[:, :, k * qkv_width : (k + 1) * qkv_width],
                    up_weight[:, :, k * up_width : (k + 1) * up_width],
                ],
                2,
            )
            for k in range(2)
        ],
        1,
    ).astype(BF)
    wb = jnp.concatenate([out_weight, down_weight], 1).astype(BF)
    wc = jnp.pad(
        jnp.concatenate([qkv_bias, up_bias], 1), ((0, 14), (0, -sum(bias_widths) % 128))
    ).astype(BF)
    vec = jnp.pad(row_vectors, ((0, 0), (0, 2), (0, 0))).reshape(LAYERS * VEC_ROWS, -1)
    hid_all, cot_all, vec, wa_one, wb_one, full_a, full_b, full_c = start_exchange(
        grid, cut, hidden_in, cotangent, vec, wa, wb, wc
    )
    full_c = full_c.reshape(n_dp, *wc.shape)
    biases = []
    for k in range(LAYERS):
        rows = [
            full_c[:, k, : bias_widths[0]].reshape(1, -1),
            full_c[:, k, bias_widths[0] : sum(bias_widths)].reshape(1, -1),
        ]
        biases.append(
            jnp.concatenate([jnp.pad(v, ((0, 0), (0, D - v.shape[1]))) for v in rows], 0).astype(F32)
        )

    positions, allowed, live_rows = sequence_layout(seq_ids)
    tables = rope_lanes(*rope_tables(positions))
    mask = jnp.where(allowed, 0.0, MASK_VALUE).astype(F32)
    live = jnp.broadcast_to(live_rows[:, None], (group_len, 128))

    state_one, inv_one, hat_one, *cache, next_a, next_b = first_layer(
        grid, cut, sizes, hid_all, vec, tables, mask, biases[0], full_a, full_b, wa_one, wb_one
    )
    hidden_out, grad_one, grad_all, ga_one, gb_one, sums_one = last_layer(
        grid,
        sizes,
        hat_one,
        vec,
        tables,
        mask,
        biases[1],
        next_a,
        next_b,
        state_one,
        inv_one,
        cot_all,
        live,
    )
    grad_state, own_a, own_b, all_v = final_layer(
        grid,
        cut,
        sizes,
        hid_all,
        vec,
        tables,
        mask,
        biases[0],
        full_a,
        full_b,
        cache,
        grad_all,
        grad_one,
        ga_one,
        gb_one,
        sums_one,
    )
    grad_qkv = jnp.concatenate([own_a[:, 0, :, :qkv_width], own_a[:, 1, :, :qkv_width]], 2)
    grad_up = jnp.concatenate([own_a[:, 0, :, qkv_width:], own_a[:, 1, :, qkv_width:]], 2)
    all_v = all_v.reshape(2, LAYERS, VEC_ROWS, D)
    lanes = hidden_in.shape[1]
    vector_grad = lax.dynamic_slice_in_dim(all_v[0], r * lanes, lanes, axis=2)
    vector_grad = jnp.concatenate([vector_grad[:, :5], vector_grad[:, 4:5]], 1)
    grad_qkv_bias = lax.dynamic_slice_in_dim(
        all_v[1, :, 5], d * bias_widths[0], bias_widths[0], axis=1
    )
    grad_up_bias = lax.dynamic_slice_in_dim(
        all_v[1, :, 6], d * bias_widths[1], bias_widths[1], axis=1
    )
    stacked = (
        grad_qkv.astype(F32),
        own_b[:, :out_rows].astype(F32),
        grad_up.astype(F32),
        own_b[:, out_rows:].astype(F32),
        grad_qkv_bias,
        grad_up_bias,
    )
    qkv_new = adamw(qkv_weight, qkv_first, qkv_second, stacked[0], RATE_MATRIX, DECAY_MATRIX)
    out_new = adamw(out_weight, out_first, out_second, stacked[1], RATE_MATRIX, DECAY_MATRIX)
    up_new = adamw(up_weight, up_first, up_second, stacked[2], RATE_MATRIX, DECAY_MATRIX)
    down_new = adamw(down_weight, down_first, down_second, stacked[3], RATE_MATRIX, DECAY_MATRIX)
    qkv_bias_new = adamw(qkv_bias, qkv_bias_first, qkv_bias_second, stacked[4], RATE_MATRIX, 0.0)
    up_bias_new = adamw(up_bias, up_bias_first, up_bias_second, stacked[5], RATE_MATRIX, 0.0)
    row_new = adamw(row_vectors, row_first, row_second, vector_grad, RATE_VECTOR, 0.0)
    return (
        hidden_out,
        grad_state,
        qkv_new[0],
        qkv_new[1],
        qkv_new[2],
        out_new[0],
        out_new[1],
        out_new[2],
        up_new[0],
        up_new[1],
        up_new[2],
        down_new[0],
        down_new[1],
        down_new[2],
        qkv_bias_new[0],
        qkv_bias_new[1],
        qkv_bias_new[2],
        up_bias_new[0],
        up_bias_new[1],
        up_bias_new[2],
        row_new[0],
        row_new[1],
        row_new[2],
    )


def solution(mesh):
    placed = (
        P(("dp", "col"), "row"),
        P(("dp", "col"), "row"),
        P("dp"),
        P(None, ("row", "dp"), "col"),
        P(None, ("row", "dp"), "col"),
        P(None, ("row", "dp"), "col"),
        P(None, ("col", "dp"), "row"),
        P(None, ("col", "dp"), "row"),
        P(None, ("col", "dp"), "row"),
        P(None, ("row", "dp"), "col"),
        P(None, ("row", "dp"), "col"),
        P(None, ("row", "dp"), "col"),
        P(None, ("col", "dp"), "row"),
        P(None, ("col", "dp"), "row"),
        P(None, ("col", "dp"), "row"),
        P(None, ("col", "row", "dp")),
        P(None, ("col", "row", "dp")),
        P(None, ("col", "row", "dp")),
        P(None, ("col", "row", "dp")),
        P(None, ("col", "row", "dp")),
        P(None, ("col", "row", "dp")),
        P(None, None, "row"),
        P(None, None, "row"),
        P(None, None, "row"),
    )
    return jax.shard_map(
        on_device,
        mesh=mesh,
        in_specs=placed,
        out_specs=(
            P(("dp", "col"), "row"),
            P(("dp", "col"), "row"),
            P(None, ("row", "dp"), "col"),
            P(None, ("row", "dp"), "col"),
            P(None, ("row", "dp"), "col"),
            P(None, ("col", "dp"), "row"),
            P(None, ("col", "dp"), "row"),
            P(None, ("col", "dp"), "row"),
            P(None, ("row", "dp"), "col"),
            P(None, ("row", "dp"), "col"),
            P(None, ("row", "dp"), "col"),
            P(None, ("col", "dp"), "row"),
            P(None, ("col", "dp"), "row"),
            P(None, ("col", "dp"), "row"),
            P(None, ("col", "row", "dp")),
            P(None, ("col", "row", "dp")),
            P(None, ("col", "row", "dp")),
            P(None, ("col", "row", "dp")),
            P(None, ("col", "row", "dp")),
            P(None, ("col", "row", "dp")),
            P(None, None, "row"),
            P(None, None, "row"),
            P(None, None, "row"),
        ),
        check_vma=False,
    )
```

```python
import math
from functools import partial
from types import SimpleNamespace

import jax
import jax.numpy as jnp
from jax import lax
from jax.experimental import pallas as pl
from jax.experimental.pallas import tpu as pltpu
from jax.sharding import PartitionSpec as P

D = 1024
HEAD = 64
ROT = 16
LAYERS = 2
SEQS = 3
STEP = 10


EPS_NORM = 1e-05
EPS_ADAM = 1e-08
BETA_ONE = 0.9
BETA_TWO = 0.95
RATE_MATRIX = 0.06
RATE_VECTOR = 0.6
DECAY_MATRIX = 0.01
ROPE_BASE = 10000.0
MASK_VALUE = -1e30
CONTRACT_ROWS = (((0,), (0,)), ((), ()))
CONTRACT_COLS = (((1,), (1,)), ((), ()))

BF = jnp.bfloat16
F32 = jnp.float32
MESH = pl.DeviceIdType.MESH
GRIDS = {32: (4, 4, 2), 8: (2, 2, 2)}
VEC_ROWS = 8
VMEM_SPEC = pl.BlockSpec(memory_space=pltpu.VMEM)


def params(collective_id, mib):
    return pltpu.CompilerParams(
        collective_id=collective_id, has_side_effects=True, vmem_limit_bytes=mib << 20
    )


def remote(src, dst, sends, recvs, at, device):
    return pltpu.make_async_remote_copy(
        src_ref=src,
        dst_ref=dst,
        send_sem=sends.at[at],
        recv_sem=recvs.at[at],
        device_id=device,
        device_id_type=MESH,
    )


def greet(device):
    pl.semaphore_signal(
        pltpu.get_barrier_semaphore(), inc=1, device_id=device, device_id_type=MESH
    )


def greeted(count):
    pl.semaphore_wait(pltpu.get_barrier_semaphore(), count)


def group_place():
    return lax.axis_index("row") * 2 + lax.axis_index("col")


def group_peer(place, step):
    other = lax.rem(place + step, 4)
    return {"row": other // 2, "col": lax.rem(other, 2)}


def over(lengths, body):
    total = math.prod(lengths)

    def one(index, carry):
        place, rest = [], index
        for length in reversed(lengths):
            place.append(lax.rem(rest, length))
            rest = rest // length
        body(*reversed(place))
        return carry

    lax.fori_loop(0, total, one, 0)


def adamw(master, moment_one, moment_two, gradient, step_rate, step_decay):
    one_new = BETA_ONE * moment_one + (1.0 - BETA_ONE) * gradient
    two_new = BETA_TWO * moment_two + (1.0 - BETA_TWO) * gradient * gradient
    one_hat = one_new / (1.0 - BETA_ONE**STEP)
    two_hat = two_new / (1.0 - BETA_TWO**STEP)
    master_new = master - step_rate * (
        one_hat / (jnp.sqrt(two_hat) + EPS_ADAM) + step_decay * master
    )
    return (master_new, one_new, two_new)


class Copies:
    def __init__(self, sends, recvs):
        self.sends, self.recvs, self.count = sends, recvs, 0

    def to(self, src, dst, device):
        copy = remote(src, dst, self.sends, self.recvs, self.count, device)
        self.count += 1
        return copy


class Ring:
    def __init__(self, length, place, device_at):
        self.length, self.place, self.device_at = length, place, device_at
        self.ways = ((0, 1), (1, -1)) if length > 2 else ((0, 1),)

    def at(self, step):
        return lax.rem(self.place + step + self.length, self.length)

    def device(self, step):
        return self.device_at(self.at(step))


class RingGather:
    def __init__(self, copies, ring, views, sources=None, arrived=None):
        self.copies, self.ring, self.views = copies, ring, views
        self.sources, self.arrived = sources, arrived
        self.near, self.far = [[], []], [[], []]

    def start(self):
        for way, step in self.ring.ways:
            for k, view in enumerate(self.views):
                own = view(self.ring.place, None)
                src = self.sources[k] if self.sources else own
                copy = self.copies.to(src, own, self.ring.device(step))
                copy.start()
                self.near[way].append(copy)

    def middle(self):
        for way, step in self.ring.ways:
            for copy in self.near[way]:
                copy.wait_recv()
            came_from = self.ring.at(-step)
            if self.ring.length > 2:
                for view in self.views:
                    ref = view(came_from, way)
                    if ref is not None:
                        copy = self.copies.to(ref, ref, self.ring.device(step))
                        copy.start()
                        self.far[way].append(copy)
            if self.arrived:
                self.arrived(came_from)

    def end(self):
        for copy in self.far[0] + self.far[1]:
            copy.wait_recv()
        if self.arrived and self.ring.length > 2:
            self.arrived(self.ring.at(2))

    def finish(self):
        for copy in self.near[0] + self.near[1] + self.far[0] + self.far[1]:
            copy.wait_send()


class Summand:
    def __init__(self, ref, index, count, width, near, far):
        self.ref, self.index, self.count, self.width = ref, index, count, width
        self.near, self.far = near, far

    def view(self, target, start, width):
        return self.ref.at[self.index(slice(None), target, start, width)]

    def add(self, target, start, width, other):
        def one(lead):
            at = self.index(lead, target, start, width)
            more = other[...] if self.count is None else other[lead]
            self.ref[at] = (self.ref[at].astype(F32) + more.astype(F32)).astype(BF)

        if self.count is None:
            one(None)
        else:
            over((self.count,), one)

    def total(self, lead, target, ways):
        value = self.ref[self.index(lead, target, 0, self.width)].astype(F32)
        for way in range(ways):
            more = self.far[way][...] if self.count is None else self.far[way][lead]
            value = value + more.astype(F32)
        return value


class RingSum:
    def __init__(self, copies, ring, summands):
        self.copies, self.ring, self.summands = copies, ring, summands
        self.near, self.far = [[], []], [[], []]

    def start(self):
        if self.ring.length == 2:
            return
        for way, step in self.ring.ways:
            for s in self.summands:
                half = s.width // 2
                copy = self.copies.to(
                    s.view(self.ring.at(2), way * half, half), s.near[way], self.ring.device(step)
                )
                copy.start()
                self.near[way].append(copy)

    def middle(self):
        for way, step in self.ring.ways:
            target = self.ring.at(step)
            for k, s in enumerate(self.summands):
                if self.ring.length > 2:
                    self.near[way][k].wait_recv()
                    s.add(target, way * (s.width // 2), s.width // 2, s.near[way])
                copy = self.copies.to(
                    s.view(target, 0, s.width), s.far[way], self.ring.device(step)
                )
                copy.start()
                self.far[way].append(copy)

    def end(self):
        for copy in self.far[0] + self.far[1]:
            copy.wait_recv()

    def total(self, k, lead=None):
        return self.summands[k].total(lead, self.ring.place, len(self.ring.ways))

    def finish(self):
        for copy in self.near[0] + self.near[1] + self.far[0] + self.far[1]:
            copy.wait_send()


def lanes_at(start, width):
    if not isinstance(start, int):
        start = pl.multiple_of(start, 128)
    return pl.ds(start, width)


class Slice:
    def __init__(self, grid):
        self.grid = grid
        nz, nx, nc = grid
        d = lax.axis_index("dp")
        self.d, self.z, self.x, self.core = d, d // (nx * nc), lax.rem(d // nc, nx), lax.rem(d, nc)
        self.row, self.col = lax.axis_index("row"), lax.axis_index("col")
        self.half = nz * nx * nc // 2
        self.place = group_place()
        self.zls = nz // 2
        self.partner = self.dp(self.z, self.x, 1 - self.core)
        self.z_ring = Ring(nz, self.z, lambda z: self.dp(z, self.x, self.core))
        self.x_ring = Ring(nx, self.x, lambda x: self.dp(self.z, x, self.core))
        self.y_ring = Ring(4, self.place, lambda q: {"row": q // 2, "col": lax.rem(q, 2)})

    def dp(self, z, x, core):
        _, nx, nc = self.grid
        return {"dp": (z * nx + x) * nc + core}

    def greet_rings(self, rings, whole=False):
        count = 0
        for ring in rings:
            steps = range(1, ring.length) if whole else [step for _, step in ring.ways]
            for step in steps:
                greet(ring.device(step))
                count += 1
        return count


class WeightGather:
    def __init__(self, here, cut, copies, local, own, full, spread):
        self.here, self.copies, self.core_copies = here, copies, []
        rows, lanes = own.shape
        pair = full.shape[-1] != lanes
        first = cut if pair else rows // 2
        cuts = (pl.ds(0, first), pl.ds(first, rows - first))
        z, x, core, zls = here.z, here.x, here.core, here.zls

        def part(width, half):
            return (0, width) if half is None else (half * (width // 2), width // 2)

        def chunk(order, along, half):
            zz, xx = (along, x) if order == 0 else (z, along)
            start, width = part(lanes, half)
            if pair:
                at = lanes_at((zz // zls) * lanes + start, width)
                return full.at[lax.rem(zz, zls), xx, core, cuts[order], at]
            return full.at[zz, xx, core, cuts[order], pl.ds(start, width)]

        def line(order, along, half):
            if order == 0:
                at = pl.ds(*part(full.shape[-1], half))
                return full.at[:, along, core, cuts[0], at]
            start, width = part(lanes, half)
            if pair:
                at = lanes_at((along // zls) * lanes + start, width)
                return full.at[lax.rem(along, zls), :, core, cuts[1], at]
            return full.at[along, :, core, cuts[1], pl.ds(start, width)]

        def small(order, along, half):
            return None if half == 1 else spread[1].at[along, x, core]

        def small_line(order, along, half):
            return None if half == 1 else spread[1].at[:, along, core]

        rings = ((here.z_ring, here.x_ring), (here.x_ring, here.z_ring))
        self.first, self.second, self.lines, self.own = [], [], [], []
        for order in range(2):
            sources = [own.at[cuts[order]]]
            chunks, lines = [partial(chunk, order)], [partial(line, order)]
            if order == 0 and spread:
                sources.append(spread[0])
                chunks.append(partial(small, order))
                lines.append(partial(small_line, order))
            for k, view in enumerate(chunks):
                self.own.append(
                    pltpu.make_async_copy(
                        sources[k], view(rings[order][0].place, None), local.at[order * 2 + k]
                    )
                )
            self.first.append(RingGather(copies, rings[order][0], chunks, sources))
            self.second.append(
                RingGather(copies, rings[order][1], lines, None, partial(self.forward, order))
            )
            self.lines.append(lines)

    def forward(self, order, along):
        for view in self.lines[order]:
            ref = view(along, None)
            copy = self.copies.to(ref, ref, self.here.partner)
            copy.start()
            self.core_copies.append(copy)

    def start(self):
        for ring in self.first:
            ring.start()
        for copy in self.own:
            copy.start()

    def first_middle(self):
        for ring in self.first:
            ring.middle()

    def turn(self):
        for copy in self.own:
            copy.wait()
        for order in range(2):
            self.first[order].end()
            self.second[order].start()
            self.forward(order, self.second[order].ring.place)

    def second_middle(self):
        for ring in self.second:
            ring.middle()

    def end(self):
        for ring in self.second:
            ring.end()

    def arrive(self):
        for copy in self.core_copies:
            copy.wait_recv()

    def finish(self):
        for ring in self.first + self.second:
            ring.finish()
        for copy in self.core_copies:
            copy.wait_send()


def dot(left, right):
    return jnp.dot(left, right, preferred_element_type=F32)


def dot_rows(left, right):
    return lax.dot_general(left, right, CONTRACT_ROWS, preferred_element_type=F32)


def dot_cols(left, right):
    return lax.dot_general(left, right, CONTRACT_COLS, preferred_element_type=F32)


def norm_stats(state):
    width = state.shape[1]
    average = jnp.sum(state, 1, keepdims=True) / width
    spread = jnp.sum(state * state, 1, keepdims=True) / width - average * average
    inv_std = lax.rsqrt(spread + EPS_NORM)
    return ((state - average) * inv_std, inv_std)


def norm_back(grad_hat, hat):
    width = hat.shape[1]
    first = jnp.sum(grad_hat, 1, keepdims=True) / width
    second = jnp.sum(grad_hat * hat, 1, keepdims=True) / width
    return grad_hat - first - hat * second


class Layer:
    def __init__(self, layer, vec, tables, mask, bias, full_q, full_u, full_b, sizes):
        self.vec, self.tables, self.mask, self.bias = vec, tables, mask, bias
        self.layer, self.full_q, self.full_u, self.full_b = layer, full_q, full_u, full_b
        self.qkv_width, self.up_width, self.out_rows = sizes
        self.heads_here = self.qkv_width // (3 * HEAD)

    def vector(self, k):
        at = self.layer * VEC_ROWS + k
        return self.vec[at : at + 1, :]

    def q_matrix(self, start, width):
        return self.full_q[:, :, :, :, start : start + width].reshape(-1, width)

    def u_matrix(self, start, width):
        return self.full_u[:, :, :, :, start : start + width].reshape(-1, width)

    def b_matrix(self, low, high, start, width):
        value = self.full_b[:, :, :, low:high, start : start + width]
        return value.reshape(-1, width)

    def out_matrix(self, start, width):
        return self.b_matrix(0, self.out_rows, start, width)

    def down_matrix(self, start, width):
        return self.b_matrix(self.out_rows, self.full_b.shape[3], start, width)

    def inputs(self, hat, attn_in, mlp_in):
        attn_in[...] = (hat * self.vector(0) + self.vector(1)).astype(BF)
        mlp_in[...] = (hat * self.vector(2) + self.vector(3)).astype(BF)

    def project(self, attn_in, joined):
        pair = 6 * HEAD
        cosine, left, right = self.tables
        for start in range(0, self.qkv_width, pair):
            value = dot(attn_in[...], self.q_matrix(start, pair))
            value = value + self.bias[0:1, start : start + pair]
            value = (
                value * cosine[...]
                + pltpu.roll(value, pair - ROT // 2, 1) * left[...]
                + pltpu.roll(value, ROT // 2, 1) * right[...]
            )
            joined[:, start : start + pair] = value.astype(BF)

    def head(self, joined, h):
        start = h * 3 * HEAD
        return [joined[:, start + k * HEAD : start + (k + 1) * HEAD] for k in range(3)]

    def attend(self, joined, probs, heads):
        for h in range(self.heads_here):
            query, key_rows, value_rows = self.head(joined, h)
            scores = dot_cols(query, key_rows) * HEAD**-0.5 + self.mask[...]
            expo = jnp.exp(scores - jnp.max(scores, 1, keepdims=True))
            low = (expo / jnp.sum(expo, 1, keepdims=True)).astype(BF)
            probs[h] = low
            heads[:, h * HEAD : (h + 1) * HEAD] = dot(low, value_rows).astype(BF)

    def units(self, mlp_in, slope, units):
        width = 256
        for start in range(0, self.up_width, width):
            at = slice(start, start + width)
            value = dot(mlp_in[...], self.u_matrix(start, width))
            value = value + self.bias[1:2, at]
            below = 0.5 * (1.0 + lax.erf(value * 0.5**0.5))
            density = jnp.exp(value * value * -0.5) * ((2.0 * math.pi) ** -0.5)
            units[:, at] = (value * below).astype(BF)
            slope[:, at] = (below + value * density).astype(BF)

    def outputs(self, heads, units, start, width):
        return dot(heads[...], self.out_matrix(start, width)) + dot(
            units[...], self.down_matrix(start, width)
        )

    def branch_back(self, grad, slope, grad_heads, grad_pre):
        grad_heads[...] = dot_cols(grad[...], self.out_matrix(0, D)).astype(BF)
        zls = self.full_b.shape[0]
        width = self.up_width // zls
        step = min(width, 256)
        for zl in range(zls):
            matrix = self.full_b[zl, :, :, self.out_rows :, :].reshape(-1, D)
            for start in range(0, width, step):
                at = slice(zl * width + start, zl * width + start + step)
                pull = dot_cols(grad[...], matrix[start : start + step])
                grad_pre[:, at] = (pull * slope[:, at].astype(F32)).astype(BF)

    def attend_back(self, joined, probs, grad_heads, raw, grad_joined):
        for h in range(self.heads_here):
            query, key_rows, value_rows = self.head(joined, h)
            grad = grad_heads[:, h * HEAD : (h + 1) * HEAD]
            low = probs[h]
            high = low.astype(F32)
            grad_probs = dot_cols(grad, value_rows)
            inner = jnp.sum(grad_probs * high, 1, keepdims=True)
            grad_raw = (high * (grad_probs - inner) * HEAD**-0.5).astype(BF)
            start = h * 3 * HEAD
            raw[:, start : start + HEAD] = dot(grad_raw, key_rows)
            raw[:, start + HEAD : start + 2 * HEAD] = dot_rows(grad_raw, query)
            raw[:, start + 2 * HEAD : start + 3 * HEAD] = dot_rows(low, grad)
        pair = 6 * HEAD
        cosine, left, right = self.tables
        for start in range(0, self.qkv_width, pair):
            value = raw[:, start : start + pair]
            value = (
                value * cosine[...]
                + pltpu.roll(value * left[...], ROT // 2, 1)
                + pltpu.roll(value * right[...], pair - ROT // 2, 1)
            )
            grad_joined[:, start : start + pair] = value.astype(BF)

    def inputs_back(self, grad_joined, grad_pre, hat, grad, sums):
        grad_attn_in = dot_cols(grad_joined[...], self.q_matrix(0, self.qkv_width))
        rows = [
            jnp.sum(grad_attn_in * hat, 0, keepdims=True),
            jnp.sum(grad_attn_in, 0, keepdims=True),
        ]
        grad_hat = grad_attn_in * self.vector(0)
        grad_mlp_in = dot_cols(grad_pre[...], self.u_matrix(0, self.up_width))
        rows += [
            jnp.sum(grad_mlp_in * hat, 0, keepdims=True),
            jnp.sum(grad_mlp_in, 0, keepdims=True),
            jnp.sum(grad[...].astype(F32), 0, keepdims=True) * 0.25,
        ]
        for k, row in enumerate(rows):
            sums[k : k + 1, :] = row
        for k, (ref, width) in enumerate(
            ((grad_joined, self.qkv_width), (grad_pre, self.up_width))
        ):
            sums[5 + k : 6 + k, :] = jnp.zeros((1, D), F32)
            sums[5 + k : 6 + k, :width] = jnp.sum(ref[...].astype(F32), 0, keepdims=True)
        sums[7:8, :] = jnp.zeros((1, D), F32)
        return norm_back(grad_hat + grad_mlp_in * self.vector(2), hat)


def grads_a(left, right, out):
    width = right.shape[1]
    nz = out.shape[0]
    block = left.shape[1] // nz
    for k in range(nz):
        value = dot_rows(left[:, k * block : (k + 1) * block], right[...]).astype(BF)
        out[k] = value.reshape(*out.shape[1:4], width)


def grads_b(left, right, out, low, high):
    zls = out.shape[0]
    block = left.shape[1] // zls
    for k in range(zls):
        value = dot_rows(left[:, k * block : (k + 1) * block], right[...]).astype(BF)
        out[k, :, :, low:high, :] = value.reshape(*out.shape[1:3], high - low, D)


def rows_index(rows):
    def index(lead, target, start, width):
        return (
            pl.ds(pl.multiple_of(target * rows, rows), rows),
            lanes_at(start, width),
        )

    return index


def blocks_index(rows, lanes):
    def index(lead, target, start, width):
        return (
            pl.ds(pl.multiple_of(lax.rem(target, 2) * rows, rows), rows),
            lanes_at((target // 2) * lanes + start, width),
        )

    return index


def group_sum(here, copies, part, index, width, near, far):
    summand = Summand(part, index, None, width, (near.at[0], near.at[1]), (far.at[0], far.at[1]))
    return RingSum(copies, here.y_ring, [summand])


def group_gather(here, copies, whole, rows):
    def view(target, half):
        width = whole.shape[1]
        start, width = (0, width) if half is None else (half * (width // 2), width // 2)
        return whole.at[pl.ds(pl.multiple_of(target * rows, rows), rows), pl.ds(start, width)]

    return RingGather(copies, here.y_ring, [view])


def own_rows(here, rows):
    return pl.ds(pl.multiple_of(here.place * rows, rows), rows)


def ring_scratch(rows, width):
    return [pltpu.VMEM((2, rows, width // 2), BF), pltpu.VMEM((2, rows, width), BF)]


class GradSum:
    def __init__(self, here, cut, copies, kind, g, s, buffers):
        self.here, self.copies, self.kind, self.g, self.s = here, copies, kind, g, s
        self.near, self.far, self.mid, self.near_two, self.far_two, self.fin = buffers
        rows = g.shape[3]
        first = rows // 2 if kind == "a" else cut
        self.cuts = (pl.ds(0, first), pl.ds(first, rows - first))
        self.full = g.shape[4]
        self.lanes = self.full // 2
        self.lines, self.turns = [None, None], [None, None]

    def start(self):
        self.core = []
        for order in range(2):
            copy = self.copies.to(
                self.g.at[:, :, 1 - self.here.core, self.cuts[order]],
                self.s.at[:, :, self.cuts[order]],
                self.here.partner,
            )
            copy.start()
            self.core.append(copy)

    def line(self, order):
        here, at, zls = self.here, self.cuts[order], self.here.zls
        self.core[order].wait_recv()

        def add(zz, xx):
            self.s[zz, xx, at] = (
                self.s[zz, xx, at].astype(F32) + self.g[zz, xx, here.core, at].astype(F32)
            ).astype(BF)

        over(self.s.shape[:2], add)
        nx = self.s.shape[1]
        if order == 0:
            ring, count, width = here.x_ring, self.s.shape[0], self.full

            def index(lead, target, start, width):
                return (lead, target, at, lanes_at(start, width))

        elif self.kind == "a":
            ring, count, width = here.z_ring, nx, self.full

            def index(lead, target, start, width):
                return (target, lead, at, lanes_at(start, width))

        else:
            ring, count, width = here.z_ring, nx, self.lanes

            def index(lead, target, start, width):
                return (
                    lax.rem(target, zls),
                    lead,
                    at,
                    lanes_at((target // zls) * self.lanes + start, width),
                )

        summand = Summand(
            self.s,
            index,
            count,
            width,
            (self.near[order].at[0], self.near[order].at[1]),
            (self.far[order].at[0], self.far[order].at[1]),
        )
        self.lines[order] = RingSum(self.copies, ring, [summand])
        self.lines[order].start()

    def line_middle(self, order):
        self.lines[order].middle()

    def turn(self, order):
        here, zls, mid = self.here, self.here.zls, self.mid[order]
        line = self.lines[order]
        line.end()

        def put(lead):
            mid[lead] = line.total(0, lead).astype(BF)

        over(mid.shape[:1], put)
        ring = here.z_ring if order == 0 else here.x_ring
        if self.kind == "b" and order == 0:

            def index(lead, target, start, width):
                return (
                    lax.rem(target, zls),
                    slice(None),
                    lanes_at((target // zls) * self.lanes + start, width),
                )

        else:

            def index(lead, target, start, width):
                return (target, slice(None), lanes_at(start, width))

        summand = Summand(
            mid,
            index,
            None,
            self.full if self.kind == "a" else self.lanes,
            (self.near_two[order].at[0], self.near_two[order].at[1]),
            (self.far_two[order].at[0], self.far_two[order].at[1]),
        )
        self.turns[order] = RingSum(self.copies, ring, [summand])
        self.turns[order].start()

    def turn_middle(self, order):
        self.turns[order].middle()

    def end(self, order):
        self.turns[order].end()
        value = self.turns[order].total(0).astype(BF)
        if self.kind == "a":
            self.fin[order] = value
        else:
            self.fin[self.cuts[order]] = value

    def finish(self):
        for copy in self.core:
            copy.wait_send()
        for order in range(2):
            self.lines[order].finish()
            self.turns[order].finish()


def grad_buffers(grid, cut, g_shape, kind):
    nz, nx, _ = grid
    rows, full = g_shape[3:]
    zls = g_shape[0]
    first = rows // 2 if kind == "a" else cut
    lanes = full if kind == "a" else full // 2
    cuts = (first, rows - first)

    def low(*dims):
        return pltpu.VMEM(dims, BF)

    counts = (zls, nx)
    widths = (full, lanes)
    fin = low(2, first, full) if kind == "a" else low(rows, lanes)
    return [
        low(zls, nx, rows, full),
        *[low(2, counts[o], cuts[o], widths[o] // 2) for o in range(2)],
        *[low(2, counts[o], cuts[o], widths[o]) for o in range(2)],
        *[low(counts[o], cuts[o], widths[o]) for o in range(2)],
        *[low(2, cuts[o], lanes // 2) for o in range(2)],
        *[low(2, cuts[o], lanes) for o in range(2)],
        fin,
    ]


def grad_sum(here, cut, copies, kind, g, refs):
    s, near0, near1, far0, far1, mid0, mid1, low0, low1, top0, top1, fin = refs
    return GradSum(
        here,
        cut,
        copies,
        kind,
        g,
        s,
        ((near0, near1), (far0, far1), (mid0, mid1), (low0, low1), (top0, top1), fin),
    )


def lane_iota(rows, lanes):
    return lax.broadcasted_iota(jnp.int32, (rows, lanes), 1)


def make_tables(ids, live, cosine, left, right, mask):
    length = ids.shape[1]
    other = ids[...]
    row = lax.broadcasted_iota(jnp.int32, (length, length), 0)
    column = lax.broadcasted_iota(jnp.int32, (length, length), 1)
    other = jnp.broadcast_to(other.astype(F32), (length, length))
    own = jnp.sum(jnp.where(row == column, other, 0.0), 1, keepdims=True)
    live[...] = jnp.broadcast_to(jnp.where(own < SEQS, 1.0, 0.0), live.shape)
    earlier = jnp.sum((other < own).astype(F32), 1, keepdims=True)
    mask[...] = jnp.where((other == own) & (column <= row), 0.0, MASK_VALUE)
    place = lax.broadcasted_iota(jnp.int32, (length, 1), 0).astype(F32) - earlier
    lane = lane_iota(1, 128)
    at = lax.rem(lane, HEAD)
    turned = at < ROT
    power = lax.rem(at, ROT // 2).astype(F32)
    frequency = jnp.exp(power * (-2.0 / ROT * math.log(ROPE_BASE)))
    angles = place * frequency
    cos_part = jnp.where(turned, jnp.cos(angles), 1.0)
    sin_part = jnp.sin(angles)
    left_part = jnp.where(at < ROT // 2, -sin_part, 0.0)
    right_part = jnp.where(turned & (at >= ROT // 2), sin_part, 0.0)
    low_half = lane < HEAD
    for ref, value, rest in ((cosine, cos_part, 1.0), (left, left_part, 0.0), (right, right_part, 0.0)):
        ref[:, 0:128] = value
        ref[:, 128:256] = jnp.where(low_half, rest, value)
        ref[:, 256:384] = jnp.where(low_half, value, rest)


def make_biases(full_c, bias, widths):
    n_dp = math.prod(full_c.shape[:3])
    table = full_c[...].reshape(n_dp, *full_c.shape[3:])
    lanes = full_c.shape[4]
    for layer in range(LAYERS):
        values = table[:, layer, :].astype(BF)
        first = 0
        for k, width in enumerate(widths):
            total = n_dp * width
            lane = lax.broadcasted_iota(jnp.int32, (lanes, total), 0)
            column = lax.broadcasted_iota(jnp.int32, (lanes, total), 1)
            pick = jnp.where(lane == lax.rem(column, width) + first, 1.0, 0.0).astype(BF)
            spread = dot(values, pick)
            device = lax.broadcasted_iota(jnp.int32, (n_dp, total), 0)
            column = lax.broadcasted_iota(jnp.int32, (n_dp, total), 1)
            mine = jnp.where(column // width == device, spread, 0.0)
            bias[layer * 2 + k : layer * 2 + k + 1, :total] = jnp.sum(mine, 0, keepdims=True)
            first += width


def whole_kernel(grid, cut, sizes, widths, tree, *refs):
    at = SimpleNamespace(**jax.tree.unflatten(tree, refs))
    sends, recvs, local = at.sends, at.recvs, at.local
    here = Slice(grid)
    nz, nx, _ = grid
    copies = Copies(sends, recvs)
    copies.count = 48
    d, r, c, half = here.d, here.row, here.col, here.half
    hid, cot = at.hid, at.cot
    hid_all, cot_all, vec = at.hid_all, at.cot_all, at.vec
    rows, lanes = hid.shape
    quarter = rows // 2
    dh, dl = d // half, lax.rem(d, half)
    swap_needed = dh != r
    swap_to = {"dp": r * half + dl, "row": dh}
    slot_rows = at.qkv_weight.shape[1]
    forth = [{"dp": r * half + d // 2, "row": k} for k in range(2)]
    back_to = [{"dp": 2 * dl + k, "row": dh} for k in range(2)]
    forth_self = [(r == k) & (r * half + d // 2 == d) for k in range(2)]
    back_self = [(dh == r) & (2 * dl + k == d) for k in range(2)]
    slot = lax.rem(d, 2)

    count = here.greet_rings([here.z_ring, here.x_ring, here.y_ring], whole=True)
    greet(here.partner)
    for k in range(2):
        for device, itself in ((forth[k], forth_self[k]), (back_to[k], back_self[k])):

            @pl.when(jnp.logical_not(itself))
            def _():
                greet(device)

    @pl.when(swap_needed)
    def _():
        greet(swap_to)

    qkv_width, up_width, out_rows = sizes
    wa, wb = (at.wq, at.wu), at.wb

    def cast(layer):
        for ref, given, width in ((wa[0], at.qkv_weight, qkv_width), (wa[1], at.up_weight, up_width)):
            for k in range(2):
                ref[layer, k] = given[layer, :, k * width : (k + 1) * width].astype(BF)
        wb[layer, :out_rows] = at.out_weight[layer].astype(BF)
        wb[layer, out_rows:] = at.down_weight[layer].astype(BF)

    cast(0)
    vec_own, wc = at.vec_own, at.wc
    vec_own[...] = jnp.zeros(vec_own.shape, F32)
    for layer in range(LAYERS):
        vec_own[layer * VEC_ROWS : layer * VEC_ROWS + 6] = at.row_vectors[layer]
    wc[...] = jnp.zeros(wc.shape, F32)
    wc[:LAYERS, : widths[0]] = at.qkv_bias[...]
    wc[:LAYERS, widths[0] : sum(widths)] = at.up_bias[...]
    greeted(
        count
        + 5
        + swap_needed.astype(jnp.int32)
        - sum(k.astype(jnp.int32) for k in forth_self + back_self)
    )

    def when_else(condition, there, here_do):
        pl.when(condition)(there)
        pl.when(jnp.logical_not(condition))(here_do)

    def pair(src, dst, send, recv, device):
        return pltpu.make_async_remote_copy(
            src_ref=src,
            dst_ref=dst,
            send_sem=sends.at[send],
            recv_sem=recvs.at[recv],
            device_id=device,
            device_id_type=MESH,
        )

    a_own, b_own = (at.q_own, at.u_own), at.b_own
    slot_at = pl.ds(pl.multiple_of(slot * slot_rows, slot_rows), slot_rows)

    def a_copy(layer, kind, k):
        base = layer * 8 + kind * 2
        return pair(
            wa[kind].at[layer, k], a_own[kind].at[layer, slot_at], base + k, base + slot, forth[k]
        )

    def a_arrival(layer, kind, k):
        base = layer * 8 + kind * 2
        into = a_own[kind].at[layer, pl.ds(k * slot_rows, slot_rows)]
        return pair(wa[kind].at[layer, 0], into, base, base + k, back_to[k])

    def a_local(layer, kind, k):
        return pltpu.make_async_copy(
            wa[kind].at[layer, k], a_own[kind].at[layer, slot_at], local.at[24 + layer * 2 + kind]
        )

    def swap_copy(layer):
        return pair(wb.at[layer], b_own.at[layer], layer * 8 + 4, layer * 8 + 4, swap_to)

    def swap_local(layer):
        return pltpu.make_async_copy(wb.at[layer], b_own.at[layer], local.at[28 + layer])

    def begin(layer):
        for kind in range(2):
            for k in range(2):
                when_else(
                    forth_self[k],
                    lambda: a_local(layer, kind, k).start(),
                    lambda: a_copy(layer, kind, k).start(),
                )
        when_else(
            swap_needed, lambda: swap_copy(layer).start(), lambda: swap_local(layer).start()
        )

    def complete_a(layer, kind):
        for k in range(2):
            when_else(
                forth_self[k],
                lambda: a_local(layer, kind, k).wait(),
                lambda: a_copy(layer, kind, k).wait_send(),
            )

            @pl.when(jnp.logical_not(back_self[k]))
            def _():
                a_arrival(layer, kind, k).wait_recv()

    def complete_b(layer):
        when_else(swap_needed, lambda: swap_copy(layer).wait(), lambda: swap_local(layer).wait())

    begin(0)
    tokens = pl.ds(pl.multiple_of(c * rows, rows), rows)
    features = pl.ds(pl.multiple_of(r * lanes, lanes), lanes)
    hid_copies = [
        copies.to(hid, hid_all.at[tokens, features], here.y_ring.device(k)) for k in range(1, 4)
    ]
    cot_copies = [
        copies.to(cot, cot_all.at[tokens, features], here.y_ring.device(k)) for k in range(1, 4)
    ]
    hid_copies.append(copies.to(vec_own, vec.at[:, features], {"row": 1 - r}))
    own = [
        pltpu.make_async_copy(hid, hid_all.at[tokens, features], local.at[36]),
        pltpu.make_async_copy(cot, cot_all.at[tokens, features], local.at[37]),
        pltpu.make_async_copy(vec_own, vec.at[:, features], local.at[38]),
    ]
    for copy in hid_copies + own:
        copy.start()
    tables, mask, bias = (at.cosine, at.left, at.right), at.mask, at.bias
    complete_a(0, 0)

    full = ((at.q_zero, at.u_zero, at.b_zero), (at.q_one, at.u_one, at.b_one))
    full_c = at.full_c
    gathers = []
    for k in range(LAYERS):
        for kind in range(3):
            source = (a_own + (b_own,))[kind].at[k]
            spread = (wc, full_c) if k == 0 and kind == 0 else None
            count = 4 * (3 * k + kind)
            gathers.append(
                WeightGather(
                    here, cut, copies, local.at[pl.ds(count, 4)], source, full[k][kind], spread
                )
            )
    near, late = gathers[:3], gathers[3:]
    near[0].start()
    complete_a(0, 1)
    near[1].start()
    complete_b(0)
    near[2].start()
    cast(1)
    begin(1)
    near[0].first_middle()
    for copy in hid_copies + own:
        copy.wait()
    layers = [
        Layer(k, vec, tables, mask, bias.at[pl.ds(2 * k, 2)], *full[k], sizes)
        for k in range(LAYERS)
    ]
    attn_in, mlp_in, joined, probs = at.attn_in, at.mlp_in, at.joined, at.probs
    heads, slope, units = at.heads, at.slope, at.units
    near[0].turn()
    near[1].first_middle()
    near[2].first_middle()
    make_tables(at.ids, at.live, *tables, mask)
    near[1].turn()
    near[0].second_middle()
    near[2].turn()
    near[0].end()
    near[1].second_middle()
    hat, _ = norm_stats(hid_all[...].astype(F32))
    layers[0].inputs(hat, attn_in[0], mlp_in[0])
    near[0].arrive()
    near[1].end()
    near[2].second_middle()
    make_biases(full_c, bias, widths)
    complete_a(1, 0)
    late[0].start()
    complete_a(1, 1)
    late[1].start()
    complete_b(1)
    late[2].start()
    for copy in cot_copies:
        copy.start()
    mine = own_rows(here, quarter)
    layers[0].project(attn_in[0], joined[0])
    near[2].end()
    for one in late:
        one.first_middle()
    layers[0].attend(joined[0], probs[0], heads[0])
    for one in late:
        one.turn()
    near[1].arrive()
    layers[0].units(mlp_in[0], slope[0], units[0])
    for one in late[:2]:
        one.second_middle()
    near[2].arrive()
    part = at.part[0]
    for start in (0, D // 2):
        part[:, start : start + D // 2] = (
            layers[0].outputs(heads[0], units[0], start, D // 2).astype(BF)
        )
    summed = group_sum(here, copies, part, rows_index(quarter), D, at.near[0], at.far[0])
    summed.start()
    late[2].second_middle()
    summed.middle()
    state = hid_all[mine, :].astype(F32) + layers[0].vector(4) + layers[0].vector(5)
    summed.end()
    state = state + summed.total(0)
    at.state[...] = state
    hat, inverse = norm_stats(state)
    inv_std, hat_all = at.inv_std, at.hat_all
    inv_std[...] = jnp.broadcast_to(inverse, inv_std.shape)
    hat_all[mine, :] = hat.astype(BF)
    spread = group_gather(here, copies, hat_all, quarter)
    spread.start()
    grad = (at.grad[0], at.grad[1])
    for copy in cot_copies:
        copy.wait()
    grad[1][...] = (
        cot_all[...].astype(F32) * at.live[:, :1]
    ).astype(BF)
    spread.middle()
    for one in late:
        one.end()
    spread.end()
    for one in late:
        one.arrive()
    for one in gathers:
        one.finish()
    rings = [summed, spread]

    layer = layers[1]
    layer.inputs(hat_all[...].astype(F32), attn_in[1], mlp_in[1])
    layer.project(attn_in[1], joined[1])
    layer.attend(joined[1], probs[1], heads[1])
    layer.units(mlp_in[1], slope[1], units[1])
    part = at.part[1]
    for start in (0, D // 2):
        part[:, start : start + D // 2] = (
            layer.outputs(heads[1], units[1], start, D // 2).astype(BF)
        )
    part[mine, :] = (part[mine, :].astype(F32) + at.state[...]).astype(BF)
    out_sum = group_sum(
        here, copies, part, blocks_index(rows, lanes), lanes, at.near[1], at.far[1]
    )
    out_sum.start()
    grad_heads, grad_pre, raw, grad_joined = (
        at.grad_heads,
        at.grad_pre,
        at.raw,
        at.grad_joined,
    )
    sums = (at.sums[0], at.sums[1])
    layer.branch_back(grad[1], slope[1], grad_heads, grad_pre)
    out_sum.middle()
    layer.attend_back(joined[1], probs[1], grad_heads, raw, grad_joined)
    back = at.back[1]
    back[...] = layer.inputs_back(
        grad_joined, grad_pre, hat_all[...].astype(F32), grad[1], sums[1]
    ).astype(BF)
    summed = group_sum(here, copies, back, rows_index(quarter), D, at.near[2], at.far[2])
    summed.start()

    grads = [
        full[1],
        (at.gq, at.gu, at.gb),
    ]
    sum_q, sum_u, sum_b = [
        [
            grad_sum(
                here,
                cut,
                copies,
                "aab"[kind],
                grads[k][kind],
                at.sum_buffers[k][kind],
            )
            for k in range(LAYERS)
        ]
        for kind in range(3)
    ]
    out_q, out_u, out_b = at.out_q, at.out_u, at.out_b

    def owner_copy(layer, kind, order):
        out, one = ((out_q, sum_q), (out_u, sum_u))[kind]
        base = 16 + layer * 8 + kind * 2
        return pair(
            one[layer].fin.at[order], out.at[layer, r], base + order, base + r, back_to[order]
        )

    def owner_arrival(layer, kind, k):
        out, one = ((out_q, sum_q), (out_u, sum_u))[kind]
        base = 16 + layer * 8 + kind * 2
        return pair(one[layer].fin.at[0], out.at[layer, k], base, base + k, forth[k])

    def owner_local(layer, kind, order):
        out, one = ((out_q, sum_q), (out_u, sum_u))[kind]
        return pltpu.make_async_copy(
            one[layer].fin.at[order], out.at[layer, r], local.at[30 + layer * 2 + kind]
        )

    def out_swap(layer):
        return pair(sum_b[layer].fin, out_b.at[layer], 20 + layer * 8, 20 + layer * 8, swap_to)

    def out_local(layer):
        return pltpu.make_async_copy(sum_b[layer].fin, out_b.at[layer], local.at[34 + layer])

    def hand_a(layer, kind):
        for order in range(2):
            when_else(
                back_self[order],
                lambda: owner_local(layer, kind, order).start(),
                lambda: owner_copy(layer, kind, order).start(),
            )

    def hand_b(layer):
        when_else(swap_needed, lambda: out_swap(layer).start(), lambda: out_local(layer).start())

    def handed(layer):
        for kind in range(2):
            for k in range(2):
                when_else(
                    back_self[k],
                    lambda: owner_local(layer, kind, k).wait(),
                    lambda: owner_copy(layer, kind, k).wait_send(),
                )

                @pl.when(jnp.logical_not(forth_self[k]))
                def _():
                    owner_arrival(layer, kind, k).wait_recv()

        when_else(swap_needed, lambda: out_swap(layer).wait(), lambda: out_local(layer).wait())

    def phase(step, which):
        for order in range(2):
            for one in which:
                step(one, order)

    grads_a(mlp_in[1], grad_pre, grads[1][1])
    sum_u[1].start()
    summed.middle()
    grads_a(attn_in[1], grad_joined, grads[1][0])
    sum_q[1].start()
    out_sum.end()
    bias_sum = vec[VEC_ROWS + 4 : VEC_ROWS + 5, features] + vec[VEC_ROWS + 5 : VEC_ROWS + 6, features]
    at.hidden[...] = (out_sum.total(0) + bias_sum).astype(BF)
    summed.end()
    grad_one = at.grad_one
    total = grad[1][mine, :].astype(F32) + inv_std[:, :1] * summed.total(0)
    grad_one[...] = total
    grad[0][mine, :] = total.astype(BF)
    spread = group_gather(here, copies, grad[0], quarter)
    spread.start()
    grads_b(heads[1], grad[1], grads[1][2], 0, out_rows)
    grads_b(units[1], grad[1], grads[1][2], out_rows, at.gb.shape[3])
    sum_b[1].start()
    spread.middle()
    phase(GradSum.line, [sum_u[1], sum_q[1]])
    spread.end()
    rings += [out_sum, summed, spread]

    layer = layers[0]
    grads_b(heads[0], grad[0], grads[0][2], 0, out_rows)
    grads_b(units[0], grad[0], grads[0][2], out_rows, at.gb.shape[3])
    sum_b[0].start()
    phase(GradSum.line, [sum_b[1]])
    phase(GradSum.line_middle, [sum_u[1], sum_q[1]])
    layer.branch_back(grad[0], slope[0], grad_heads, grad_pre)
    phase(GradSum.line_middle, [sum_b[1]])
    grads_a(mlp_in[0], grad_pre, grads[0][1])
    sum_u[0].start()
    phase(GradSum.turn, [sum_u[1], sum_q[1]])
    layer.attend_back(joined[0], probs[0], grad_heads, raw, grad_joined)
    phase(GradSum.turn, [sum_b[1]])
    phase(GradSum.line, [sum_b[0]])
    grads_a(attn_in[0], grad_joined, grads[0][0])
    sum_q[0].start()
    phase(GradSum.line, [sum_u[0]])
    phase(GradSum.turn_middle, [sum_u[1], sum_q[1], sum_b[1]])
    hat, inverse = norm_stats(hid_all[...].astype(F32))
    value = layer.inputs_back(grad_joined, grad_pre, hat, grad[0], sums[0])
    back = at.back[0]
    back[...] = (inverse * value).astype(BF)
    back[mine, :] = (back[mine, :].astype(F32) + grad_one[...]).astype(BF)
    summed = group_sum(
        here, copies, back, blocks_index(rows, lanes), lanes, at.near[3], at.far[3]
    )
    summed.start()
    phase(GradSum.line_middle, [sum_b[0]])
    phase(GradSum.line, [sum_q[0]])
    phase(GradSum.line_middle, [sum_u[0]])
    v_core, v_line, v_last, v_group = at.v_core, at.v_line, at.v_last, at.v_group
    v_lanes = D // 2
    v_mine = pl.ds(pl.multiple_of(here.core * v_lanes, v_lanes), v_lanes)
    v_other = pl.ds(pl.multiple_of((1 - here.core) * v_lanes, v_lanes), v_lanes)
    v_copies = [copies.to(sums[k].at[:, v_other], v_core.at[k], here.partner) for k in range(2)]
    for copy in v_copies:
        copy.start()
    summed.middle()
    for order in range(2):
        for one in (sum_q[1], sum_u[1], sum_b[1]):
            one.end(order)
    hand_a(1, 0)
    hand_a(1, 1)
    hand_b(1)
    for copy in v_copies:
        copy.wait()
    for k in range(LAYERS):
        v_line[here.x, k * VEC_ROWS : (k + 1) * VEC_ROWS] = v_core[k] + sums[k][:, v_mine]
    v_x = [
        copies.to(v_line.at[here.x], v_line.at[here.x], here.x_ring.device(k))
        for k in range(1, nx)
    ]
    for copy in v_x:
        copy.start()
    phase(GradSum.line_middle, [sum_q[0]])
    phase(GradSum.turn, [sum_b[0], sum_u[0]])
    summed.end()
    at.grad_out[...] = summed.total(0)
    rings.append(summed)
    for copy in v_x:
        copy.wait()
    total = v_line[0]
    for k in range(1, nx):
        total = total + v_line[k]
    v_last[here.z] = total
    v_z = [
        copies.to(v_last.at[here.z], v_last.at[here.z], here.z_ring.device(k))
        for k in range(1, nz)
    ]
    for copy in v_z:
        copy.start()
    phase(GradSum.turn_middle, [sum_b[0], sum_u[0]])
    phase(GradSum.turn, [sum_q[0]])
    for copy in v_z:
        copy.wait()
    total = v_last[0]
    for k in range(1, nz):
        total = total + v_last[k]
    v_group[here.place] = total
    v_y = [
        copies.to(v_group.at[here.place], v_group.at[here.place], here.y_ring.device(k))
        for k in range(1, 4)
    ]
    for copy in v_y:
        copy.start()
    phase(GradSum.turn_middle, [sum_q[0]])
    for order in range(2):
        sum_b[0].end(order)
        sum_u[0].end(order)
    hand_b(0)
    hand_a(0, 1)
    for copy in v_y:
        copy.wait()
    total = v_group[0]
    for k in range(1, 4):
        total = total + v_group[k]
    out_v = at.out_v
    out_v[0, :, v_mine] = total
    out_v[1, :, v_mine] = v_group[here.place]
    v_swap = copies.to(out_v.at[:, :, v_mine], out_v.at[:, :, v_mine], here.partner)
    v_swap.start()
    for order in range(2):
        sum_q[0].end(order)
    hand_a(0, 0)
    v_swap.wait()
    handed(1)
    handed(0)
    assert copies.count <= sends.shape[0], copies.count
    for ring in rings:
        ring.finish()
    for one in sum_q + sum_u + sum_b:
        one.finish()


def whole(grid, cut, sizes, widths, ins):
    nz, nx, nc = grid
    qkv_width, up_width, out_rows = sizes
    rows, lanes = ins["hid"].shape
    group, quarter = 2 * rows, rows // 2
    slot_rows, down_rows = ins["qkv_weight"].shape[1], ins["down_weight"].shape[1]
    b_rows = out_rows + down_rows
    heads_here = qkv_width // (3 * HEAD)

    def low(*dims):
        return pltpu.VMEM(dims, BF)

    def high(*dims):
        return pltpu.VMEM(dims, F32)

    def twice(make, *dims):
        return [make(*dims) for _ in range(LAYERS)]

    shape = jax.ShapeDtypeStruct
    outs = dict(
        hidden=shape((rows, lanes), BF),
        grad_out=shape((rows, lanes), F32),
        out_q=shape((LAYERS, 2, slot_rows, qkv_width), BF),
        out_u=shape((LAYERS, 2, slot_rows, up_width), BF),
        out_b=shape((LAYERS, b_rows, lanes), BF),
        out_v=shape((2, LAYERS * VEC_ROWS, D), F32),
    )
    q_shape = (nz, nx, nc, 2 * slot_rows, qkv_width)
    u_shape = (nz, nx, nc, 2 * slot_rows, up_width)
    b_shape = (nz // 2, nx, nc, b_rows, 2 * lanes)
    c_shape = (8, -(-sum(widths) // 128) * 128)
    kinds = ((q_shape, "a"), (u_shape, "a"), (b_shape, "b"))
    blocks = [ring_scratch(quarter, D), ring_scratch(rows, lanes)] * 2
    scratch = dict(
        hid_all=low(group, D),
        cot_all=low(group, D),
        vec=high(LAYERS * VEC_ROWS, D),
        vec_own=high(LAYERS * VEC_ROWS, lanes),
        wq=low(LAYERS, 2, slot_rows, qkv_width),
        wu=low(LAYERS, 2, slot_rows, up_width),
        wb=low(LAYERS, b_rows, lanes),
        wc=high(*c_shape),
        q_own=low(LAYERS, 2 * slot_rows, qkv_width),
        u_own=low(LAYERS, 2 * slot_rows, up_width),
        b_own=low(LAYERS, b_rows, lanes),
        q_zero=low(*q_shape),
        q_one=low(*q_shape),
        u_zero=low(*u_shape),
        u_one=low(*u_shape),
        b_zero=low(*b_shape),
        b_one=low(*b_shape),
        full_c=high(nz, nx, nc, *c_shape),
        cosine=high(group, 6 * HEAD),
        left=high(group, 6 * HEAD),
        right=high(group, 6 * HEAD),
        mask=high(group, group),
        live=high(group, 128),
        bias=high(2 * LAYERS, D),
        state=high(quarter, D),
        inv_std=high(quarter, 128),
        hat_all=low(group, D),
        grad_one=high(quarter, D),
        grad_heads=low(group, heads_here * HEAD),
        grad_pre=low(group, up_width),
        raw=high(group, qkv_width),
        grad_joined=low(group, qkv_width),
        gq=low(*q_shape),
        gu=low(*u_shape),
        gb=low(*b_shape),
        v_core=high(2, VEC_ROWS, D // 2),
        v_line=high(nx, LAYERS * VEC_ROWS, D // 2),
        v_last=high(nz, LAYERS * VEC_ROWS, D // 2),
        v_group=high(4, LAYERS * VEC_ROWS, D // 2),
        attn_in=twice(low, group, D),
        mlp_in=twice(low, group, D),
        joined=twice(low, group, qkv_width),
        probs=twice(low, heads_here, group, group),
        heads=twice(low, group, heads_here * HEAD),
        slope=twice(low, group, up_width),
        units=twice(low, group, up_width),
        part=twice(low, group, D),
        back=twice(low, group, D),
        grad=twice(low, group, D),
        sums=twice(high, VEC_ROWS, D),
        sum_buffers=[
            [grad_buffers(grid, cut, dims, kind) for dims, kind in kinds] for _ in range(LAYERS)
        ],
        near=[block[0] for block in blocks],
        far=[block[1] for block in blocks],
        sends=pltpu.SemaphoreType.DMA((480,)),
        recvs=pltpu.SemaphoreType.DMA((480,)),
        local=pltpu.SemaphoreType.DMA((40,)),
    )
    flat = jax.tree.leaves(scratch)
    tree = jax.tree.structure(dict(**ins, **outs, **scratch))
    order = [*ins.values(), *outs.values(), *scratch.values()]
    names = [*ins, *outs, *scratch]
    ranks = jax.tree.unflatten(
        jax.tree.structure(dict(zip(names, order))), range(tree.num_leaves)
    )
    given = jax.tree.leaves([ranks[name] for name in names])

    def kernel(*refs):
        placed = [None] * len(refs)
        for rank, ref in zip(given, refs):
            placed[rank] = ref
        whole_kernel(grid, cut, sizes, widths, tree, *placed)

    flat = jax.tree.leaves(list(scratch.values()))
    return pl.pallas_call(
        kernel,
        out_shape=tuple(outs.values()),
        in_specs=[VMEM_SPEC] * len(ins),
        out_specs=(VMEM_SPEC,) * len(outs),
        scratch_shapes=flat,
        compiler_params=params(0, 63),
        name="whole_step",
    )(*ins.values())


def update_kernel(n_dp, bias_widths, out_rows, *refs):
    own_q, own_u, own_b, all_v = refs[:4]
    old, new = refs[4:25], refs[25:]
    d, r = lax.axis_index("dp"), lax.axis_index("row")

    def update(k, gradient, rate, decay):
        values = adamw(*[ref[...] for ref in old[3 * k : 3 * k + 3]], gradient, rate, decay)
        for ref, value in zip(new[3 * k : 3 * k + 3], values):
            ref[...] = value

    for k, own in ((0, own_q), (2, own_u)):
        width = own.shape[3]
        for layer in range(LAYERS):
            for side in range(2):
                at = (layer, slice(None), slice(side * width, (side + 1) * width))
                gradient = own[layer, side].astype(F32)
                values = adamw(
                    *[ref[at] for ref in old[3 * k : 3 * k + 3]], gradient, RATE_MATRIX, DECAY_MATRIX
                )
                for ref, value in zip(new[3 * k : 3 * k + 3], values):
                    ref[at] = value
    update(1, own_b[:, :out_rows].astype(F32), RATE_MATRIX, DECAY_MATRIX)
    update(3, own_b[:, out_rows:].astype(F32), RATE_MATRIX, DECAY_MATRIX)
    for k, width in enumerate(bias_widths):
        for layer in range(LAYERS):
            rows = all_v[1, layer * VEC_ROWS : (layer + 1) * VEC_ROWS, :]
            moved = pltpu.roll(rows, lax.rem(D - d * width, D), 1)
            at = (slice(layer, layer + 1), slice(None))
            values = adamw(
                *[ref[at] for ref in old[12 + 3 * k : 15 + 3 * k]],
                moved[5 + k : 6 + k, :width],
                RATE_MATRIX,
                0.0,
            )
            for ref, value in zip(new[12 + 3 * k : 15 + 3 * k], values):
                ref[at] = value
    lanes = old[18].shape[2]
    features = pl.ds(pl.multiple_of(r * lanes, lanes), lanes)
    for layer in range(LAYERS):
        for k in range(6):
            row = layer * VEC_ROWS + min(k, 4)
            at = (layer, slice(k, k + 1), slice(None))
            values = adamw(
                *[ref[at] for ref in old[18:21]],
                all_v[0, row : row + 1, features],
                RATE_VECTOR,
                0.0,
            )
            for ref, value in zip(new[18:21], values):
                ref[at] = value


def update_all(n_dp, bias_widths, out_rows, gradients, old):
    return pl.pallas_call(
        partial(update_kernel, n_dp, bias_widths, out_rows),
        out_shape=tuple(jax.ShapeDtypeStruct(a.shape, F32) for a in old),
        in_specs=[VMEM_SPEC] * (4 + len(old)),
        out_specs=(VMEM_SPEC,) * len(old),
        compiler_params=pltpu.CompilerParams(vmem_limit_bytes=32 << 20),
        name="update_all",
    )(*gradients, *old)


def on_device(
    hidden_in,
    cotangent,
    seq_ids,
    qkv_weight,
    qkv_first,
    qkv_second,
    out_weight,
    out_first,
    out_second,
    up_weight,
    up_first,
    up_second,
    down_weight,
    down_first,
    down_second,
    qkv_bias,
    qkv_bias_first,
    qkv_bias_second,
    up_bias,
    up_bias_first,
    up_bias_second,
    row_vectors,
    row_first,
    row_second,
):
    n_dp = lax.axis_size("dp")
    grid = GRIDS[n_dp]
    group_len = seq_ids.shape[0]
    qkv_width, up_width = qkv_weight.shape[2] // 2, up_weight.shape[2] // 2
    out_rows, down_rows = out_weight.shape[1], down_weight.shape[1]
    bias_widths = qkv_bias.shape[1], up_bias.shape[1]
    cut = out_rows + down_rows // 2
    sizes = (qkv_width, up_width, out_rows)

    ins = dict(
        hid=hidden_in,
        cot=cotangent,
        ids=seq_ids.reshape(1, group_len),
        row_vectors=row_vectors,
        qkv_bias=qkv_bias,
        up_bias=up_bias,
        qkv_weight=qkv_weight,
        out_weight=out_weight,
        up_weight=up_weight,
        down_weight=down_weight,
    )
    hidden_out, grad_state, *gradients = whole(grid, cut, sizes, bias_widths, ins)
    old = (
        qkv_weight,
        qkv_first,
        qkv_second,
        out_weight,
        out_first,
        out_second,
        up_weight,
        up_first,
        up_second,
        down_weight,
        down_first,
        down_second,
        qkv_bias,
        qkv_bias_first,
        qkv_bias_second,
        up_bias,
        up_bias_first,
        up_bias_second,
        row_vectors,
        row_first,
        row_second,
    )
    return hidden_out, grad_state, *update_all(n_dp, bias_widths, out_rows, gradients, old)


def solution(mesh):
    placed = (
        P(("dp", "col"), "row"),
        P(("dp", "col"), "row"),
        P("dp"),
        P(None, ("row", "dp"), "col"),
        P(None, ("row", "dp"), "col"),
        P(None, ("row", "dp"), "col"),
        P(None, ("col", "dp"), "row"),
        P(None, ("col", "dp"), "row"),
        P(None, ("col", "dp"), "row"),
        P(None, ("row", "dp"), "col"),
        P(None, ("row", "dp"), "col"),
        P(None, ("row", "dp"), "col"),
        P(None, ("col", "dp"), "row"),
        P(None, ("col", "dp"), "row"),
        P(None, ("col", "dp"), "row"),
        P(None, ("col", "row", "dp")),
        P(None, ("col", "row", "dp")),
        P(None, ("col", "row", "dp")),
        P(None, ("col", "row", "dp")),
        P(None, ("col", "row", "dp")),
        P(None, ("col", "row", "dp")),
        P(None, None, "row"),
        P(None, None, "row"),
        P(None, None, "row"),
    )
    return jax.shard_map(
        on_device,
        mesh=mesh,
        in_specs=placed,
        out_specs=(
            P(("dp", "col"), "row"),
            P(("dp", "col"), "row"),
            P(None, ("row", "dp"), "col"),
            P(None, ("row", "dp"), "col"),
            P(None, ("row", "dp"), "col"),
            P(None, ("col", "dp"), "row"),
            P(None, ("col", "dp"), "row"),
            P(None, ("col", "dp"), "row"),
            P(None, ("row", "dp"), "col"),
            P(None, ("row", "dp"), "col"),
            P(None, ("row", "dp"), "col"),
            P(None, ("col", "dp"), "row"),
            P(None, ("col", "dp"), "row"),
            P(None, ("col", "dp"), "row"),
            P(None, ("col", "row", "dp")),
            P(None, ("col", "row", "dp")),
            P(None, ("col", "row", "dp")),
            P(None, ("col", "row", "dp")),
            P(None, ("col", "row", "dp")),
            P(None, ("col", "row", "dp")),
            P(None, None, "row"),
            P(None, None, "row"),
            P(None, None, "row"),
        ),
        check_vma=False,
    )
```

```python
import math
from functools import partial
from types import SimpleNamespace

import jax
import jax.numpy as jnp
from jax import lax
from jax.experimental import pallas as pl
from jax.experimental.pallas import tpu as pltpu
from jax.sharding import PartitionSpec as P

D = 1024
HEAD = 64
ROT = 16
LAYERS = 2
SEQS = 3
STEP = 10


EPS_NORM = 1e-05
EPS_ADAM = 1e-08
BETA_ONE = 0.9
BETA_TWO = 0.95
RATE_MATRIX = 0.06
RATE_VECTOR = 0.6
DECAY_MATRIX = 0.01
ROPE_BASE = 10000.0
MASK_VALUE = -1e30
CONTRACT_ROWS = (((0,), (0,)), ((), ()))
CONTRACT_COLS = (((1,), (1,)), ((), ()))

BF = jnp.bfloat16
F32 = jnp.float32
MESH = pl.DeviceIdType.MESH
GRIDS = {32: (4, 4, 2), 8: (2, 2, 2)}
VEC_ROWS = 8
VMEM_SPEC = pl.BlockSpec(memory_space=pltpu.VMEM)


def params(collective_id, mib):
    return pltpu.CompilerParams(
        collective_id=collective_id, has_side_effects=True, vmem_limit_bytes=mib << 20
    )


def remote(src, dst, sends, recvs, at, device):
    return pltpu.make_async_remote_copy(
        src_ref=src,
        dst_ref=dst,
        send_sem=sends.at[at],
        recv_sem=recvs.at[at],
        device_id=device,
        device_id_type=MESH,
    )


def greet(device):
    pl.semaphore_signal(
        pltpu.get_barrier_semaphore(), inc=1, device_id=device, device_id_type=MESH
    )


def greeted(count):
    pl.semaphore_wait(pltpu.get_barrier_semaphore(), count)


def group_place():
    return lax.axis_index("row") * 2 + lax.axis_index("col")


def group_peer(place, step):
    other = lax.rem(place + step, 4)
    return {"row": other // 2, "col": lax.rem(other, 2)}


def over(lengths, body):
    total = math.prod(lengths)

    def one(index, carry):
        place, rest = [], index
        for length in reversed(lengths):
            place.append(lax.rem(rest, length))
            rest = rest // length
        body(*reversed(place))
        return carry

    lax.fori_loop(0, total, one, 0)


def adamw(master, moment_one, moment_two, gradient, step_rate, step_decay):
    one_new = BETA_ONE * moment_one + (1.0 - BETA_ONE) * gradient
    two_new = BETA_TWO * moment_two + (1.0 - BETA_TWO) * gradient * gradient
    one_hat = one_new / (1.0 - BETA_ONE**STEP)
    two_hat = two_new / (1.0 - BETA_TWO**STEP)
    master_new = master - step_rate * (
        one_hat / (jnp.sqrt(two_hat) + EPS_ADAM) + step_decay * master
    )
    return (master_new, one_new, two_new)


class Copies:
    def __init__(self, sends, recvs):
        self.sends, self.recvs, self.count = sends, recvs, 0

    def to(self, src, dst, device):
        copy = remote(src, dst, self.sends, self.recvs, self.count, device)
        self.count += 1
        return copy


class Ring:
    def __init__(self, length, place, device_at):
        self.length, self.place, self.device_at = length, place, device_at
        self.ways = ((0, 1), (1, -1)) if length > 2 else ((0, 1),)

    def at(self, step):
        return lax.rem(self.place + step + self.length, self.length)

    def device(self, step):
        return self.device_at(self.at(step))


class RingGather:
    def __init__(self, copies, ring, views, sources=None, arrived=None):
        self.copies, self.ring, self.views = copies, ring, views
        self.sources, self.arrived = sources, arrived
        self.near, self.far = [[], []], [[], []]

    def start(self):
        for way, step in self.ring.ways:
            for k, view in enumerate(self.views):
                own = view(self.ring.place, None)
                src = self.sources[k] if self.sources else own
                copy = self.copies.to(src, own, self.ring.device(step))
                copy.start()
                self.near[way].append(copy)

    def middle(self):
        for way, step in self.ring.ways:
            for copy in self.near[way]:
                copy.wait_recv()
            came_from = self.ring.at(-step)
            if self.ring.length > 2:
                for view in self.views:
                    ref = view(came_from, way)
                    if ref is not None:
                        copy = self.copies.to(ref, ref, self.ring.device(step))
                        copy.start()
                        self.far[way].append(copy)
            if self.arrived:
                self.arrived(came_from)

    def end(self):
        for copy in self.far[0] + self.far[1]:
            copy.wait_recv()
        if self.arrived and self.ring.length > 2:
            self.arrived(self.ring.at(2))

    def finish(self):
        for copy in self.near[0] + self.near[1] + self.far[0] + self.far[1]:
            copy.wait_send()


class DirectGather:
    def __init__(self, copies, ring, views, sources):
        self.copies, self.ring, self.views, self.sources = copies, ring, views, sources
        self.sent = []

    def start(self):
        for step in range(1, self.ring.length):
            for view, source in zip(self.views, self.sources):
                own = view(self.ring.place, None)
                copy = self.copies.to(source, own, self.ring.device(step))
                copy.start()
                self.sent.append(copy)

    def end(self):
        for copy in self.sent:
            copy.wait_recv()

    def finish(self):
        for copy in self.sent:
            copy.wait_send()


class Summand:
    def __init__(self, ref, index, count, width, near, far):
        self.ref, self.index, self.count, self.width = ref, index, count, width
        self.near, self.far = near, far

    def view(self, target, start, width):
        return self.ref.at[self.index(slice(None), target, start, width)]

    def add(self, target, start, width, other):
        def one(lead):
            at = self.index(lead, target, start, width)
            more = other[...] if self.count is None else other[lead]
            self.ref[at] = (self.ref[at].astype(F32) + more.astype(F32)).astype(BF)

        if self.count is None:
            one(None)
        else:
            over((self.count,), one)

    def total(self, lead, target, ways):
        value = self.ref[self.index(lead, target, 0, self.width)].astype(F32)
        for way in range(ways):
            more = self.far[way][...] if self.count is None else self.far[way][lead]
            value = value + more.astype(F32)
        return value


class RingSum:
    def __init__(self, copies, ring, summands):
        self.copies, self.ring, self.summands = copies, ring, summands
        self.near, self.far = [[], []], [[], []]

    def start(self):
        if self.ring.length == 2:
            return
        for way, step in self.ring.ways:
            for s in self.summands:
                half = s.width // 2
                copy = self.copies.to(
                    s.view(self.ring.at(2), way * half, half), s.near[way], self.ring.device(step)
                )
                copy.start()
                self.near[way].append(copy)

    def middle(self):
        for way, step in self.ring.ways:
            target = self.ring.at(step)
            for k, s in enumerate(self.summands):
                if self.ring.length > 2:
                    self.near[way][k].wait_recv()
                    s.add(target, way * (s.width // 2), s.width // 2, s.near[way])
                copy = self.copies.to(
                    s.view(target, 0, s.width), s.far[way], self.ring.device(step)
                )
                copy.start()
                self.far[way].append(copy)

    def end(self):
        for copy in self.far[0] + self.far[1]:
            copy.wait_recv()

    def total(self, k, lead=None):
        return self.summands[k].total(lead, self.ring.place, len(self.ring.ways))

    def finish(self):
        for copy in self.near[0] + self.near[1] + self.far[0] + self.far[1]:
            copy.wait_send()


class DirectSum:
    def __init__(self, copies, ring, summand):
        self.copies, self.ring, self.summand = copies, ring, summand
        self.sent = []

    def start(self):
        for step in range(1, self.ring.length):
            copy = self.copies.to(
                self.summand.view(self.ring.at(step), 0, self.summand.width),
                self.summand.far[step - 1],
                self.ring.device(step),
            )
            copy.start()
            self.sent.append(copy)

    def end(self):
        for copy in self.sent:
            copy.wait_recv()

    def total(self):
        return self.summand.total(None, self.ring.place, self.ring.length - 1)

    def finish(self):
        for copy in self.sent:
            copy.wait_send()


def lanes_at(start, width):
    if not isinstance(start, int):
        start = pl.multiple_of(start, 128)
    return pl.ds(start, width)


class Slice:
    def __init__(self, grid):
        self.grid = grid
        nz, nx, nc = grid
        d = lax.axis_index("dp")
        self.d, self.z, self.x, self.core = d, d // (nx * nc), lax.rem(d // nc, nx), lax.rem(d, nc)
        self.row, self.col = lax.axis_index("row"), lax.axis_index("col")
        self.half = nz * nx * nc // 2
        self.place = group_place()
        self.zls = nz // 2
        self.partner = self.dp(self.z, self.x, 1 - self.core)
        self.z_ring = Ring(nz, self.z, lambda z: self.dp(z, self.x, self.core))
        self.x_ring = Ring(nx, self.x, lambda x: self.dp(self.z, x, self.core))
        self.y_ring = Ring(4, self.place, lambda q: {"row": q // 2, "col": lax.rem(q, 2)})

    def dp(self, z, x, core):
        _, nx, nc = self.grid
        return {"dp": (z * nx + x) * nc + core}

    def greet_rings(self, rings, whole=False):
        count = 0
        for ring in rings:
            steps = range(1, ring.length) if whole else [step for _, step in ring.ways]
            for step in steps:
                greet(ring.device(step))
                count += 1
        return count


class WeightGather:
    def __init__(self, here, cut, copies, local, own, full, spread):
        self.here, self.copies, self.core_copies = here, copies, []
        rows, lanes = own.shape
        pair = full.shape[-1] != lanes
        first = cut if pair else rows // 2
        cuts = (pl.ds(0, first), pl.ds(first, rows - first))
        z, x, core, zls = here.z, here.x, here.core, here.zls

        def part(width, half):
            return (0, width) if half is None else (half * (width // 2), width // 2)

        def chunk(order, along, half):
            zz, xx = (along, x) if order == 0 else (z, along)
            start, width = part(lanes, half)
            if pair:
                at = lanes_at((zz // zls) * lanes + start, width)
                return full.at[lax.rem(zz, zls), xx, core, cuts[order], at]
            return full.at[zz, xx, core, cuts[order], pl.ds(start, width)]

        def line(order, along, half):
            if order == 0:
                at = pl.ds(*part(full.shape[-1], half))
                return full.at[:, along, core, cuts[0], at]
            start, width = part(lanes, half)
            if pair:
                at = lanes_at((along // zls) * lanes + start, width)
                return full.at[lax.rem(along, zls), :, core, cuts[1], at]
            return full.at[along, :, core, cuts[1], pl.ds(start, width)]

        def small(order, along, half):
            return None if half == 1 else spread[1].at[along, x, core]

        def small_line(order, along, half):
            return None if half == 1 else spread[1].at[:, along, core]

        rings = ((here.z_ring, here.x_ring), (here.x_ring, here.z_ring))
        self.first, self.second, self.lines, self.own = [], [], [], []
        for order in range(2):
            sources = [own.at[cuts[order]]]
            chunks, lines = [partial(chunk, order)], [partial(line, order)]
            if order == 0 and spread:
                sources.append(spread[0])
                chunks.append(partial(small, order))
                lines.append(partial(small_line, order))
            for k, view in enumerate(chunks):
                self.own.append(
                    pltpu.make_async_copy(
                        sources[k], view(rings[order][0].place, None), local.at[order * 2 + k]
                    )
                )
            self.first.append(DirectGather(copies, rings[order][0], chunks, sources))
            self.second.append(
                RingGather(copies, rings[order][1], lines, None, partial(self.forward, order))
            )
            self.lines.append(lines)

    def forward(self, order, along):
        for view in self.lines[order]:
            ref = view(along, None)
            copy = self.copies.to(ref, ref, self.here.partner)
            copy.start()
            self.core_copies.append(copy)

    def start(self):
        for ring in self.first:
            ring.start()
        for copy in self.own:
            copy.start()

    def turn(self):
        for copy in self.own:
            copy.wait()
        for order in range(2):
            self.first[order].end()
            self.second[order].start()
            self.forward(order, self.second[order].ring.place)

    def second_middle(self):
        for ring in self.second:
            ring.middle()

    def end(self):
        for ring in self.second:
            ring.end()

    def arrive(self):
        for copy in self.core_copies:
            copy.wait_recv()

    def finish(self):
        for ring in self.first + self.second:
            ring.finish()
        for copy in self.core_copies:
            copy.wait_send()


def dot(left, right):
    return jnp.dot(left, right, preferred_element_type=F32)


def dot_rows(left, right):
    return lax.dot_general(left, right, CONTRACT_ROWS, preferred_element_type=F32)


def dot_cols(left, right):
    return lax.dot_general(left, right, CONTRACT_COLS, preferred_element_type=F32)


def norm_stats(state):
    width = state.shape[1]
    average = jnp.sum(state, 1, keepdims=True) / width
    spread = jnp.sum(state * state, 1, keepdims=True) / width - average * average
    inv_std = lax.rsqrt(spread + EPS_NORM)
    return ((state - average) * inv_std, inv_std)


def norm_back(grad_hat, hat):
    width = hat.shape[1]
    first = jnp.sum(grad_hat, 1, keepdims=True) / width
    second = jnp.sum(grad_hat * hat, 1, keepdims=True) / width
    return grad_hat - first - hat * second


class Layer:
    def __init__(self, layer, vec, tables, mask, bias, full_q, full_u, full_b, sizes):
        self.vec, self.tables, self.mask, self.bias = vec, tables, mask, bias
        self.layer, self.full_q, self.full_u, self.full_b = layer, full_q, full_u, full_b
        self.qkv_width, self.up_width, self.out_rows = sizes
        self.heads_here = self.qkv_width // (3 * HEAD)

    def vector(self, k):
        at = self.layer * VEC_ROWS + k
        return self.vec[at : at + 1, :]

    def q_matrix(self, start, width):
        return self.full_q[:, :, :, :, start : start + width].reshape(-1, width)

    def u_matrix(self, start, width):
        return self.full_u[:, :, :, :, start : start + width].reshape(-1, width)

    def b_matrix(self, low, high, start, width):
        value = self.full_b[:, :, :, low:high, start : start + width]
        return value.reshape(-1, width)

    def out_matrix(self, start, width):
        return self.b_matrix(0, self.out_rows, start, width)

    def down_matrix(self, start, width):
        return self.b_matrix(self.out_rows, self.full_b.shape[3], start, width)

    def inputs(self, hat, attn_in, mlp_in):
        attn_in[...] = (hat * self.vector(0) + self.vector(1)).astype(BF)
        mlp_in[...] = (hat * self.vector(2) + self.vector(3)).astype(BF)

    def project(self, attn_in, joined):
        pair = 6 * HEAD
        cosine, left, right = self.tables
        for start in range(0, self.qkv_width, pair):
            value = dot(attn_in[...], self.q_matrix(start, pair))
            value = value + self.bias[0:1, start : start + pair]
            value = (
                value * cosine[...]
                + pltpu.roll(value, pair - ROT // 2, 1) * left[...]
                + pltpu.roll(value, ROT // 2, 1) * right[...]
            )
            joined[:, start : start + pair] = value.astype(BF)

    def head(self, joined, h):
        start = h * 3 * HEAD
        return [joined[:, start + k * HEAD : start + (k + 1) * HEAD] for k in range(3)]

    def attend(self, joined, probs, heads):
        for h in range(self.heads_here):
            query, key_rows, value_rows = self.head(joined, h)
            scores = dot_cols(query, key_rows) * HEAD**-0.5 + self.mask[...]
            expo = jnp.exp(scores - jnp.max(scores, 1, keepdims=True))
            low = (expo / jnp.sum(expo, 1, keepdims=True)).astype(BF)
            probs[h] = low
            heads[:, h * HEAD : (h + 1) * HEAD] = dot(low, value_rows).astype(BF)

    def units(self, mlp_in, slope, units):
        width = 256
        for start in range(0, self.up_width, width):
            at = slice(start, start + width)
            value = dot(mlp_in[...], self.u_matrix(start, width))
            value = value + self.bias[1:2, at]
            below = 0.5 * (1.0 + lax.erf(value * 0.5**0.5))
            density = jnp.exp(value * value * -0.5) * ((2.0 * math.pi) ** -0.5)
            units[:, at] = (value * below).astype(BF)
            slope[:, at] = (below + value * density).astype(BF)

    def outputs(self, heads, units, start, width):
        return dot(heads[...], self.out_matrix(start, width)) + dot(
            units[...], self.down_matrix(start, width)
        )

    def branch_back(self, grad, slope, grad_heads, grad_pre):
        grad_heads[...] = dot_cols(grad[...], self.out_matrix(0, D)).astype(BF)
        zls = self.full_b.shape[0]
        width = self.up_width // zls
        step = min(width, 256)
        for zl in range(zls):
            matrix = self.full_b[zl, :, :, self.out_rows :, :].reshape(-1, D)
            for start in range(0, width, step):
                at = slice(zl * width + start, zl * width + start + step)
                pull = dot_cols(grad[...], matrix[start : start + step])
                grad_pre[:, at] = (pull * slope[:, at].astype(F32)).astype(BF)

    def attend_back(self, joined, probs, grad_heads, raw, grad_joined):
        for h in range(self.heads_here):
            query, key_rows, value_rows = self.head(joined, h)
            grad = grad_heads[:, h * HEAD : (h + 1) * HEAD]
            low = probs[h]
            high = low.astype(F32)
            grad_probs = dot_cols(grad, value_rows)
            inner = jnp.sum(grad_probs * high, 1, keepdims=True)
            grad_raw = (high * (grad_probs - inner) * HEAD**-0.5).astype(BF)
            start = h * 3 * HEAD
            raw[:, start : start + HEAD] = dot(grad_raw, key_rows)
            raw[:, start + HEAD : start + 2 * HEAD] = dot_rows(grad_raw, query)
            raw[:, start + 2 * HEAD : start + 3 * HEAD] = dot_rows(low, grad)
        pair = 6 * HEAD
        cosine, left, right = self.tables
        for start in range(0, self.qkv_width, pair):
            value = raw[:, start : start + pair]
            value = (
                value * cosine[...]
                + pltpu.roll(value * left[...], ROT // 2, 1)
                + pltpu.roll(value * right[...], pair - ROT // 2, 1)
            )
            grad_joined[:, start : start + pair] = value.astype(BF)

    def inputs_back(self, grad_joined, grad_pre, hat, grad, sums):
        grad_attn_in = dot_cols(grad_joined[...], self.q_matrix(0, self.qkv_width))
        rows = [
            jnp.sum(grad_attn_in * hat, 0, keepdims=True),
            jnp.sum(grad_attn_in, 0, keepdims=True),
        ]
        grad_hat = grad_attn_in * self.vector(0)
        grad_mlp_in = dot_cols(grad_pre[...], self.u_matrix(0, self.up_width))
        rows += [
            jnp.sum(grad_mlp_in * hat, 0, keepdims=True),
            jnp.sum(grad_mlp_in, 0, keepdims=True),
            jnp.sum(grad[...].astype(F32), 0, keepdims=True) * 0.25,
        ]
        for k, row in enumerate(rows):
            sums[k : k + 1, :] = row
        for k, (ref, width) in enumerate(
            ((grad_joined, self.qkv_width), (grad_pre, self.up_width))
        ):
            sums[5 + k : 6 + k, :] = jnp.zeros((1, D), F32)
            sums[5 + k : 6 + k, :width] = jnp.sum(ref[...].astype(F32), 0, keepdims=True)
        sums[7:8, :] = jnp.zeros((1, D), F32)
        return norm_back(grad_hat + grad_mlp_in * self.vector(2), hat)


def grads_a(left, right, out):
    width = right.shape[1]
    nz = out.shape[0]
    block = left.shape[1] // nz
    for k in range(nz):
        value = dot_rows(left[:, k * block : (k + 1) * block], right[...]).astype(BF)
        out[k] = value.reshape(*out.shape[1:4], width)


def grads_b(left, right, out, low, high):
    zls = out.shape[0]
    block = left.shape[1] // zls
    for k in range(zls):
        value = dot_rows(left[:, k * block : (k + 1) * block], right[...]).astype(BF)
        out[k, :, :, low:high, :] = value.reshape(*out.shape[1:3], high - low, D)


def rows_index(rows):
    def index(lead, target, start, width):
        return (
            pl.ds(pl.multiple_of(target * rows, rows), rows),
            lanes_at(start, width),
        )

    return index


def blocks_index(rows, lanes):
    def index(lead, target, start, width):
        return (
            pl.ds(pl.multiple_of(lax.rem(target, 2) * rows, rows), rows),
            lanes_at((target // 2) * lanes + start, width),
        )

    return index


def group_sum(here, copies, part, index, width, near, far):
    summand = Summand(part, index, None, width, (near.at[0], near.at[1]), (far.at[0], far.at[1]))
    return RingSum(copies, here.y_ring, [summand])


def group_gather(here, copies, whole, rows):
    def view(target, half):
        width = whole.shape[1]
        start, width = (0, width) if half is None else (half * (width // 2), width // 2)
        return whole.at[pl.ds(pl.multiple_of(target * rows, rows), rows), pl.ds(start, width)]

    return RingGather(copies, here.y_ring, [view])


def own_rows(here, rows):
    return pl.ds(pl.multiple_of(here.place * rows, rows), rows)


def ring_scratch(rows, width):
    return [pltpu.VMEM((2, rows, width // 2), BF), pltpu.VMEM((2, rows, width), BF)]


class GradSum:
    def __init__(self, here, cut, copies, kind, g, s, buffers):
        self.here, self.copies, self.kind, self.g, self.s = here, copies, kind, g, s
        self.near, self.far, self.mid, self.top, self.fin = buffers
        rows = g.shape[3]
        first = rows // 2 if kind == "a" else cut
        self.cuts = (pl.ds(0, first), pl.ds(first, rows - first))
        self.full = g.shape[4]
        self.lanes = self.full // 2
        self.lines, self.turns = [None, None], [None, None]

    def start(self):
        self.core = []
        for order in range(2):
            copy = self.copies.to(
                self.g.at[:, :, 1 - self.here.core, self.cuts[order]],
                self.s.at[:, :, self.cuts[order]],
                self.here.partner,
            )
            copy.start()
            self.core.append(copy)

    def line(self, order):
        here, at, zls = self.here, self.cuts[order], self.here.zls
        self.core[order].wait_recv()

        def add(zz, xx):
            self.s[zz, xx, at] = (
                self.s[zz, xx, at].astype(F32) + self.g[zz, xx, here.core, at].astype(F32)
            ).astype(BF)

        over(self.s.shape[:2], add)
        nx = self.s.shape[1]
        if order == 0:
            ring, count, width = here.x_ring, self.s.shape[0], self.full

            def index(lead, target, start, width):
                return (lead, target, at, lanes_at(start, width))

        elif self.kind == "a":
            ring, count, width = here.z_ring, nx, self.full

            def index(lead, target, start, width):
                return (target, lead, at, lanes_at(start, width))

        else:
            ring, count, width = here.z_ring, nx, self.lanes

            def index(lead, target, start, width):
                return (
                    lax.rem(target, zls),
                    lead,
                    at,
                    lanes_at((target // zls) * self.lanes + start, width),
                )

        summand = Summand(
            self.s,
            index,
            count,
            width,
            (self.near[order].at[0], self.near[order].at[1]),
            (self.far[order].at[0], self.far[order].at[1]),
        )
        self.lines[order] = RingSum(self.copies, ring, [summand])
        self.lines[order].start()

    def line_middle(self, order):
        self.lines[order].middle()

    def turn(self, order):
        here, zls, mid = self.here, self.here.zls, self.mid[order]
        line = self.lines[order]
        line.end()

        def put(lead):
            mid[lead] = line.total(0, lead).astype(BF)

        over(mid.shape[:1], put)
        ring = here.z_ring if order == 0 else here.x_ring
        if self.kind == "b" and order == 0:

            def index(lead, target, start, width):
                return (
                    lax.rem(target, zls),
                    slice(None),
                    lanes_at((target // zls) * self.lanes + start, width),
                )

        else:

            def index(lead, target, start, width):
                return (target, slice(None), lanes_at(start, width))

        summand = Summand(
            mid,
            index,
            None,
            self.full if self.kind == "a" else self.lanes,
            None,
            [self.top[order].at[k] for k in range(ring.length - 1)],
        )
        self.turns[order] = DirectSum(self.copies, ring, summand)
        self.turns[order].start()

    def end(self, order):
        self.turns[order].end()
        value = self.turns[order].total().astype(BF)
        if self.kind == "a":
            self.fin[order] = value
        else:
            self.fin[self.cuts[order]] = value

    def finish(self):
        for copy in self.core:
            copy.wait_send()
        for order in range(2):
            self.lines[order].finish()
            self.turns[order].finish()


def grad_buffers(grid, cut, g_shape, kind):
    nz, nx, _ = grid
    rows, full = g_shape[3:]
    zls = g_shape[0]
    first = rows // 2 if kind == "a" else cut
    lanes = full if kind == "a" else full // 2
    cuts = (first, rows - first)

    def low(*dims):
        return pltpu.VMEM(dims, BF)

    counts = (zls, nx)
    widths = (full, lanes)
    fin = low(2, first, full) if kind == "a" else low(rows, lanes)
    return [
        low(zls, nx, rows, full),
        *[low(2, counts[o], cuts[o], widths[o] // 2) for o in range(2)],
        *[low(2, counts[o], cuts[o], widths[o]) for o in range(2)],
        *[low(counts[o], cuts[o], widths[o]) for o in range(2)],
        *[low((nz, nx)[o] - 1, cuts[o], lanes) for o in range(2)],
        fin,
    ]


def grad_sum(here, cut, copies, kind, g, refs):
    s, near0, near1, far0, far1, mid0, mid1, top0, top1, fin = refs
    return GradSum(
        here,
        cut,
        copies,
        kind,
        g,
        s,
        ((near0, near1), (far0, far1), (mid0, mid1), (top0, top1), fin),
    )


def lane_iota(rows, lanes):
    return lax.broadcasted_iota(jnp.int32, (rows, lanes), 1)


def make_tables(ids, live, cosine, left, right, mask):
    length = ids.shape[1]
    other = ids[...]
    row = lax.broadcasted_iota(jnp.int32, (length, length), 0)
    column = lax.broadcasted_iota(jnp.int32, (length, length), 1)
    other = jnp.broadcast_to(other.astype(F32), (length, length))
    own = jnp.sum(jnp.where(row == column, other, 0.0), 1, keepdims=True)
    live[...] = jnp.broadcast_to(jnp.where(own < SEQS, 1.0, 0.0), live.shape)
    earlier = jnp.sum((other < own).astype(F32), 1, keepdims=True)
    mask[...] = jnp.where((other == own) & (column <= row), 0.0, MASK_VALUE)
    place = lax.broadcasted_iota(jnp.int32, (length, 1), 0).astype(F32) - earlier
    lane = lane_iota(1, 128)
    at = lax.rem(lane, HEAD)
    turned = at < ROT
    power = lax.rem(at, ROT // 2).astype(F32)
    frequency = jnp.exp(power * (-2.0 / ROT * math.log(ROPE_BASE)))
    angles = place * frequency
    cos_part = jnp.where(turned, jnp.cos(angles), 1.0)
    sin_part = jnp.sin(angles)
    left_part = jnp.where(at < ROT // 2, -sin_part, 0.0)
    right_part = jnp.where(turned & (at >= ROT // 2), sin_part, 0.0)
    low_half = lane < HEAD
    for ref, value, rest in ((cosine, cos_part, 1.0), (left, left_part, 0.0), (right, right_part, 0.0)):
        ref[:, 0:128] = value
        ref[:, 128:256] = jnp.where(low_half, rest, value)
        ref[:, 256:384] = jnp.where(low_half, value, rest)


def make_biases(full_c, bias, widths):
    n_dp = math.prod(full_c.shape[:3])
    table = full_c[...].reshape(n_dp, *full_c.shape[3:])
    lanes = full_c.shape[4]
    for layer in range(LAYERS):
        values = table[:, layer, :].astype(BF)
        first = 0
        for k, width in enumerate(widths):
            total = n_dp * width
            lane = lax.broadcasted_iota(jnp.int32, (lanes, total), 0)
            column = lax.broadcasted_iota(jnp.int32, (lanes, total), 1)
            pick = jnp.where(lane == lax.rem(column, width) + first, 1.0, 0.0).astype(BF)
            spread = dot(values, pick)
            device = lax.broadcasted_iota(jnp.int32, (n_dp, total), 0)
            column = lax.broadcasted_iota(jnp.int32, (n_dp, total), 1)
            mine = jnp.where(column // width == device, spread, 0.0)
            bias[layer * 2 + k : layer * 2 + k + 1, :total] = jnp.sum(mine, 0, keepdims=True)
            first += width


def whole_kernel(grid, cut, sizes, widths, tree, *refs):
    at = SimpleNamespace(**jax.tree.unflatten(tree, refs))
    sends, recvs, local = at.sends, at.recvs, at.local
    here = Slice(grid)
    nz, nx, _ = grid
    copies = Copies(sends, recvs)
    copies.count = 48
    d, r, c, half = here.d, here.row, here.col, here.half
    hid, cot = at.hid, at.cot
    hid_all, cot_all, vec = at.hid_all, at.cot_all, at.vec
    rows, lanes = hid.shape
    quarter = rows // 2
    dh, dl = d // half, lax.rem(d, half)
    swap_needed = dh != r
    swap_to = {"dp": r * half + dl, "row": dh}
    slot_rows = at.qkv_weight.shape[1]
    forth = [{"dp": r * half + d // 2, "row": k} for k in range(2)]
    back_to = [{"dp": 2 * dl + k, "row": dh} for k in range(2)]
    forth_self = [(r == k) & (r * half + d // 2 == d) for k in range(2)]
    back_self = [(dh == r) & (2 * dl + k == d) for k in range(2)]
    slot = lax.rem(d, 2)

    count = here.greet_rings([here.z_ring, here.x_ring, here.y_ring], whole=True)
    greet(here.partner)
    for k in range(2):
        for device, itself in ((forth[k], forth_self[k]), (back_to[k], back_self[k])):

            @pl.when(jnp.logical_not(itself))
            def _():
                greet(device)

    @pl.when(swap_needed)
    def _():
        greet(swap_to)

    qkv_width, up_width, out_rows = sizes
    wa, wb = (at.wq, at.wu), at.wb

    def cast(layer):
        for ref, given, width in ((wa[0], at.qkv_weight, qkv_width), (wa[1], at.up_weight, up_width)):
            for k in range(2):
                ref[layer, k] = given[layer, :, k * width : (k + 1) * width].astype(BF)
        wb[layer, :out_rows] = at.out_weight[layer].astype(BF)
        wb[layer, out_rows:] = at.down_weight[layer].astype(BF)

    cast(0)
    vec_own, wc = at.vec_own, at.wc
    vec_own[...] = jnp.zeros(vec_own.shape, F32)
    for layer in range(LAYERS):
        for k in range(6):
            row = layer * VEC_ROWS + k
            vec_own[row : row + 1] = at.row_vectors[k, layer : layer + 1]
    wc[...] = jnp.zeros(wc.shape, F32)
    wc[:LAYERS, : widths[0]] = at.qkv_bias[...]
    wc[:LAYERS, widths[0] : sum(widths)] = at.up_bias[...]
    greeted(
        count
        + 5
        + swap_needed.astype(jnp.int32)
        - sum(k.astype(jnp.int32) for k in forth_self + back_self)
    )

    def when_else(condition, there, here_do):
        pl.when(condition)(there)
        pl.when(jnp.logical_not(condition))(here_do)

    def pair(src, dst, send, recv, device):
        return pltpu.make_async_remote_copy(
            src_ref=src,
            dst_ref=dst,
            send_sem=sends.at[send],
            recv_sem=recvs.at[recv],
            device_id=device,
            device_id_type=MESH,
        )

    a_own, b_own = (at.q_own, at.u_own), at.b_own
    slot_at = pl.ds(pl.multiple_of(slot * slot_rows, slot_rows), slot_rows)

    def a_copy(layer, kind, k):
        base = layer * 8 + kind * 2
        return pair(
            wa[kind].at[layer, k], a_own[kind].at[layer, slot_at], base + k, base + slot, forth[k]
        )

    def a_arrival(layer, kind, k):
        base = layer * 8 + kind * 2
        into = a_own[kind].at[layer, pl.ds(k * slot_rows, slot_rows)]
        return pair(wa[kind].at[layer, 0], into, base, base + k, back_to[k])

    def a_local(layer, kind, k):
        return pltpu.make_async_copy(
            wa[kind].at[layer, k], a_own[kind].at[layer, slot_at], local.at[24 + layer * 2 + kind]
        )

    def swap_copy(layer):
        return pair(wb.at[layer], b_own.at[layer], layer * 8 + 4, layer * 8 + 4, swap_to)

    def swap_local(layer):
        return pltpu.make_async_copy(wb.at[layer], b_own.at[layer], local.at[28 + layer])

    def begin(layer):
        for kind in range(2):
            for k in range(2):
                when_else(
                    forth_self[k],
                    lambda: a_local(layer, kind, k).start(),
                    lambda: a_copy(layer, kind, k).start(),
                )
        when_else(
            swap_needed, lambda: swap_copy(layer).start(), lambda: swap_local(layer).start()
        )

    def complete_a(layer, kind):
        for k in range(2):
            when_else(
                forth_self[k],
                lambda: a_local(layer, kind, k).wait(),
                lambda: a_copy(layer, kind, k).wait_send(),
            )

            @pl.when(jnp.logical_not(back_self[k]))
            def _():
                a_arrival(layer, kind, k).wait_recv()

    def complete_b(layer):
        when_else(swap_needed, lambda: swap_copy(layer).wait(), lambda: swap_local(layer).wait())

    begin(0)
    tokens = pl.ds(pl.multiple_of(c * rows, rows), rows)
    features = pl.ds(pl.multiple_of(r * lanes, lanes), lanes)
    hid_copies = [
        copies.to(hid, hid_all.at[tokens, features], here.y_ring.device(k)) for k in range(1, 4)
    ]
    cot_copies = [
        copies.to(cot, cot_all.at[tokens, features], here.y_ring.device(k)) for k in range(1, 4)
    ]
    hid_copies.append(copies.to(vec_own, vec.at[:, features], {"row": 1 - r}))
    own = [
        pltpu.make_async_copy(hid, hid_all.at[tokens, features], local.at[36]),
        pltpu.make_async_copy(cot, cot_all.at[tokens, features], local.at[37]),
        pltpu.make_async_copy(vec_own, vec.at[:, features], local.at[38]),
    ]
    for copy in hid_copies + own:
        copy.start()
    tables, mask, bias = (at.cosine, at.left, at.right), at.mask, at.bias
    complete_a(0, 0)

    full = ((at.q_zero, at.u_zero, at.b_zero), (at.q_one, at.u_one, at.b_one))
    full_c = at.full_c
    gathers = []
    for k in range(LAYERS):
        for kind in range(3):
            source = (a_own + (b_own,))[kind].at[k]
            spread = (wc, full_c) if k == 0 and kind == 0 else None
            count = 4 * (3 * k + kind)
            gathers.append(
                WeightGather(
                    here, cut, copies, local.at[pl.ds(count, 4)], source, full[k][kind], spread
                )
            )
    near, late = gathers[:3], gathers[3:]
    near[0].start()
    complete_a(0, 1)
    near[1].start()
    complete_b(0)
    near[2].start()
    make_tables(at.ids, at.live, *tables, mask)
    layers = [
        Layer(k, vec, tables, mask, bias.at[pl.ds(2 * k, 2)], *full[k], sizes)
        for k in range(LAYERS)
    ]
    attn_in, mlp_in, joined, probs = at.attn_in, at.mlp_in, at.joined, at.probs
    heads, slope, units = at.heads, at.slope, at.units
    near[0].turn()
    for copy in hid_copies + own:
        copy.wait()
    near[0].second_middle()
    near[1].turn()
    hat, _ = norm_stats(hid_all[...].astype(F32))
    layers[0].inputs(hat, attn_in[0], mlp_in[0])
    near[0].end()
    near[1].second_middle()
    near[2].turn()
    cast(1)
    begin(1)
    near[0].arrive()
    make_biases(full_c, bias, widths)
    layers[0].project(attn_in[0], joined[0])
    near[1].end()
    near[2].second_middle()
    complete_a(1, 0)
    late[0].start()
    complete_a(1, 1)
    late[1].start()
    complete_b(1)
    late[2].start()
    for copy in cot_copies:
        copy.start()
    mine = own_rows(here, quarter)
    layers[0].attend(joined[0], probs[0], heads[0])
    near[2].end()
    near[1].arrive()
    late[0].turn()
    layers[0].units(mlp_in[0], slope[0], units[0])
    late[0].second_middle()
    late[1].turn()
    near[2].arrive()
    part = at.part[0]
    for start in (0, D // 2):
        part[:, start : start + D // 2] = (
            layers[0].outputs(heads[0], units[0], start, D // 2).astype(BF)
        )
    summed = group_sum(here, copies, part, rows_index(quarter), D, at.near[0], at.far[0])
    summed.start()
    late[1].second_middle()
    late[2].turn()
    summed.middle()
    state = hid_all[mine, :].astype(F32) + layers[0].vector(4) + layers[0].vector(5)
    summed.end()
    state = state + summed.total(0)
    at.state[...] = state
    hat, inverse = norm_stats(state)
    inv_std, hat_all = at.inv_std, at.hat_all
    inv_std[...] = jnp.broadcast_to(inverse, inv_std.shape)
    hat_all[mine, :] = hat.astype(BF)
    spread = group_gather(here, copies, hat_all, quarter)
    spread.start()
    grad = (at.grad[0], at.grad[1])
    for copy in cot_copies:
        copy.wait()
    grad[1][...] = (
        cot_all[...].astype(F32) * at.live[:, :1]
    ).astype(BF)
    spread.middle()
    late[2].second_middle()
    for one in late:
        one.end()
    spread.end()
    for one in late:
        one.arrive()
    for one in gathers:
        one.finish()
    rings = [summed, spread]

    grads = [
        full[1],
        (at.gq, at.gu, at.gb),
    ]
    sum_q, sum_u, sum_b = [
        [
            grad_sum(
                here,
                cut,
                copies,
                "aab"[kind],
                grads[k][kind],
                at.sum_buffers[k][kind],
            )
            for k in range(LAYERS)
        ]
        for kind in range(3)
    ]
    out_q, out_u, out_b = at.out_q, at.out_u, at.out_b

    def owner_copy(layer, kind, order):
        out, one = ((out_q, sum_q), (out_u, sum_u))[kind]
        base = 16 + layer * 8 + kind * 2
        return pair(
            one[layer].fin.at[order], out.at[layer, r], base + order, base + r, back_to[order]
        )

    def owner_arrival(layer, kind, k):
        out, one = ((out_q, sum_q), (out_u, sum_u))[kind]
        base = 16 + layer * 8 + kind * 2
        return pair(one[layer].fin.at[0], out.at[layer, k], base, base + k, forth[k])

    def owner_local(layer, kind, order):
        out, one = ((out_q, sum_q), (out_u, sum_u))[kind]
        return pltpu.make_async_copy(
            one[layer].fin.at[order], out.at[layer, r], local.at[30 + layer * 2 + kind]
        )

    def out_swap(layer):
        return pair(sum_b[layer].fin, out_b.at[layer], 20 + layer * 8, 20 + layer * 8, swap_to)

    def out_local(layer):
        return pltpu.make_async_copy(sum_b[layer].fin, out_b.at[layer], local.at[34 + layer])

    def hand_a(layer, kind):
        for order in range(2):
            when_else(
                back_self[order],
                lambda: owner_local(layer, kind, order).start(),
                lambda: owner_copy(layer, kind, order).start(),
            )

    def hand_b(layer):
        when_else(swap_needed, lambda: out_swap(layer).start(), lambda: out_local(layer).start())

    def handed(layer):
        for kind in range(2):
            for k in range(2):
                when_else(
                    back_self[k],
                    lambda: owner_local(layer, kind, k).wait(),
                    lambda: owner_copy(layer, kind, k).wait_send(),
                )

                @pl.when(jnp.logical_not(forth_self[k]))
                def _():
                    owner_arrival(layer, kind, k).wait_recv()

        when_else(swap_needed, lambda: out_swap(layer).wait(), lambda: out_local(layer).wait())

    def phase(step, which):
        for order in range(2):
            for one in which:
                step(one, order)

    layer = layers[1]
    layer.inputs(hat_all[...].astype(F32), attn_in[1], mlp_in[1])
    layer.project(attn_in[1], joined[1])
    layer.attend(joined[1], probs[1], heads[1])
    layer.units(mlp_in[1], slope[1], units[1])
    b_high = at.gb.shape[3]
    grads_b(heads[1], grad[1], grads[1][2], 0, out_rows)
    grads_b(units[1], grad[1], grads[1][2], out_rows, b_high)
    sum_b[1].start()
    part = at.part[1]
    for start in (0, D // 2):
        part[:, start : start + D // 2] = (
            layer.outputs(heads[1], units[1], start, D // 2).astype(BF)
        )
    part[mine, :] = (part[mine, :].astype(F32) + at.state[...]).astype(BF)
    out_sum = group_sum(
        here, copies, part, blocks_index(rows, lanes), lanes, at.near[1], at.far[1]
    )
    out_sum.start()
    grad_heads, grad_pre, raw, grad_joined = at.grad_heads, at.grad_pre, at.raw, at.grad_joined
    sums = at.sums
    layer.branch_back(grad[1], slope[1], grad_heads, grad_pre)
    phase(GradSum.line, [sum_b[1]])
    layer.attend_back(joined[1], probs[1], grad_heads, raw, grad_joined)
    phase(GradSum.line_middle, [sum_b[1]])
    back = at.back[1]
    back[...] = layer.inputs_back(
        grad_joined, grad_pre, hat_all[...].astype(F32), grad[1], sums[1]
    ).astype(BF)
    summed = group_sum(here, copies, back, rows_index(quarter), D, at.near[2], at.far[2])
    summed.start()
    grads_a(mlp_in[1], grad_pre, grads[1][1])
    sum_u[1].start()
    summed.middle()
    grads_a(attn_in[1], grad_joined, grads[1][0])
    sum_q[1].start()
    out_sum.middle()
    phase(GradSum.turn, [sum_b[1]])
    summed.end()
    grad_one = at.grad_one
    total = grad[1][mine, :].astype(F32) + inv_std[:, :1] * summed.total(0)
    grad_one[...] = total
    grad[0][mine, :] = total.astype(BF)
    spread = group_gather(here, copies, grad[0], quarter)
    spread.start()
    phase(GradSum.line, [sum_u[1]])
    spread.middle()
    phase(GradSum.line, [sum_q[1]])
    out_sum.end()
    first_bias = vec[VEC_ROWS + 4 : VEC_ROWS + 5, features]
    bias_sum = first_bias + vec[VEC_ROWS + 5 : VEC_ROWS + 6, features]
    at.hidden[...] = (out_sum.total(0) + bias_sum).astype(BF)
    phase(GradSum.line_middle, [sum_u[1]])
    spread.end()
    rings += [out_sum, summed, spread]

    def conclude(layer_index, one, kind):
        for order in range(2):
            one.end(order)
        if kind == 2:
            hand_b(layer_index)
        else:
            hand_a(layer_index, kind)

    layer = layers[0]
    grads_b(heads[0], grad[0], grads[0][2], 0, out_rows)
    grads_b(units[0], grad[0], grads[0][2], out_rows, b_high)
    sum_b[0].start()
    phase(GradSum.line_middle, [sum_q[1]])
    layer.branch_back(grad[0], slope[0], grad_heads, grad_pre)
    conclude(1, sum_b[1], 2)
    phase(GradSum.turn, [sum_u[1]])
    phase(GradSum.line, [sum_b[0]])
    grads_a(mlp_in[0], grad_pre, grads[0][1])
    sum_u[0].start()
    phase(GradSum.turn, [sum_q[1]])
    layer.attend_back(joined[0], probs[0], grad_heads, raw, grad_joined)
    phase(GradSum.line_middle, [sum_b[0]])
    grads_a(attn_in[0], grad_joined, grads[0][0])
    sum_q[0].start()
    phase(GradSum.line, [sum_u[0]])
    hat, inverse = norm_stats(hid_all[...].astype(F32))
    value = layer.inputs_back(grad_joined, grad_pre, hat, grad[0], sums[0])
    back = at.back[0]
    back[...] = (inverse * value).astype(BF)
    back[mine, :] = (back[mine, :].astype(F32) + grad_one[...]).astype(BF)
    summed = group_sum(
        here, copies, back, blocks_index(rows, lanes), lanes, at.near[3], at.far[3]
    )
    summed.start()
    phase(GradSum.line, [sum_q[0]])
    v_core, v_line, v_last, v_group = at.v_core, at.v_line, at.v_last, at.v_group
    v_lanes = D // 2
    v_mine = pl.ds(pl.multiple_of(here.core * v_lanes, v_lanes), v_lanes)
    v_other = pl.ds(pl.multiple_of((1 - here.core) * v_lanes, v_lanes), v_lanes)
    v_copies = [copies.to(sums[k].at[:, v_other], v_core.at[k], here.partner) for k in range(2)]
    for copy in v_copies:
        copy.start()
    phase(GradSum.line_middle, [sum_u[0]])
    summed.middle()
    conclude(1, sum_u[1], 1)
    conclude(1, sum_q[1], 0)
    phase(GradSum.turn, [sum_b[0]])
    for copy in v_copies:
        copy.wait()
    for k in range(LAYERS):
        v_line[here.x, k * VEC_ROWS : (k + 1) * VEC_ROWS] = v_core[k] + sums[k][:, v_mine]
    v_x = [
        copies.to(v_line.at[here.x], v_line.at[here.x], here.x_ring.device(k))
        for k in range(1, nx)
    ]
    for copy in v_x:
        copy.start()
    phase(GradSum.line_middle, [sum_q[0]])
    phase(GradSum.turn, [sum_u[0]])
    summed.end()
    at.grad_out[...] = summed.total(0)
    rings.append(summed)
    for copy in v_x:
        copy.wait()
    total = v_line[0]
    for k in range(1, nx):
        total = total + v_line[k]
    v_last[here.z] = total
    v_z = [
        copies.to(v_last.at[here.z], v_last.at[here.z], here.z_ring.device(k))
        for k in range(1, nz)
    ]
    for copy in v_z:
        copy.start()
    phase(GradSum.turn, [sum_q[0]])
    conclude(0, sum_b[0], 2)
    for copy in v_z:
        copy.wait()
    total = v_last[0]
    for k in range(1, nz):
        total = total + v_last[k]
    v_group[here.place] = total
    v_y = [
        copies.to(v_group.at[here.place], v_group.at[here.place], here.y_ring.device(k))
        for k in range(1, 4)
    ]
    for copy in v_y:
        copy.start()
    conclude(0, sum_u[0], 1)
    conclude(0, sum_q[0], 0)
    for copy in v_y:
        copy.wait()
    total = v_group[0]
    for k in range(1, 4):
        total = total + v_group[k]
    out_v = at.out_v
    out_v[0, :, v_mine] = total
    out_v[1, :, v_mine] = v_group[here.place]
    v_swap = copies.to(out_v.at[:, :, v_mine], out_v.at[:, :, v_mine], here.partner)
    v_swap.start()
    v_swap.wait()
    handed(1)
    handed(0)
    assert copies.count <= sends.shape[0], copies.count
    for ring in rings:
        ring.finish()
    for one in sum_q + sum_u + sum_b:
        one.finish()


def whole(grid, cut, sizes, widths, ins):
    nz, nx, nc = grid
    qkv_width, up_width, out_rows = sizes
    rows, lanes = ins["hid"].shape
    group, quarter = 2 * rows, rows // 2
    slot_rows, down_rows = ins["qkv_weight"].shape[1], ins["down_weight"].shape[1]
    b_rows = out_rows + down_rows
    heads_here = qkv_width // (3 * HEAD)

    def low(*dims):
        return pltpu.VMEM(dims, BF)

    def high(*dims):
        return pltpu.VMEM(dims, F32)

    def twice(make, *dims):
        return [make(*dims) for _ in range(LAYERS)]

    shape = jax.ShapeDtypeStruct
    outs = dict(
        hidden=shape((rows, lanes), BF),
        grad_out=shape((rows, lanes), F32),
        out_q=shape((LAYERS, 2, slot_rows, qkv_width), BF),
        out_u=shape((LAYERS, 2, slot_rows, up_width), BF),
        out_b=shape((LAYERS, b_rows, lanes), BF),
        out_v=shape((2, LAYERS * VEC_ROWS, D), F32),
    )
    q_shape = (nz, nx, nc, 2 * slot_rows, qkv_width)
    u_shape = (nz, nx, nc, 2 * slot_rows, up_width)
    b_shape = (nz // 2, nx, nc, b_rows, 2 * lanes)
    c_shape = (8, -(-sum(widths) // 128) * 128)
    kinds = ((q_shape, "a"), (u_shape, "a"), (b_shape, "b"))
    blocks = [ring_scratch(quarter, D), ring_scratch(rows, lanes)] * 2
    scratch = dict(
        hid_all=low(group, D),
        cot_all=low(group, D),
        vec=high(LAYERS * VEC_ROWS, D),
        vec_own=high(LAYERS * VEC_ROWS, lanes),
        wq=low(LAYERS, 2, slot_rows, qkv_width),
        wu=low(LAYERS, 2, slot_rows, up_width),
        wb=low(LAYERS, b_rows, lanes),
        wc=high(*c_shape),
        q_own=low(LAYERS, 2 * slot_rows, qkv_width),
        u_own=low(LAYERS, 2 * slot_rows, up_width),
        b_own=low(LAYERS, b_rows, lanes),
        q_zero=low(*q_shape),
        q_one=low(*q_shape),
        u_zero=low(*u_shape),
        u_one=low(*u_shape),
        b_zero=low(*b_shape),
        b_one=low(*b_shape),
        full_c=high(nz, nx, nc, *c_shape),
        cosine=high(group, 6 * HEAD),
        left=high(group, 6 * HEAD),
        right=high(group, 6 * HEAD),
        mask=high(group, group),
        live=high(group, 128),
        bias=high(2 * LAYERS, D),
        state=high(quarter, D),
        inv_std=high(quarter, 128),
        hat_all=low(group, D),
        grad_one=high(quarter, D),
        grad_heads=low(group, heads_here * HEAD),
        grad_pre=low(group, up_width),
        raw=high(group, qkv_width),
        grad_joined=low(group, qkv_width),
        gq=low(*q_shape),
        gu=low(*u_shape),
        gb=low(*b_shape),
        v_core=high(2, VEC_ROWS, D // 2),
        v_line=high(nx, LAYERS * VEC_ROWS, D // 2),
        v_last=high(nz, LAYERS * VEC_ROWS, D // 2),
        v_group=high(4, LAYERS * VEC_ROWS, D // 2),
        attn_in=twice(low, group, D),
        mlp_in=twice(low, group, D),
        joined=twice(low, group, qkv_width),
        probs=twice(low, heads_here, group, group),
        heads=twice(low, group, heads_here * HEAD),
        slope=twice(low, group, up_width),
        units=twice(low, group, up_width),
        part=twice(low, group, D),
        back=twice(low, group, D),
        grad=twice(low, group, D),
        sums=twice(high, VEC_ROWS, D),
        sum_buffers=[
            [grad_buffers(grid, cut, dims, kind) for dims, kind in kinds] for _ in range(LAYERS)
        ],
        near=[block[0] for block in blocks],
        far=[block[1] for block in blocks],
        sends=pltpu.SemaphoreType.DMA((480,)),
        recvs=pltpu.SemaphoreType.DMA((480,)),
        local=pltpu.SemaphoreType.DMA((40,)),
    )
    flat = jax.tree.leaves(scratch)
    tree = jax.tree.structure(dict(**ins, **outs, **scratch))
    order = [*ins.values(), *outs.values(), *scratch.values()]
    names = [*ins, *outs, *scratch]
    ranks = jax.tree.unflatten(
        jax.tree.structure(dict(zip(names, order))), range(tree.num_leaves)
    )
    given = jax.tree.leaves([ranks[name] for name in names])

    def kernel(*refs):
        placed = [None] * len(refs)
        for rank, ref in zip(given, refs):
            placed[rank] = ref
        whole_kernel(grid, cut, sizes, widths, tree, *placed)

    flat = jax.tree.leaves(list(scratch.values()))
    return pl.pallas_call(
        kernel,
        out_shape=tuple(outs.values()),
        in_specs=[VMEM_SPEC] * len(ins),
        out_specs=(VMEM_SPEC,) * len(outs),
        scratch_shapes=flat,
        compiler_params=params(0, 63),
        name="whole_step",
    )(*ins.values())


def update_kernel(n_dp, bias_widths, out_rows, whole_count, *refs):
    passed, refs = refs[:whole_count], refs[whole_count:]
    given, refs = refs[:25], refs[25:]
    passed_out, refs = refs[:whole_count], refs[whole_count:]
    results, refs = refs[:21], refs[21:]
    held, made, in_sems, out_sems = refs[:25], refs[25:46], refs[46], refs[47]
    d, r = lax.axis_index("dp"), lax.axis_index("row")
    loads = [
        pltpu.make_async_copy(src, dst, in_sems.at[k])
        for k, (src, dst) in enumerate(zip(given, held))
    ]
    stores = [
        pltpu.make_async_copy(src, dst, out_sems.at[k])
        for k, (src, dst) in enumerate(zip(made + passed, results + passed_out))
    ]
    for copy in loads:
        copy.start()
    for copy in stores[21:]:
        copy.start()
    own_q, own_u, own_b, all_v = held[:4]
    old = held[4:]
    for copy in loads[:4]:
        copy.wait()

    def update(k, at, gradient, rate, decay):
        values = adamw(*[ref[at] for ref in old[3 * k : 3 * k + 3]], gradient, rate, decay)
        for ref, value in zip(made[3 * k : 3 * k + 3], values):
            ref[at] = value

    def begin(k):
        for copy in loads[4 + 3 * k : 7 + 3 * k]:
            copy.wait()

    def finish(k):
        for copy in stores[3 * k : 3 * k + 3]:
            copy.start()

    for k, own in ((0, own_q), (2, own_u)):
        begin(k)
        width = own.shape[3]
        for layer in range(LAYERS):
            for side in range(2):
                at = (layer, slice(None), slice(side * width, (side + 1) * width))
                update(k, at, own[layer, side].astype(F32), RATE_MATRIX, DECAY_MATRIX)
        finish(k)
    for k, rows in ((1, slice(0, out_rows)), (3, slice(out_rows, None))):
        begin(k)
        update(k, ..., own_b[:, rows].astype(F32), RATE_MATRIX, DECAY_MATRIX)
        finish(k)
    for k, width in enumerate(bias_widths):
        begin(4 + k)
        for layer in range(LAYERS):
            rows = all_v[1, layer * VEC_ROWS : (layer + 1) * VEC_ROWS, :]
            moved = pltpu.roll(rows, lax.rem(D - d * width, D), 1)
            at = (slice(layer, layer + 1), slice(None))
            update(4 + k, at, moved[5 + k : 6 + k, :width], RATE_MATRIX, 0.0)
        finish(4 + k)
    lanes = old[18].shape[2]
    features = pl.ds(pl.multiple_of(r * lanes, lanes), lanes)
    begin(6)
    for layer in range(LAYERS):
        for k in range(6):
            row = layer * VEC_ROWS + min(k, 4)
            at = (k, slice(layer, layer + 1), slice(None))
            update(6, at, all_v[0, row : row + 1, features], RATE_VECTOR, 0.0)
    finish(6)
    for copy in stores:
        copy.wait()


def update_all(n_dp, bias_widths, out_rows, passed, gradients, old):
    anywhere = pl.BlockSpec(memory_space=pl.ANY)
    given = (*gradients, *old)
    results = [jax.ShapeDtypeStruct(a.shape, F32) for a in old]
    count = len(passed)
    return pl.pallas_call(
        partial(update_kernel, n_dp, bias_widths, out_rows, count),
        out_shape=(*[jax.ShapeDtypeStruct(a.shape, a.dtype) for a in passed], *results),
        in_specs=[anywhere] * (count + len(given)),
        out_specs=(anywhere,) * (count + len(old)),
        scratch_shapes=[
            *[pltpu.VMEM(a.shape, a.dtype) for a in given],
            *[pltpu.VMEM(a.shape, F32) for a in old],
            pltpu.SemaphoreType.DMA((len(given),)),
            pltpu.SemaphoreType.DMA((count + len(old),)),
        ],
        compiler_params=pltpu.CompilerParams(vmem_limit_bytes=60 << 20),
        name="update_all",
    )(*passed, *given)


def on_device(
    hidden_in,
    cotangent,
    seq_ids,
    qkv_weight,
    qkv_first,
    qkv_second,
    out_weight,
    out_first,
    out_second,
    up_weight,
    up_first,
    up_second,
    down_weight,
    down_first,
    down_second,
    qkv_bias,
    qkv_bias_first,
    qkv_bias_second,
    up_bias,
    up_bias_first,
    up_bias_second,
    row_vectors,
    row_first,
    row_second,
):
    n_dp = lax.axis_size("dp")
    grid = GRIDS[n_dp]
    group_len = seq_ids.shape[0]
    qkv_width, up_width = qkv_weight.shape[2] // 2, up_weight.shape[2] // 2
    out_rows, down_rows = out_weight.shape[1], down_weight.shape[1]
    bias_widths = qkv_bias.shape[1], up_bias.shape[1]
    cut = out_rows + down_rows // 2
    sizes = (qkv_width, up_width, out_rows)

    ins = dict(
        hid=hidden_in,
        cot=cotangent,
        ids=seq_ids.reshape(1, group_len),
        row_vectors=row_vectors.transpose(1, 0, 2),
        qkv_bias=qkv_bias,
        up_bias=up_bias,
        qkv_weight=qkv_weight,
        out_weight=out_weight,
        up_weight=up_weight,
        down_weight=down_weight,
    )
    *passed, own_q, own_u, own_b, all_v = whole(grid, cut, sizes, bias_widths, ins)
    gradients = (own_q, own_u, own_b, all_v)
    old = (
        qkv_weight,
        qkv_first,
        qkv_second,
        out_weight,
        out_first,
        out_second,
        up_weight,
        up_first,
        up_second,
        down_weight,
        down_first,
        down_second,
        qkv_bias,
        qkv_bias_first,
        qkv_bias_second,
        up_bias,
        up_bias_first,
        up_bias_second,
        row_vectors.transpose(1, 0, 2),
        row_first.transpose(1, 0, 2),
        row_second.transpose(1, 0, 2),
    )
    *new, row_new, row_one, row_two = update_all(
        n_dp, bias_widths, out_rows, passed, gradients, old
    )
    return *new, *[a.transpose(1, 0, 2) for a in (row_new, row_one, row_two)]


def solution(mesh):
    placed = (
        P(("dp", "col"), "row"),
        P(("dp", "col"), "row"),
        P("dp"),
        P(None, ("row", "dp"), "col"),
        P(None, ("row", "dp"), "col"),
        P(None, ("row", "dp"), "col"),
        P(None, ("col", "dp"), "row"),
        P(None, ("col", "dp"), "row"),
        P(None, ("col", "dp"), "row"),
        P(None, ("row", "dp"), "col"),
        P(None, ("row", "dp"), "col"),
        P(None, ("row", "dp"), "col"),
        P(None, ("col", "dp"), "row"),
        P(None, ("col", "dp"), "row"),
        P(None, ("col", "dp"), "row"),
        P(None, ("col", "row", "dp")),
        P(None, ("col", "row", "dp")),
        P(None, ("col", "row", "dp")),
        P(None, ("col", "row", "dp")),
        P(None, ("col", "row", "dp")),
        P(None, ("col", "row", "dp")),
        P(None, None, "row"),
        P(None, None, "row"),
        P(None, None, "row"),
    )
    return jax.shard_map(
        on_device,
        mesh=mesh,
        in_specs=placed,
        out_specs=(
            P(("dp", "col"), "row"),
            P(("dp", "col"), "row"),
            P(None, ("row", "dp"), "col"),
            P(None, ("row", "dp"), "col"),
            P(None, ("row", "dp"), "col"),
            P(None, ("col", "dp"), "row"),
            P(None, ("col", "dp"), "row"),
            P(None, ("col", "dp"), "row"),
            P(None, ("row", "dp"), "col"),
            P(None, ("row", "dp"), "col"),
            P(None, ("row", "dp"), "col"),
            P(None, ("col", "dp"), "row"),
            P(None, ("col", "dp"), "row"),
            P(None, ("col", "dp"), "row"),
            P(None, ("col", "row", "dp")),
            P(None, ("col", "row", "dp")),
            P(None, ("col", "row", "dp")),
            P(None, ("col", "row", "dp")),
            P(None, ("col", "row", "dp")),
            P(None, ("col", "row", "dp")),
            P(None, None, "row"),
            P(None, None, "row"),
            P(None, None, "row"),
        ),
        check_vma=False,
    )
```

```python
import math
from functools import partial
from types import SimpleNamespace

import jax
import jax.numpy as jnp
from jax import lax
from jax.experimental import pallas as pl
from jax.experimental.pallas import tpu as pltpu
from jax.sharding import PartitionSpec as P

D = 1024
HEAD = 64
ROT = 16
LAYERS = 2
SEQS = 3
STEP = 10


EPS_NORM = 1e-05
EPS_ADAM = 1e-08
BETA_ONE = 0.9
BETA_TWO = 0.95
RATE_MATRIX = 0.06
RATE_VECTOR = 0.6
DECAY_MATRIX = 0.01
ROPE_BASE = 10000.0
MASK_VALUE = -1e30
CONTRACT_ROWS = (((0,), (0,)), ((), ()))
CONTRACT_COLS = (((1,), (1,)), ((), ()))

BF = jnp.bfloat16
F32 = jnp.float32
MESH = pl.DeviceIdType.MESH
GRIDS = {32: (4, 4, 2), 8: (2, 2, 2)}
VEC_ROWS = 8
VMEM_SPEC = pl.BlockSpec(memory_space=pltpu.VMEM)


def params(collective_id, mib):
    return pltpu.CompilerParams(
        collective_id=collective_id, has_side_effects=True, vmem_limit_bytes=mib << 20
    )


def remote(src, dst, sends, recvs, at, device):
    return pltpu.make_async_remote_copy(
        src_ref=src,
        dst_ref=dst,
        send_sem=sends.at[at],
        recv_sem=recvs.at[at],
        device_id=device,
        device_id_type=MESH,
    )


def greet(device):
    pl.semaphore_signal(
        pltpu.get_barrier_semaphore(), inc=1, device_id=device, device_id_type=MESH
    )


def greeted(count):
    pl.semaphore_wait(pltpu.get_barrier_semaphore(), count)


def group_place():
    return lax.axis_index("row") * 2 + lax.axis_index("col")


def group_peer(place, step):
    other = lax.rem(place + step, 4)
    return {"row": other // 2, "col": lax.rem(other, 2)}


def over(lengths, body):
    total = math.prod(lengths)

    def one(index, carry):
        place, rest = [], index
        for length in reversed(lengths):
            place.append(lax.rem(rest, length))
            rest = rest // length
        body(*reversed(place))
        return carry

    lax.fori_loop(0, total, one, 0)


def adamw(master, moment_one, moment_two, gradient, step_rate, step_decay):
    one_new = BETA_ONE * moment_one + (1.0 - BETA_ONE) * gradient
    two_new = BETA_TWO * moment_two + (1.0 - BETA_TWO) * gradient * gradient
    one_hat = one_new / (1.0 - BETA_ONE**STEP)
    two_hat = two_new / (1.0 - BETA_TWO**STEP)
    master_new = master - step_rate * (
        one_hat / (jnp.sqrt(two_hat) + EPS_ADAM) + step_decay * master
    )
    return (master_new, one_new, two_new)


class Copies:
    def __init__(self, sends, recvs):
        self.sends, self.recvs, self.count = sends, recvs, 0

    def to(self, src, dst, device):
        copy = remote(src, dst, self.sends, self.recvs, self.count, device)
        self.count += 1
        return copy


class Ring:
    def __init__(self, length, place, device_at):
        self.length, self.place, self.device_at = length, place, device_at
        self.ways = ((0, 1), (1, -1)) if length > 2 else ((0, 1),)

    def at(self, step):
        return lax.rem(self.place + step + self.length, self.length)

    def device(self, step):
        return self.device_at(self.at(step))


class RingGather:
    def __init__(self, copies, ring, views, sources=None, arrived=None):
        self.copies, self.ring, self.views = copies, ring, views
        self.sources, self.arrived = sources, arrived
        self.near, self.far = [[], []], [[], []]

    def start(self):
        for way, step in self.ring.ways:
            for k, view in enumerate(self.views):
                own = view(self.ring.place, None)
                src = self.sources[k] if self.sources else own
                copy = self.copies.to(src, own, self.ring.device(step))
                copy.start()
                self.near[way].append(copy)

    def middle(self):
        for way, step in self.ring.ways:
            for copy in self.near[way]:
                copy.wait_recv()
            came_from = self.ring.at(-step)
            if self.ring.length > 2:
                for view in self.views:
                    ref = view(came_from, way)
                    if ref is not None:
                        copy = self.copies.to(ref, ref, self.ring.device(step))
                        copy.start()
                        self.far[way].append(copy)
            if self.arrived:
                self.arrived(came_from)

    def end(self):
        for copy in self.far[0] + self.far[1]:
            copy.wait_recv()
        if self.arrived and self.ring.length > 2:
            self.arrived(self.ring.at(2))

    def finish(self):
        for copy in self.near[0] + self.near[1] + self.far[0] + self.far[1]:
            copy.wait_send()


class DirectGather:
    def __init__(self, copies, ring, views, sources):
        self.copies, self.ring, self.views, self.sources = copies, ring, views, sources
        self.sent = []

    def start(self):
        for step in range(1, self.ring.length):
            for view, source in zip(self.views, self.sources):
                own = view(self.ring.place, None)
                copy = self.copies.to(source, own, self.ring.device(step))
                copy.start()
                self.sent.append(copy)

    def end(self):
        for copy in self.sent:
            copy.wait_recv()

    def finish(self):
        for copy in self.sent:
            copy.wait_send()


class Summand:
    def __init__(self, ref, index, count, width, near, far):
        self.ref, self.index, self.count, self.width = ref, index, count, width
        self.near, self.far = near, far

    def view(self, target, start, width):
        return self.ref.at[self.index(slice(None), target, start, width)]

    def add(self, target, start, width, other):
        def one(lead):
            at = self.index(lead, target, start, width)
            more = other[...] if self.count is None else other[lead]
            self.ref[at] = self.ref[at] + more

        if self.count is None:
            one(None)
        else:
            over((self.count,), one)

    def total(self, lead, target, ways):
        value = self.ref[self.index(lead, target, 0, self.width)].astype(F32)
        for way in range(ways):
            more = self.far[way][...] if self.count is None else self.far[way][lead]
            value = value + more.astype(F32)
        return value


class RingSum:
    def __init__(self, copies, ring, summands):
        self.copies, self.ring, self.summands = copies, ring, summands
        self.near, self.far = [[], []], [[], []]

    def start(self):
        if self.ring.length == 2:
            return
        for way, step in self.ring.ways:
            for s in self.summands:
                half = s.width // 2
                copy = self.copies.to(
                    s.view(self.ring.at(2), way * half, half), s.near[way], self.ring.device(step)
                )
                copy.start()
                self.near[way].append(copy)

    def middle(self):
        for way, step in self.ring.ways:
            target = self.ring.at(step)
            for k, s in enumerate(self.summands):
                if self.ring.length > 2:
                    self.near[way][k].wait_recv()
                    s.add(target, way * (s.width // 2), s.width // 2, s.near[way])
                copy = self.copies.to(
                    s.view(target, 0, s.width), s.far[way], self.ring.device(step)
                )
                copy.start()
                self.far[way].append(copy)

    def end(self):
        for copy in self.far[0] + self.far[1]:
            copy.wait_recv()

    def total(self, k, lead=None):
        return self.summands[k].total(lead, self.ring.place, len(self.ring.ways))

    def finish(self):
        for copy in self.near[0] + self.near[1] + self.far[0] + self.far[1]:
            copy.wait_send()


class DirectSum:
    def __init__(self, copies, ring, summand):
        self.copies, self.ring, self.summand = copies, ring, summand
        self.sent = []

    def start(self):
        for step in range(1, self.ring.length):
            copy = self.copies.to(
                self.summand.view(self.ring.at(step), 0, self.summand.width),
                self.summand.far[step - 1],
                self.ring.device(step),
            )
            copy.start()
            self.sent.append(copy)

    def end(self):
        for copy in self.sent:
            copy.wait_recv()

    def total(self):
        return self.summand.total(None, self.ring.place, self.ring.length - 1)

    def finish(self):
        for copy in self.sent:
            copy.wait_send()


def lanes_at(start, width):
    if not isinstance(start, int):
        start = pl.multiple_of(start, 128)
    return pl.ds(start, width)


class Slice:
    def __init__(self, grid):
        self.grid = grid
        nz, nx, nc = grid
        d = lax.axis_index("dp")
        self.d, self.z, self.x, self.core = d, d // (nx * nc), lax.rem(d // nc, nx), lax.rem(d, nc)
        self.row, self.col = lax.axis_index("row"), lax.axis_index("col")
        self.half = nz * nx * nc // 2
        self.place = group_place()
        self.zls = nz // 2
        self.partner = self.dp(self.z, self.x, 1 - self.core)
        self.z_ring = Ring(nz, self.z, lambda z: self.dp(z, self.x, self.core))
        self.x_ring = Ring(nx, self.x, lambda x: self.dp(self.z, x, self.core))
        self.y_ring = Ring(4, self.place, lambda q: {"row": q // 2, "col": lax.rem(q, 2)})

    def dp(self, z, x, core):
        _, nx, nc = self.grid
        return {"dp": (z * nx + x) * nc + core}

    def greet_rings(self, rings, whole=False):
        count = 0
        for ring in rings:
            steps = range(1, ring.length) if whole else [step for _, step in ring.ways]
            for step in steps:
                greet(ring.device(step))
                count += 1
        return count


class WeightGather:
    def __init__(self, here, cut, copies, local, own, full, spread):
        self.here, self.copies, self.core_copies = here, copies, []
        rows, lanes = own.shape
        pair = full.shape[-1] != lanes
        first = cut if pair else rows // 2
        cuts = (pl.ds(0, first), pl.ds(first, rows - first))
        z, x, core, zls = here.z, here.x, here.core, here.zls

        def part(width, half):
            return (0, width) if half is None else (half * (width // 2), width // 2)

        def chunk(order, along, half):
            zz, xx = (along, x) if order == 0 else (z, along)
            start, width = part(lanes, half)
            if pair:
                at = lanes_at((zz // zls) * lanes + start, width)
                return full.at[lax.rem(zz, zls), xx, core, cuts[order], at]
            return full.at[zz, xx, core, cuts[order], pl.ds(start, width)]

        def line(order, along, half):
            if order == 0:
                at = pl.ds(*part(full.shape[-1], half))
                return full.at[:, along, core, cuts[0], at]
            start, width = part(lanes, half)
            if pair:
                at = lanes_at((along // zls) * lanes + start, width)
                return full.at[lax.rem(along, zls), :, core, cuts[1], at]
            return full.at[along, :, core, cuts[1], pl.ds(start, width)]

        def small(order, along, half):
            return None if half == 1 else spread[1].at[along, x, core]

        def small_line(order, along, half):
            return None if half == 1 else spread[1].at[:, along, core]

        rings = ((here.z_ring, here.x_ring), (here.x_ring, here.z_ring))
        self.first, self.second, self.lines, self.own = [], [], [], []
        for order in range(2):
            sources = [own.at[cuts[order]]]
            chunks, lines = [partial(chunk, order)], [partial(line, order)]
            if order == 0 and spread:
                sources.append(spread[0])
                chunks.append(partial(small, order))
                lines.append(partial(small_line, order))
            for k, view in enumerate(chunks):
                self.own.append(
                    pltpu.make_async_copy(
                        sources[k], view(rings[order][0].place, None), local.at[order * 2 + k]
                    )
                )
            self.first.append(DirectGather(copies, rings[order][0], chunks, sources))
            self.second.append(
                RingGather(copies, rings[order][1], lines, None, partial(self.forward, order))
            )
            self.lines.append(lines)

    def forward(self, order, along):
        for view in self.lines[order]:
            ref = view(along, None)
            copy = self.copies.to(ref, ref, self.here.partner)
            copy.start()
            self.core_copies.append(copy)

    def start(self):
        for ring in self.first:
            ring.start()
        for copy in self.own:
            copy.start()

    def turn(self):
        for copy in self.own:
            copy.wait()
        for order in range(2):
            self.first[order].end()
            self.second[order].start()
            self.forward(order, self.second[order].ring.place)

    def second_middle(self):
        for ring in self.second:
            ring.middle()

    def end(self):
        for ring in self.second:
            ring.end()

    def arrive(self):
        for copy in self.core_copies:
            copy.wait_recv()

    def finish(self):
        for ring in self.first + self.second:
            ring.finish()
        for copy in self.core_copies:
            copy.wait_send()


def dot(left, right):
    return jnp.dot(left, right, preferred_element_type=F32)


def dot_rows(left, right):
    return lax.dot_general(left, right, CONTRACT_ROWS, preferred_element_type=F32)


def dot_cols(left, right):
    return lax.dot_general(left, right, CONTRACT_COLS, preferred_element_type=F32)


def norm_stats(state):
    width = state.shape[1]
    average = jnp.sum(state, 1, keepdims=True) / width
    spread = jnp.sum(state * state, 1, keepdims=True) / width - average * average
    inv_std = lax.rsqrt(spread + EPS_NORM)
    return ((state - average) * inv_std, inv_std)


def norm_back(grad_hat, hat):
    width = hat.shape[1]
    first = jnp.sum(grad_hat, 1, keepdims=True) / width
    second = jnp.sum(grad_hat * hat, 1, keepdims=True) / width
    return grad_hat - first - hat * second


class Layer:
    def __init__(self, layer, vec, tables, mask, bias, full_q, full_u, full_b, sizes):
        self.vec, self.tables, self.mask, self.bias = vec, tables, mask, bias
        self.layer, self.full_q, self.full_u, self.full_b = layer, full_q, full_u, full_b
        self.qkv_width, self.up_width, self.out_rows = sizes
        self.heads_here = self.qkv_width // (3 * HEAD)

    def vector(self, k):
        at = self.layer * VEC_ROWS + k
        return self.vec[at : at + 1, :]

    def q_matrix(self, start, width):
        return self.full_q[:, :, :, :, start : start + width].reshape(-1, width)

    def u_matrix(self, start, width):
        return self.full_u[:, :, :, :, start : start + width].reshape(-1, width)

    def b_matrix(self, low, high, start, width):
        value = self.full_b[:, :, :, low:high, start : start + width]
        return value.reshape(-1, width)

    def out_matrix(self, start, width):
        return self.b_matrix(0, self.out_rows, start, width)

    def down_matrix(self, start, width):
        return self.b_matrix(self.out_rows, self.full_b.shape[3], start, width)

    def inputs(self, hat, attn_in, mlp_in):
        attn_in[...] = (hat * self.vector(0) + self.vector(1)).astype(BF)
        mlp_in[...] = (hat * self.vector(2) + self.vector(3)).astype(BF)

    def project(self, attn_in, joined):
        pair = 6 * HEAD
        cosine, left, right = self.tables
        for start in range(0, self.qkv_width, pair):
            value = dot(attn_in[...], self.q_matrix(start, pair))
            value = value + self.bias[0:1, start : start + pair]
            value = (
                value * cosine[...]
                + pltpu.roll(value, pair - ROT // 2, 1) * left[...]
                + pltpu.roll(value, ROT // 2, 1) * right[...]
            )
            joined[:, start : start + pair] = value.astype(BF)

    def head(self, joined, h):
        start = h * 3 * HEAD
        return [joined[:, start + k * HEAD : start + (k + 1) * HEAD] for k in range(3)]

    def attend(self, joined, probs, heads):
        for h in range(self.heads_here):
            query, key_rows, value_rows = self.head(joined, h)
            scores = dot_cols(query, key_rows) * HEAD**-0.5 + self.mask[...]
            expo = jnp.exp(scores - jnp.max(scores, 1, keepdims=True))
            low = (expo / jnp.sum(expo, 1, keepdims=True)).astype(BF)
            probs[h] = low
            heads[:, h * HEAD : (h + 1) * HEAD] = dot(low, value_rows).astype(BF)

    def units(self, mlp_in, slope, units):
        width = 256
        for start in range(0, self.up_width, width):
            at = slice(start, start + width)
            value = dot(mlp_in[...], self.u_matrix(start, width))
            value = value + self.bias[1:2, at]
            below = 0.5 * (1.0 + lax.erf(value * 0.5**0.5))
            density = jnp.exp(value * value * -0.5) * ((2.0 * math.pi) ** -0.5)
            units[:, at] = (value * below).astype(BF)
            slope[:, at] = (below + value * density).astype(BF)

    def outputs(self, heads, units, start, width):
        return dot(heads[...], self.out_matrix(start, width)) + dot(
            units[...], self.down_matrix(start, width)
        )

    def branch_back(self, grad, slope, grad_heads, grad_pre):
        grad_heads[...] = dot_cols(grad[...], self.out_matrix(0, D)).astype(BF)
        zls = self.full_b.shape[0]
        width = self.up_width // zls
        step = min(width, 256)
        for zl in range(zls):
            matrix = self.full_b[zl, :, :, self.out_rows :, :].reshape(-1, D)
            for start in range(0, width, step):
                at = slice(zl * width + start, zl * width + start + step)
                pull = dot_cols(grad[...], matrix[start : start + step])
                grad_pre[:, at] = (pull * slope[:, at].astype(F32)).astype(BF)

    def attend_back(self, joined, probs, grad_heads, raw, grad_joined):
        for h in range(self.heads_here):
            query, key_rows, value_rows = self.head(joined, h)
            grad = grad_heads[:, h * HEAD : (h + 1) * HEAD]
            low = probs[h]
            high = low.astype(F32)
            grad_probs = dot_cols(grad, value_rows)
            inner = jnp.sum(grad_probs * high, 1, keepdims=True)
            grad_raw = (high * (grad_probs - inner) * HEAD**-0.5).astype(BF)
            start = h * 3 * HEAD
            raw[:, start : start + HEAD] = dot(grad_raw, key_rows)
            raw[:, start + HEAD : start + 2 * HEAD] = dot_rows(grad_raw, query)
            raw[:, start + 2 * HEAD : start + 3 * HEAD] = dot_rows(low, grad)
        pair = 6 * HEAD
        cosine, left, right = self.tables
        for start in range(0, self.qkv_width, pair):
            value = raw[:, start : start + pair]
            value = (
                value * cosine[...]
                + pltpu.roll(value * left[...], ROT // 2, 1)
                + pltpu.roll(value * right[...], pair - ROT // 2, 1)
            )
            grad_joined[:, start : start + pair] = value.astype(BF)

    def inputs_back(self, grad_joined, grad_pre, hat, grad, sums):
        grad_attn_in = dot_cols(grad_joined[...], self.q_matrix(0, self.qkv_width))
        rows = [
            jnp.sum(grad_attn_in * hat, 0, keepdims=True),
            jnp.sum(grad_attn_in, 0, keepdims=True),
        ]
        grad_hat = grad_attn_in * self.vector(0)
        grad_mlp_in = dot_cols(grad_pre[...], self.u_matrix(0, self.up_width))
        rows += [
            jnp.sum(grad_mlp_in * hat, 0, keepdims=True),
            jnp.sum(grad_mlp_in, 0, keepdims=True),
            jnp.sum(grad[...].astype(F32), 0, keepdims=True) * 0.25,
        ]
        for k, row in enumerate(rows):
            sums[k : k + 1, :] = row
        for k, (ref, width) in enumerate(
            ((grad_joined, self.qkv_width), (grad_pre, self.up_width))
        ):
            sums[5 + k : 6 + k, :] = jnp.zeros((1, D), F32)
            sums[5 + k : 6 + k, :width] = jnp.sum(ref[...].astype(F32), 0, keepdims=True)
        sums[7:8, :] = jnp.zeros((1, D), F32)
        return norm_back(grad_hat + grad_mlp_in * self.vector(2), hat)


def grads_a(left, right, out):
    width = right.shape[1]
    nz = out.shape[0]
    block = left.shape[1] // nz
    for k in range(nz):
        value = dot_rows(left[:, k * block : (k + 1) * block], right[...]).astype(BF)
        out[k] = value.reshape(*out.shape[1:4], width)


def grads_b(left, right, out, low, high):
    zls = out.shape[0]
    block = left.shape[1] // zls
    for k in range(zls):
        value = dot_rows(left[:, k * block : (k + 1) * block], right[...]).astype(BF)
        out[k, :, :, low:high, :] = value.reshape(*out.shape[1:3], high - low, D)


def rows_index(rows):
    def index(lead, target, start, width):
        return (
            pl.ds(pl.multiple_of(target * rows, rows), rows),
            lanes_at(start, width),
        )

    return index


def blocks_index(rows, lanes):
    def index(lead, target, start, width):
        return (
            pl.ds(pl.multiple_of(lax.rem(target, 2) * rows, rows), rows),
            lanes_at((target // 2) * lanes + start, width),
        )

    return index


def group_sum(here, copies, part, index, width, near, far):
    summand = Summand(part, index, None, width, (near.at[0], near.at[1]), (far.at[0], far.at[1]))
    return RingSum(copies, here.y_ring, [summand])


def group_gather(here, copies, whole, rows):
    def view(target, half):
        width = whole.shape[1]
        start, width = (0, width) if half is None else (half * (width // 2), width // 2)
        return whole.at[pl.ds(pl.multiple_of(target * rows, rows), rows), pl.ds(start, width)]

    return RingGather(copies, here.y_ring, [view])


def own_rows(here, rows):
    return pl.ds(pl.multiple_of(here.place * rows, rows), rows)


def ring_scratch(rows, width):
    return [pltpu.VMEM((2, rows, width // 2), BF), pltpu.VMEM((2, rows, width), BF)]


class GradSum:
    def __init__(self, here, cut, copies, kind, g, s, buffers):
        self.here, self.copies, self.kind, self.g, self.s = here, copies, kind, g, s
        self.near, self.far, self.mid, self.top, self.fin = buffers
        rows = g.shape[3]
        first = rows // 2 if kind == "a" else cut
        self.cuts = (pl.ds(0, first), pl.ds(first, rows - first))
        self.full = g.shape[4]
        self.lanes = self.full // 2
        self.lines, self.turns = [None, None], [None, None]

    def start(self):
        self.core = []
        for order in range(2):
            copy = self.copies.to(
                self.g.at[:, :, 1 - self.here.core, self.cuts[order]],
                self.s.at[:, :, self.cuts[order]],
                self.here.partner,
            )
            copy.start()
            self.core.append(copy)

    def line(self, order):
        here, at, zls = self.here, self.cuts[order], self.here.zls
        self.core[order].wait_recv()

        for zz in range(self.s.shape[0]):
            self.s[zz, :, at] = self.s[zz, :, at] + self.g[zz, :, here.core, at]
        nx = self.s.shape[1]
        if order == 0:
            ring, count, width = here.x_ring, self.s.shape[0], self.full

            def index(lead, target, start, width):
                return (lead, target, at, lanes_at(start, width))

        elif self.kind == "a":
            ring, count, width = here.z_ring, nx, self.full

            def index(lead, target, start, width):
                return (target, lead, at, lanes_at(start, width))

        else:
            ring, count, width = here.z_ring, nx, self.lanes

            def index(lead, target, start, width):
                return (
                    lax.rem(target, zls),
                    lead,
                    at,
                    lanes_at((target // zls) * self.lanes + start, width),
                )

        summand = Summand(
            self.s,
            index,
            count,
            width,
            (self.near[order].at[0], self.near[order].at[1]),
            (self.far[order].at[0], self.far[order].at[1]),
        )
        self.lines[order] = RingSum(self.copies, ring, [summand])
        self.lines[order].start()

    def line_middle(self, order):
        self.lines[order].middle()

    def turn(self, order):
        here, zls, mid = self.here, self.here.zls, self.mid[order]
        line = self.lines[order]
        line.end()

        def put(lead):
            mid[lead] = line.total(0, lead).astype(BF)

        over(mid.shape[:1], put)
        ring = here.z_ring if order == 0 else here.x_ring
        if self.kind == "b" and order == 0:

            def index(lead, target, start, width):
                return (
                    lax.rem(target, zls),
                    slice(None),
                    lanes_at((target // zls) * self.lanes + start, width),
                )

        else:

            def index(lead, target, start, width):
                return (target, slice(None), lanes_at(start, width))

        summand = Summand(
            mid,
            index,
            None,
            self.full if self.kind == "a" else self.lanes,
            None,
            [self.top[order].at[k] for k in range(ring.length - 1)],
        )
        self.turns[order] = DirectSum(self.copies, ring, summand)
        self.turns[order].start()

    def end(self, order):
        self.turns[order].end()
        value = self.turns[order].total().astype(BF)
        if self.kind == "a":
            self.fin[order] = value
        else:
            self.fin[self.cuts[order]] = value

    def finish(self):
        for copy in self.core:
            copy.wait_send()
        for order in range(2):
            self.lines[order].finish()
            self.turns[order].finish()


def grad_buffers(grid, cut, g_shape, kind):
    nz, nx, _ = grid
    rows, full = g_shape[3:]
    zls = g_shape[0]
    first = rows // 2 if kind == "a" else cut
    lanes = full if kind == "a" else full // 2
    cuts = (first, rows - first)

    def low(*dims):
        return pltpu.VMEM(dims, BF)

    counts = (zls, nx)
    widths = (full, lanes)
    fin = low(2, first, full) if kind == "a" else low(rows, lanes)
    return [
        low(zls, nx, rows, full),
        *[low(2, counts[o], cuts[o], widths[o] // 2) for o in range(2)],
        *[low(2, counts[o], cuts[o], widths[o]) for o in range(2)],
        *[low(counts[o], cuts[o], widths[o]) for o in range(2)],
        *[low((nz, nx)[o] - 1, cuts[o], lanes) for o in range(2)],
        fin,
    ]


def grad_sum(here, cut, copies, kind, g, refs):
    s, near0, near1, far0, far1, mid0, mid1, top0, top1, fin = refs
    return GradSum(
        here,
        cut,
        copies,
        kind,
        g,
        s,
        ((near0, near1), (far0, far1), (mid0, mid1), (top0, top1), fin),
    )


def lane_iota(rows, lanes):
    return lax.broadcasted_iota(jnp.int32, (rows, lanes), 1)


def make_tables(ids, live, cosine, left, right, mask):
    length = ids.shape[1]
    other = ids[...]
    row = lax.broadcasted_iota(jnp.int32, (length, length), 0)
    column = lax.broadcasted_iota(jnp.int32, (length, length), 1)
    other = jnp.broadcast_to(other.astype(F32), (length, length))
    own = jnp.sum(jnp.where(row == column, other, 0.0), 1, keepdims=True)
    live[...] = jnp.broadcast_to(jnp.where(own < SEQS, 1.0, 0.0), live.shape)
    earlier = jnp.sum((other < own).astype(F32), 1, keepdims=True)
    mask[...] = jnp.where((other == own) & (column <= row), 0.0, MASK_VALUE)
    place = lax.broadcasted_iota(jnp.int32, (length, 1), 0).astype(F32) - earlier
    lane = lane_iota(1, 128)
    at = lax.rem(lane, HEAD)
    turned = at < ROT
    power = lax.rem(at, ROT // 2).astype(F32)
    frequency = jnp.exp(power * (-2.0 / ROT * math.log(ROPE_BASE)))
    angles = place * frequency
    cos_part = jnp.where(turned, jnp.cos(angles), 1.0)
    sin_part = jnp.sin(angles)
    left_part = jnp.where(at < ROT // 2, -sin_part, 0.0)
    right_part = jnp.where(turned & (at >= ROT // 2), sin_part, 0.0)
    low_half = lane < HEAD
    for ref, value, rest in ((cosine, cos_part, 1.0), (left, left_part, 0.0), (right, right_part, 0.0)):
        ref[:, 0:128] = value
        ref[:, 128:256] = jnp.where(low_half, rest, value)
        ref[:, 256:384] = jnp.where(low_half, value, rest)


def make_biases(full_c, bias, widths):
    n_dp = math.prod(full_c.shape[:3])
    table = full_c[...].reshape(n_dp, *full_c.shape[3:])
    lanes = full_c.shape[4]
    for layer in range(LAYERS):
        values = table[:, layer, :].astype(BF)
        first = 0
        for k, width in enumerate(widths):
            total = n_dp * width
            lane = lax.broadcasted_iota(jnp.int32, (lanes, total), 0)
            column = lax.broadcasted_iota(jnp.int32, (lanes, total), 1)
            pick = jnp.where(lane == lax.rem(column, width) + first, 1.0, 0.0).astype(BF)
            spread = dot(values, pick)
            device = lax.broadcasted_iota(jnp.int32, (n_dp, total), 0)
            column = lax.broadcasted_iota(jnp.int32, (n_dp, total), 1)
            mine = jnp.where(column // width == device, spread, 0.0)
            bias[layer * 2 + k : layer * 2 + k + 1, :total] = jnp.sum(mine, 0, keepdims=True)
            first += width


def whole_kernel(grid, cut, sizes, widths, tree, *refs):
    at = SimpleNamespace(**jax.tree.unflatten(tree, refs))
    sends, recvs, local = at.sends, at.recvs, at.local
    here = Slice(grid)
    nz, nx, _ = grid
    copies = Copies(sends, recvs)
    copies.count = 48
    d, r, c, half = here.d, here.row, here.col, here.half
    hid, cot = at.hid, at.cot
    hid_all, cot_all, vec = at.hid_all, at.cot_all, at.vec
    rows, lanes = hid.shape
    quarter = rows // 2
    dh, dl = d // half, lax.rem(d, half)
    swap_needed = dh != r
    swap_to = {"dp": r * half + dl, "row": dh}
    slot_rows = at.qkv_weight.shape[1]
    forth = [{"dp": r * half + d // 2, "row": k} for k in range(2)]
    back_to = [{"dp": 2 * dl + k, "row": dh} for k in range(2)]
    forth_self = [(r == k) & (r * half + d // 2 == d) for k in range(2)]
    back_self = [(dh == r) & (2 * dl + k == d) for k in range(2)]
    slot = lax.rem(d, 2)

    count = here.greet_rings([here.z_ring, here.x_ring, here.y_ring], whole=True)
    greet(here.partner)
    for k in range(2):
        for device, itself in ((forth[k], forth_self[k]), (back_to[k], back_self[k])):

            @pl.when(jnp.logical_not(itself))
            def _():
                greet(device)

    @pl.when(swap_needed)
    def _():
        greet(swap_to)

    qkv_width, up_width, out_rows = sizes
    wa, wb = (at.wq, at.wu), at.wb

    def cast(layer):
        for ref, given, width in ((wa[0], at.qkv_weight, qkv_width), (wa[1], at.up_weight, up_width)):
            for k in range(2):
                ref[layer, k] = given[layer, :, k * width : (k + 1) * width].astype(BF)
        wb[layer, :out_rows] = at.out_weight[layer].astype(BF)
        wb[layer, out_rows:] = at.down_weight[layer].astype(BF)

    cast(0)
    vec_own, wc = at.vec_own, at.wc
    vec_own[...] = jnp.zeros(vec_own.shape, F32)
    for layer in range(LAYERS):
        for k in range(6):
            row = layer * VEC_ROWS + k
            vec_own[row : row + 1] = at.row_vectors[k, layer : layer + 1]
    wc[...] = jnp.zeros(wc.shape, F32)
    wc[:LAYERS, : widths[0]] = at.qkv_bias[...]
    wc[:LAYERS, widths[0] : sum(widths)] = at.up_bias[...]
    greeted(
        count
        + 5
        + swap_needed.astype(jnp.int32)
        - sum(k.astype(jnp.int32) for k in forth_self + back_self)
    )

    def when_else(condition, there, here_do):
        pl.when(condition)(there)
        pl.when(jnp.logical_not(condition))(here_do)

    def pair(src, dst, send, recv, device):
        return pltpu.make_async_remote_copy(
            src_ref=src,
            dst_ref=dst,
            send_sem=sends.at[send],
            recv_sem=recvs.at[recv],
            device_id=device,
            device_id_type=MESH,
        )

    a_own, b_own = (at.q_own, at.u_own), at.b_own
    slot_at = pl.ds(pl.multiple_of(slot * slot_rows, slot_rows), slot_rows)

    def a_copy(layer, kind, k):
        base = layer * 8 + kind * 2
        return pair(
            wa[kind].at[layer, k], a_own[kind].at[layer, slot_at], base + k, base + slot, forth[k]
        )

    def a_arrival(layer, kind, k):
        base = layer * 8 + kind * 2
        into = a_own[kind].at[layer, pl.ds(k * slot_rows, slot_rows)]
        return pair(wa[kind].at[layer, 0], into, base, base + k, back_to[k])

    def a_local(layer, kind, k):
        return pltpu.make_async_copy(
            wa[kind].at[layer, k], a_own[kind].at[layer, slot_at], local.at[24 + layer * 2 + kind]
        )

    def swap_copy(layer):
        return pair(wb.at[layer], b_own.at[layer], layer * 8 + 4, layer * 8 + 4, swap_to)

    def swap_local(layer):
        return pltpu.make_async_copy(wb.at[layer], b_own.at[layer], local.at[28 + layer])

    def begin(layer):
        for kind in range(2):
            for k in range(2):
                when_else(
                    forth_self[k],
                    lambda: a_local(layer, kind, k).start(),
                    lambda: a_copy(layer, kind, k).start(),
                )
        when_else(
            swap_needed, lambda: swap_copy(layer).start(), lambda: swap_local(layer).start()
        )

    def complete_a(layer, kind):
        for k in range(2):
            when_else(
                forth_self[k],
                lambda: a_local(layer, kind, k).wait(),
                lambda: a_copy(layer, kind, k).wait_send(),
            )

            @pl.when(jnp.logical_not(back_self[k]))
            def _():
                a_arrival(layer, kind, k).wait_recv()

    def complete_b(layer):
        when_else(swap_needed, lambda: swap_copy(layer).wait(), lambda: swap_local(layer).wait())

    begin(0)
    tokens = pl.ds(pl.multiple_of(c * rows, rows), rows)
    features = pl.ds(pl.multiple_of(r * lanes, lanes), lanes)
    hid_copies = [
        copies.to(hid, hid_all.at[tokens, features], here.y_ring.device(k)) for k in range(1, 4)
    ]
    cot_copies = [
        copies.to(cot, cot_all.at[tokens, features], here.y_ring.device(k)) for k in range(1, 4)
    ]
    hid_copies.append(copies.to(vec_own, vec.at[:, features], {"row": 1 - r}))
    own = [
        pltpu.make_async_copy(hid, hid_all.at[tokens, features], local.at[36]),
        pltpu.make_async_copy(cot, cot_all.at[tokens, features], local.at[37]),
        pltpu.make_async_copy(vec_own, vec.at[:, features], local.at[38]),
    ]
    for copy in hid_copies + own:
        copy.start()
    tables, mask, bias = (at.cosine, at.left, at.right), at.mask, at.bias
    complete_a(0, 0)

    full = ((at.q_zero, at.u_zero, at.b_zero), (at.q_one, at.u_one, at.b_one))
    full_c = at.full_c
    gathers = []
    for k in range(LAYERS):
        for kind in range(3):
            source = (a_own + (b_own,))[kind].at[k]
            spread = (wc, full_c) if k == 0 and kind == 0 else None
            count = 4 * (3 * k + kind)
            gathers.append(
                WeightGather(
                    here, cut, copies, local.at[pl.ds(count, 4)], source, full[k][kind], spread
                )
            )
    near, late = gathers[:3], gathers[3:]
    near[0].start()
    complete_a(0, 1)
    near[1].start()
    complete_b(0)
    near[2].start()
    make_tables(at.ids, at.live, *tables, mask)
    layers = [
        Layer(k, vec, tables, mask, bias.at[pl.ds(2 * k, 2)], *full[k], sizes)
        for k in range(LAYERS)
    ]
    attn_in, mlp_in, joined, probs = at.attn_in, at.mlp_in, at.joined, at.probs
    heads, slope, units = at.heads, at.slope, at.units
    for one in near:
        one.turn()
    for copy in hid_copies + own:
        copy.wait()
    near[0].second_middle()
    hat, _ = norm_stats(hid_all[...].astype(F32))
    layers[0].inputs(hat, attn_in[0], mlp_in[0])
    near[1].second_middle()
    near[2].second_middle()
    cast(1)
    begin(1)
    for one in near:
        one.end()
    near[0].arrive()
    make_biases(full_c, bias, widths)
    layers[0].project(attn_in[0], joined[0])
    complete_a(1, 0)
    late[0].start()
    complete_a(1, 1)
    late[1].start()
    complete_b(1)
    late[2].start()
    for copy in cot_copies:
        copy.start()
    mine = own_rows(here, quarter)
    layers[0].attend(joined[0], probs[0], heads[0])
    for one in late:
        one.turn()
    near[1].arrive()
    layers[0].units(mlp_in[0], slope[0], units[0])
    near[2].arrive()
    part = at.part[0]
    for start in (0, D // 2):
        part[:, start : start + D // 2] = (
            layers[0].outputs(heads[0], units[0], start, D // 2).astype(BF)
        )
    summed = group_sum(here, copies, part, rows_index(quarter), D, at.near[0], at.far[0])
    summed.start()
    late[0].second_middle()
    summed.middle()
    late[1].second_middle()
    state = hid_all[mine, :].astype(F32) + layers[0].vector(4) + layers[0].vector(5)
    summed.end()
    state = state + summed.total(0)
    at.state[...] = state
    hat, inverse = norm_stats(state)
    inv_std, hat_all = at.inv_std, at.hat_all
    inv_std[...] = jnp.broadcast_to(inverse, inv_std.shape)
    hat_all[mine, :] = hat.astype(BF)
    spread = group_gather(here, copies, hat_all, quarter)
    spread.start()
    grad = (at.grad[0], at.grad[1])
    for copy in cot_copies:
        copy.wait()
    grad[1][...] = (
        cot_all[...].astype(F32) * at.live[:, :1]
    ).astype(BF)
    late[2].second_middle()
    spread.middle()
    for one in late:
        one.end()
    spread.end()
    late[0].arrive()
    rings = [summed, spread]

    grads = [
        full[1],
        (at.gq, at.gu, at.gb),
    ]
    sum_q, sum_u, sum_b = [
        [
            grad_sum(
                here,
                cut,
                copies,
                "aab"[kind],
                grads[k][kind],
                at.sum_buffers[k][kind],
            )
            for k in range(LAYERS)
        ]
        for kind in range(3)
    ]
    out_q, out_u, out_b = at.out_q, at.out_u, at.out_b

    def owner_copy(layer, kind, order):
        out, one = ((out_q, sum_q), (out_u, sum_u))[kind]
        base = 16 + layer * 8 + kind * 2
        return pair(
            one[layer].fin.at[order], out.at[layer, r], base + order, base + r, back_to[order]
        )

    def owner_arrival(layer, kind, k):
        out, one = ((out_q, sum_q), (out_u, sum_u))[kind]
        base = 16 + layer * 8 + kind * 2
        return pair(one[layer].fin.at[0], out.at[layer, k], base, base + k, forth[k])

    def owner_local(layer, kind, order):
        out, one = ((out_q, sum_q), (out_u, sum_u))[kind]
        return pltpu.make_async_copy(
            one[layer].fin.at[order], out.at[layer, r], local.at[30 + layer * 2 + kind]
        )

    def out_swap(layer):
        return pair(sum_b[layer].fin, out_b.at[layer], 20 + layer * 8, 20 + layer * 8, swap_to)

    def out_local(layer):
        return pltpu.make_async_copy(sum_b[layer].fin, out_b.at[layer], local.at[34 + layer])

    def hand_a(layer, kind):
        for order in range(2):
            when_else(
                back_self[order],
                lambda: owner_local(layer, kind, order).start(),
                lambda: owner_copy(layer, kind, order).start(),
            )

    def hand_b(layer):
        when_else(swap_needed, lambda: out_swap(layer).start(), lambda: out_local(layer).start())

    def handed(layer):
        for kind in range(2):
            for k in range(2):
                when_else(
                    back_self[k],
                    lambda: owner_local(layer, kind, k).wait(),
                    lambda: owner_copy(layer, kind, k).wait_send(),
                )

                @pl.when(jnp.logical_not(forth_self[k]))
                def _():
                    owner_arrival(layer, kind, k).wait_recv()

        when_else(swap_needed, lambda: out_swap(layer).wait(), lambda: out_local(layer).wait())

    def phase(step, which):
        for order in range(2):
            for one in which:
                step(one, order)

    layer = layers[1]
    layer.inputs(hat_all[...].astype(F32), attn_in[1], mlp_in[1])
    layer.project(attn_in[1], joined[1])
    layer.attend(joined[1], probs[1], heads[1])
    late[1].arrive()
    layer.units(mlp_in[1], slope[1], units[1])
    late[2].arrive()
    for one in gathers:
        one.finish()
    b_high = at.gb.shape[3]
    grads_b(heads[1], grad[1], grads[1][2], 0, out_rows)
    grads_b(units[1], grad[1], grads[1][2], out_rows, b_high)
    sum_b[1].start()
    part = at.part[1]
    for start in (0, D // 2):
        part[:, start : start + D // 2] = (
            layer.outputs(heads[1], units[1], start, D // 2).astype(BF)
        )
    part[mine, :] = (part[mine, :].astype(F32) + at.state[...]).astype(BF)
    out_sum = group_sum(
        here, copies, part, blocks_index(rows, lanes), lanes, at.near[1], at.far[1]
    )
    out_sum.start()
    grad_heads, grad_pre, raw, grad_joined = at.grad_heads, at.grad_pre, at.raw, at.grad_joined
    sums = at.sums
    layer.branch_back(grad[1], slope[1], grad_heads, grad_pre)
    phase(GradSum.line, [sum_b[1]])
    layer.attend_back(joined[1], probs[1], grad_heads, raw, grad_joined)
    phase(GradSum.line_middle, [sum_b[1]])
    out_sum.middle()
    back = at.back[1]
    back[...] = layer.inputs_back(
        grad_joined, grad_pre, hat_all[...].astype(F32), grad[1], sums[1]
    ).astype(BF)
    summed = group_sum(here, copies, back, rows_index(quarter), D, at.near[2], at.far[2])
    summed.start()
    grads_a(mlp_in[1], grad_pre, grads[1][1])
    sum_u[1].start()
    summed.middle()
    grads_a(attn_in[1], grad_joined, grads[1][0])
    sum_q[1].start()
    summed.end()
    grad_one = at.grad_one
    total = grad[1][mine, :].astype(F32) + inv_std[:, :1] * summed.total(0)
    grad_one[...] = total
    grad[0][mine, :] = total.astype(BF)
    spread = group_gather(here, copies, grad[0], quarter)
    spread.start()
    phase(GradSum.line, [sum_u[1]])
    spread.middle()
    phase(GradSum.turn, [sum_b[1]])
    phase(GradSum.line, [sum_q[1]])
    out_sum.end()
    first_bias = vec[VEC_ROWS + 4 : VEC_ROWS + 5, features]
    bias_sum = first_bias + vec[VEC_ROWS + 5 : VEC_ROWS + 6, features]
    at.hidden[...] = (out_sum.total(0) + bias_sum).astype(BF)
    phase(GradSum.line_middle, [sum_u[1]])
    spread.end()
    rings += [out_sum, summed, spread]

    def conclude(layer_index, one, kind):
        for order in range(2):
            one.end(order)
        if kind == 2:
            hand_b(layer_index)
        else:
            hand_a(layer_index, kind)

    layer = layers[0]
    grads_b(heads[0], grad[0], grads[0][2], 0, out_rows)
    grads_b(units[0], grad[0], grads[0][2], out_rows, b_high)
    sum_b[0].start()
    phase(GradSum.line_middle, [sum_q[1]])
    layer.branch_back(grad[0], slope[0], grad_heads, grad_pre)
    conclude(1, sum_b[1], 2)
    phase(GradSum.turn, [sum_u[1]])
    phase(GradSum.line, [sum_b[0]])
    grads_a(mlp_in[0], grad_pre, grads[0][1])
    sum_u[0].start()
    phase(GradSum.turn, [sum_q[1]])
    layer.attend_back(joined[0], probs[0], grad_heads, raw, grad_joined)
    phase(GradSum.line_middle, [sum_b[0]])
    grads_a(attn_in[0], grad_joined, grads[0][0])
    sum_q[0].start()
    phase(GradSum.line, [sum_u[0]])
    hat, inverse = norm_stats(hid_all[...].astype(F32))
    value = layer.inputs_back(grad_joined, grad_pre, hat, grad[0], sums[0])
    back = at.back[0]
    back[...] = (inverse * value).astype(BF)
    back[mine, :] = (back[mine, :].astype(F32) + grad_one[...]).astype(BF)
    summed = group_sum(
        here, copies, back, blocks_index(rows, lanes), lanes, at.near[3], at.far[3]
    )
    summed.start()
    phase(GradSum.line, [sum_q[0]])
    v_core, v_line, v_last, v_group = at.v_core, at.v_line, at.v_last, at.v_group
    v_lanes = D // 2
    v_mine = pl.ds(pl.multiple_of(here.core * v_lanes, v_lanes), v_lanes)
    v_other = pl.ds(pl.multiple_of((1 - here.core) * v_lanes, v_lanes), v_lanes)
    v_copies = [copies.to(sums[k].at[:, v_other], v_core.at[k], here.partner) for k in range(2)]
    for copy in v_copies:
        copy.start()
    phase(GradSum.line_middle, [sum_u[0]])
    summed.middle()
    conclude(1, sum_u[1], 1)
    conclude(1, sum_q[1], 0)
    phase(GradSum.turn, [sum_b[0]])
    for copy in v_copies:
        copy.wait()
    for k in range(LAYERS):
        v_line[here.x, k * VEC_ROWS : (k + 1) * VEC_ROWS] = v_core[k] + sums[k][:, v_mine]
    v_x = [
        copies.to(v_line.at[here.x], v_line.at[here.x], here.x_ring.device(k))
        for k in range(1, nx)
    ]
    for copy in v_x:
        copy.start()
    phase(GradSum.line_middle, [sum_q[0]])
    phase(GradSum.turn, [sum_u[0]])
    summed.end()
    at.grad_out[...] = summed.total(0)
    rings.append(summed)
    for copy in v_x:
        copy.wait()
    total = v_line[0]
    for k in range(1, nx):
        total = total + v_line[k]
    v_last[here.z] = total
    v_z = [
        copies.to(v_last.at[here.z], v_last.at[here.z], here.z_ring.device(k))
        for k in range(1, nz)
    ]
    for copy in v_z:
        copy.start()
    phase(GradSum.turn, [sum_q[0]])
    conclude(0, sum_b[0], 2)
    for copy in v_z:
        copy.wait()
    total = v_last[0]
    for k in range(1, nz):
        total = total + v_last[k]
    v_group[here.place] = total
    v_y = [
        copies.to(v_group.at[here.place], v_group.at[here.place], here.y_ring.device(k))
        for k in range(1, 4)
    ]
    for copy in v_y:
        copy.start()
    conclude(0, sum_u[0], 1)
    conclude(0, sum_q[0], 0)
    for copy in v_y:
        copy.wait()
    total = v_group[0]
    for k in range(1, 4):
        total = total + v_group[k]
    out_v = at.out_v
    out_v[0, :, v_mine] = total
    out_v[1, :, v_mine] = v_group[here.place]
    v_swap = copies.to(out_v.at[:, :, v_mine], out_v.at[:, :, v_mine], here.partner)
    v_swap.start()
    v_swap.wait()
    handed(1)
    handed(0)
    assert copies.count <= sends.shape[0], copies.count
    for ring in rings:
        ring.finish()
    for one in sum_q + sum_u + sum_b:
        one.finish()


def whole(grid, cut, sizes, widths, ins):
    nz, nx, nc = grid
    qkv_width, up_width, out_rows = sizes
    rows, lanes = ins["hid"].shape
    group, quarter = 2 * rows, rows // 2
    slot_rows, down_rows = ins["qkv_weight"].shape[1], ins["down_weight"].shape[1]
    b_rows = out_rows + down_rows
    heads_here = qkv_width // (3 * HEAD)

    def low(*dims):
        return pltpu.VMEM(dims, BF)

    def high(*dims):
        return pltpu.VMEM(dims, F32)

    def twice(make, *dims):
        return [make(*dims) for _ in range(LAYERS)]

    shape = jax.ShapeDtypeStruct
    outs = dict(
        hidden=shape((rows, lanes), BF),
        grad_out=shape((rows, lanes), F32),
        out_q=shape((LAYERS, 2, slot_rows, qkv_width), BF),
        out_u=shape((LAYERS, 2, slot_rows, up_width), BF),
        out_b=shape((LAYERS, b_rows, lanes), BF),
        out_v=shape((2, LAYERS * VEC_ROWS, D), F32),
    )
    q_shape = (nz, nx, nc, 2 * slot_rows, qkv_width)
    u_shape = (nz, nx, nc, 2 * slot_rows, up_width)
    b_shape = (nz // 2, nx, nc, b_rows, 2 * lanes)
    c_shape = (8, -(-sum(widths) // 128) * 128)
    kinds = ((q_shape, "a"), (u_shape, "a"), (b_shape, "b"))
    blocks = [ring_scratch(quarter, D), ring_scratch(rows, lanes)] * 2
    scratch = dict(
        hid_all=low(group, D),
        cot_all=low(group, D),
        vec=high(LAYERS * VEC_ROWS, D),
        vec_own=high(LAYERS * VEC_ROWS, lanes),
        wq=low(LAYERS, 2, slot_rows, qkv_width),
        wu=low(LAYERS, 2, slot_rows, up_width),
        wb=low(LAYERS, b_rows, lanes),
        wc=high(*c_shape),
        q_own=low(LAYERS, 2 * slot_rows, qkv_width),
        u_own=low(LAYERS, 2 * slot_rows, up_width),
        b_own=low(LAYERS, b_rows, lanes),
        q_zero=low(*q_shape),
        q_one=low(*q_shape),
        u_zero=low(*u_shape),
        u_one=low(*u_shape),
        b_zero=low(*b_shape),
        b_one=low(*b_shape),
        full_c=high(nz, nx, nc, *c_shape),
        cosine=high(group, 6 * HEAD),
        left=high(group, 6 * HEAD),
        right=high(group, 6 * HEAD),
        mask=high(group, group),
        live=high(group, 128),
        bias=high(2 * LAYERS, D),
        state=high(quarter, D),
        inv_std=high(quarter, 128),
        hat_all=low(group, D),
        grad_one=high(quarter, D),
        grad_heads=low(group, heads_here * HEAD),
        grad_pre=low(group, up_width),
        raw=high(group, qkv_width),
        grad_joined=low(group, qkv_width),
        gq=low(*q_shape),
        gu=low(*u_shape),
        gb=low(*b_shape),
        v_core=high(2, VEC_ROWS, D // 2),
        v_line=high(nx, LAYERS * VEC_ROWS, D // 2),
        v_last=high(nz, LAYERS * VEC_ROWS, D // 2),
        v_group=high(4, LAYERS * VEC_ROWS, D // 2),
        attn_in=twice(low, group, D),
        mlp_in=twice(low, group, D),
        joined=twice(low, group, qkv_width),
        probs=twice(low, heads_here, group, group),
        heads=twice(low, group, heads_here * HEAD),
        slope=twice(low, group, up_width),
        units=twice(low, group, up_width),
        part=twice(low, group, D),
        back=twice(low, group, D),
        grad=twice(low, group, D),
        sums=twice(high, VEC_ROWS, D),
        sum_buffers=[
            [grad_buffers(grid, cut, dims, kind) for dims, kind in kinds] for _ in range(LAYERS)
        ],
        near=[block[0] for block in blocks],
        far=[block[1] for block in blocks],
        sends=pltpu.SemaphoreType.DMA((480,)),
        recvs=pltpu.SemaphoreType.DMA((480,)),
        local=pltpu.SemaphoreType.DMA((40,)),
    )
    flat = jax.tree.leaves(scratch)
    tree = jax.tree.structure(dict(**ins, **outs, **scratch))
    order = [*ins.values(), *outs.values(), *scratch.values()]
    names = [*ins, *outs, *scratch]
    ranks = jax.tree.unflatten(
        jax.tree.structure(dict(zip(names, order))), range(tree.num_leaves)
    )
    given = jax.tree.leaves([ranks[name] for name in names])

    def kernel(*refs):
        placed = [None] * len(refs)
        for rank, ref in zip(given, refs):
            placed[rank] = ref
        whole_kernel(grid, cut, sizes, widths, tree, *placed)

    flat = jax.tree.leaves(list(scratch.values()))
    return pl.pallas_call(
        kernel,
        out_shape=tuple(outs.values()),
        in_specs=[VMEM_SPEC] * len(ins),
        out_specs=(VMEM_SPEC,) * len(outs),
        scratch_shapes=flat,
        compiler_params=params(0, 63),
        name="whole_step",
    )(*ins.values())


def update_kernel(n_dp, bias_widths, out_rows, *refs):
    given, refs = refs[:27], refs[27:]
    results, refs = refs[:23], refs[23:]
    held, made, in_sems, out_sems = refs[:27], refs[27:48], refs[48], refs[49]
    d, r = lax.axis_index("dp"), lax.axis_index("row")
    loads = [
        pltpu.make_async_copy(src, dst, in_sems.at[k])
        for k, (src, dst) in enumerate(zip(given, held))
    ]
    stores = [
        pltpu.make_async_copy(src, dst, out_sems.at[k])
        for k, (src, dst) in enumerate(zip((*made, *held[25:]), results))
    ]
    for copy in loads:
        copy.start()
    own_q, own_u, own_b, all_v = held[:4]
    old = held[4:25]
    for copy in loads[:4]:
        copy.wait()

    def update(k, at, gradient, rate, decay):
        values = adamw(*[ref[at] for ref in old[3 * k : 3 * k + 3]], gradient, rate, decay)
        for ref, value in zip(made[3 * k : 3 * k + 3], values):
            ref[at] = value

    def begin(k):
        for copy in loads[4 + 3 * k : 7 + 3 * k]:
            copy.wait()

    def finish(k):
        for copy in stores[3 * k : 3 * k + 3]:
            copy.start()

    for k, own in ((0, own_q), (2, own_u)):
        begin(k)
        width = own.shape[3]
        for layer in range(LAYERS):
            for side in range(2):
                at = (layer, slice(None), slice(side * width, (side + 1) * width))
                update(k, at, own[layer, side].astype(F32), RATE_MATRIX, DECAY_MATRIX)
        finish(k)
    for k, rows in ((1, slice(0, out_rows)), (3, slice(out_rows, None))):
        begin(k)
        update(k, ..., own_b[:, rows].astype(F32), RATE_MATRIX, DECAY_MATRIX)
        finish(k)
    for k, width in enumerate(bias_widths):
        begin(4 + k)
        for layer in range(LAYERS):
            rows = all_v[1, layer * VEC_ROWS : (layer + 1) * VEC_ROWS, :]
            moved = pltpu.roll(rows, lax.rem(D - d * width, D), 1)
            at = (slice(layer, layer + 1), slice(None))
            update(4 + k, at, moved[5 + k : 6 + k, :width], RATE_MATRIX, 0.0)
        finish(4 + k)
    lanes = old[18].shape[2]
    features = pl.ds(pl.multiple_of(r * lanes, lanes), lanes)
    begin(6)
    for layer in range(LAYERS):
        for k in range(6):
            row = layer * VEC_ROWS + min(k, 4)
            at = (k, slice(layer, layer + 1), slice(None))
            update(6, at, all_v[0, row : row + 1, features], RATE_VECTOR, 0.0)
    finish(6)
    for load, store in zip(loads[25:], stores[21:]):
        load.wait()
        store.start()
    for copy in stores:
        copy.wait()


def update_all(n_dp, bias_widths, out_rows, passed, gradients, old):
    anywhere = pl.BlockSpec(memory_space=pl.ANY)
    given = (*gradients, *old, *passed)
    return pl.pallas_call(
        partial(update_kernel, n_dp, bias_widths, out_rows),
        out_shape=tuple(jax.ShapeDtypeStruct(a.shape, a.dtype) for a in (*old, *passed)),
        in_specs=[anywhere] * len(given),
        out_specs=(anywhere,) * (len(old) + len(passed)),
        scratch_shapes=[
            *[pltpu.VMEM(a.shape, a.dtype) for a in given],
            *[pltpu.VMEM(a.shape, F32) for a in old],
            pltpu.SemaphoreType.DMA((len(given),)),
            pltpu.SemaphoreType.DMA((len(old) + len(passed),)),
        ],
        compiler_params=pltpu.CompilerParams(vmem_limit_bytes=60 << 20),
        name="update_all",
    )(*given)


def on_device(
    hidden_in,
    cotangent,
    seq_ids,
    qkv_weight,
    qkv_first,
    qkv_second,
    out_weight,
    out_first,
    out_second,
    up_weight,
    up_first,
    up_second,
    down_weight,
    down_first,
    down_second,
    qkv_bias,
    qkv_bias_first,
    qkv_bias_second,
    up_bias,
    up_bias_first,
    up_bias_second,
    row_vectors,
    row_first,
    row_second,
):
    n_dp = lax.axis_size("dp")
    grid = GRIDS[n_dp]
    group_len = seq_ids.shape[0]
    qkv_width, up_width = qkv_weight.shape[2] // 2, up_weight.shape[2] // 2
    out_rows, down_rows = out_weight.shape[1], down_weight.shape[1]
    bias_widths = qkv_bias.shape[1], up_bias.shape[1]
    cut = out_rows + down_rows // 2
    sizes = (qkv_width, up_width, out_rows)

    ins = dict(
        hid=hidden_in,
        cot=cotangent,
        ids=seq_ids.reshape(1, group_len),
        row_vectors=row_vectors.transpose(1, 0, 2),
        qkv_bias=qkv_bias,
        up_bias=up_bias,
        qkv_weight=qkv_weight,
        out_weight=out_weight,
        up_weight=up_weight,
        down_weight=down_weight,
    )
    *passed, own_q, own_u, own_b, all_v = whole(grid, cut, sizes, bias_widths, ins)
    gradients = (own_q, own_u, own_b, all_v)
    old = (
        qkv_weight,
        qkv_first,
        qkv_second,
        out_weight,
        out_first,
        out_second,
        up_weight,
        up_first,
        up_second,
        down_weight,
        down_first,
        down_second,
        qkv_bias,
        qkv_bias_first,
        qkv_bias_second,
        up_bias,
        up_bias_first,
        up_bias_second,
        row_vectors.transpose(1, 0, 2),
        row_first.transpose(1, 0, 2),
        row_second.transpose(1, 0, 2),
    )
    *new, row_new, row_one, row_two, hidden_out, grad_state = update_all(
        n_dp, bias_widths, out_rows, passed, gradients, old
    )
    rows = [a.transpose(1, 0, 2) for a in (row_new, row_one, row_two)]
    return hidden_out, grad_state, *new, *rows


def solution(mesh):
    placed = (
        P(("dp", "col"), "row"),
        P(("dp", "col"), "row"),
        P("dp"),
        P(None, ("row", "dp"), "col"),
        P(None, ("row", "dp"), "col"),
        P(None, ("row", "dp"), "col"),
        P(None, ("col", "dp"), "row"),
        P(None, ("col", "dp"), "row"),
        P(None, ("col", "dp"), "row"),
        P(None, ("row", "dp"), "col"),
        P(None, ("row", "dp"), "col"),
        P(None, ("row", "dp"), "col"),
        P(None, ("col", "dp"), "row"),
        P(None, ("col", "dp"), "row"),
        P(None, ("col", "dp"), "row"),
        P(None, ("col", "row", "dp")),
        P(None, ("col", "row", "dp")),
        P(None, ("col", "row", "dp")),
        P(None, ("col", "row", "dp")),
        P(None, ("col", "row", "dp")),
        P(None, ("col", "row", "dp")),
        P(None, None, "row"),
        P(None, None, "row"),
        P(None, None, "row"),
    )
    return jax.shard_map(
        on_device,
        mesh=mesh,
        in_specs=placed,
        out_specs=(
            P(("dp", "col"), "row"),
            P(("dp", "col"), "row"),
            P(None, ("row", "dp"), "col"),
            P(None, ("row", "dp"), "col"),
            P(None, ("row", "dp"), "col"),
            P(None, ("col", "dp"), "row"),
            P(None, ("col", "dp"), "row"),
            P(None, ("col", "dp"), "row"),
            P(None, ("row", "dp"), "col"),
            P(None, ("row", "dp"), "col"),
            P(None, ("row", "dp"), "col"),
            P(None, ("col", "dp"), "row"),
            P(None, ("col", "dp"), "row"),
            P(None, ("col", "dp"), "row"),
            P(None, ("col", "row", "dp")),
            P(None, ("col", "row", "dp")),
            P(None, ("col", "row", "dp")),
            P(None, ("col", "row", "dp")),
            P(None, ("col", "row", "dp")),
            P(None, ("col", "row", "dp")),
            P(None, None, "row"),
            P(None, None, "row"),
            P(None, None, "row"),
        ),
        check_vma=False,
    )
```

```python
import math
from functools import partial
from types import SimpleNamespace

import jax
import jax.numpy as jnp
from jax import lax
from jax.experimental import pallas as pl
from jax.experimental.pallas import tpu as pltpu
from jax.sharding import PartitionSpec as P

D = 1024
HEAD = 64
ROT = 16
LAYERS = 2
SEQS = 3
STEP = 10


EPS_NORM = 1e-05
EPS_ADAM = 1e-08
BETA_ONE = 0.9
BETA_TWO = 0.95
RATE_MATRIX = 0.06
RATE_VECTOR = 0.6
DECAY_MATRIX = 0.01
ROPE_BASE = 10000.0
MASK_VALUE = -1e30
CONTRACT_ROWS = (((0,), (0,)), ((), ()))
CONTRACT_COLS = (((1,), (1,)), ((), ()))

BF = jnp.bfloat16
F32 = jnp.float32
MESH = pl.DeviceIdType.MESH
GRIDS = {32: (4, 4, 2), 8: (2, 2, 2)}
VEC_ROWS = 8
VMEM_SPEC = pl.BlockSpec(memory_space=pltpu.VMEM)


def params(collective_id, mib):
    return pltpu.CompilerParams(
        collective_id=collective_id, has_side_effects=True, vmem_limit_bytes=mib << 20
    )


def remote(src, dst, sends, recvs, at, device):
    return pltpu.make_async_remote_copy(
        src_ref=src,
        dst_ref=dst,
        send_sem=sends.at[at],
        recv_sem=recvs.at[at],
        device_id=device,
        device_id_type=MESH,
    )


def greet(device):
    pl.semaphore_signal(
        pltpu.get_barrier_semaphore(), inc=1, device_id=device, device_id_type=MESH
    )


def greeted(count):
    pl.semaphore_wait(pltpu.get_barrier_semaphore(), count)


def group_place():
    return lax.axis_index("row") * 2 + lax.axis_index("col")


def group_peer(place, step):
    other = lax.rem(place + step, 4)
    return {"row": other // 2, "col": lax.rem(other, 2)}


def over(lengths, body):
    total = math.prod(lengths)

    def one(index, carry):
        place, rest = [], index
        for length in reversed(lengths):
            place.append(lax.rem(rest, length))
            rest = rest // length
        body(*reversed(place))
        return carry

    lax.fori_loop(0, total, one, 0)


def adamw(master, moment_one, moment_two, gradient, step_rate, step_decay):
    one_new = BETA_ONE * moment_one + (1.0 - BETA_ONE) * gradient
    two_new = BETA_TWO * moment_two + (1.0 - BETA_TWO) * gradient * gradient
    one_hat = one_new / (1.0 - BETA_ONE**STEP)
    two_hat = two_new / (1.0 - BETA_TWO**STEP)
    master_new = master - step_rate * (
        one_hat / (jnp.sqrt(two_hat) + EPS_ADAM) + step_decay * master
    )
    return (master_new, one_new, two_new)


class Copies:
    def __init__(self, sends, recvs):
        self.sends, self.recvs, self.count = sends, recvs, 0

    def to(self, src, dst, device):
        copy = remote(src, dst, self.sends, self.recvs, self.count, device)
        self.count += 1
        return copy


class Ring:
    def __init__(self, length, place, device_at):
        self.length, self.place, self.device_at = length, place, device_at
        self.ways = ((0, 1), (1, -1)) if length > 2 else ((0, 1),)

    def at(self, step):
        return lax.rem(self.place + step + self.length, self.length)

    def device(self, step):
        return self.device_at(self.at(step))


class RingGather:
    def __init__(self, copies, ring, views, sources=None, arrived=None):
        self.copies, self.ring, self.views = copies, ring, views
        self.sources, self.arrived = sources, arrived
        self.near, self.far = [[], []], [[], []]

    def start(self):
        for way, step in self.ring.ways:
            for k, view in enumerate(self.views):
                own = view(self.ring.place, None)
                src = self.sources[k] if self.sources else own
                copy = self.copies.to(src, own, self.ring.device(step))
                copy.start()
                self.near[way].append(copy)

    def middle(self):
        for way, step in self.ring.ways:
            for copy in self.near[way]:
                copy.wait_recv()
            came_from = self.ring.at(-step)
            if self.ring.length > 2:
                for view in self.views:
                    ref = view(came_from, way)
                    if ref is not None:
                        copy = self.copies.to(ref, ref, self.ring.device(step))
                        copy.start()
                        self.far[way].append(copy)
            if self.arrived:
                self.arrived(came_from)

    def end(self):
        for copy in self.far[0] + self.far[1]:
            copy.wait_recv()
        if self.arrived and self.ring.length > 2:
            self.arrived(self.ring.at(2))

    def finish(self):
        for copy in self.near[0] + self.near[1] + self.far[0] + self.far[1]:
            copy.wait_send()


class DirectGather:
    def __init__(self, copies, ring, views, sources):
        self.copies, self.ring, self.views, self.sources = copies, ring, views, sources
        self.sent = []

    def start(self):
        for step in range(1, self.ring.length):
            for view, source in zip(self.views, self.sources):
                own = view(self.ring.place, None)
                copy = self.copies.to(source, own, self.ring.device(step))
                copy.start()
                self.sent.append(copy)

    def end(self):
        for copy in self.sent:
            copy.wait_recv()

    def finish(self):
        for copy in self.sent:
            copy.wait_send()


class Summand:
    def __init__(self, ref, index, count, width, near, far):
        self.ref, self.index, self.count, self.width = ref, index, count, width
        self.near, self.far = near, far

    def view(self, target, start, width):
        return self.ref.at[self.index(slice(None), target, start, width)]

    def add(self, target, start, width, other):
        def one(lead):
            at = self.index(lead, target, start, width)
            more = other[...] if self.count is None else other[lead]
            self.ref[at] = self.ref[at] + more

        if self.count is None:
            one(None)
        else:
            over((self.count,), one)

    def total(self, lead, target, ways):
        value = self.ref[self.index(lead, target, 0, self.width)].astype(F32)
        for way in range(ways):
            more = self.far[way][...] if self.count is None else self.far[way][lead]
            value = value + more.astype(F32)
        return value


class RingSum:
    def __init__(self, copies, ring, summands):
        self.copies, self.ring, self.summands = copies, ring, summands
        self.near, self.far = [[], []], [[], []]

    def start(self):
        if self.ring.length == 2:
            return
        for way, step in self.ring.ways:
            for s in self.summands:
                half = s.width // 2
                copy = self.copies.to(
                    s.view(self.ring.at(2), way * half, half), s.near[way], self.ring.device(step)
                )
                copy.start()
                self.near[way].append(copy)

    def middle(self):
        for way, step in self.ring.ways:
            target = self.ring.at(step)
            for k, s in enumerate(self.summands):
                if self.ring.length > 2:
                    self.near[way][k].wait_recv()
                    s.add(target, way * (s.width // 2), s.width // 2, s.near[way])
                copy = self.copies.to(
                    s.view(target, 0, s.width), s.far[way], self.ring.device(step)
                )
                copy.start()
                self.far[way].append(copy)

    def end(self):
        for copy in self.far[0] + self.far[1]:
            copy.wait_recv()

    def total(self, k, lead=None):
        return self.summands[k].total(lead, self.ring.place, len(self.ring.ways))

    def finish(self):
        for copy in self.near[0] + self.near[1] + self.far[0] + self.far[1]:
            copy.wait_send()


class DirectSum:
    def __init__(self, copies, ring, summand):
        self.copies, self.ring, self.summand = copies, ring, summand
        self.sent = []

    def start(self):
        for step in range(1, self.ring.length):
            copy = self.copies.to(
                self.summand.view(self.ring.at(step), 0, self.summand.width),
                self.summand.far[step - 1],
                self.ring.device(step),
            )
            copy.start()
            self.sent.append(copy)

    def end(self):
        for copy in self.sent:
            copy.wait_recv()

    def total(self):
        return self.summand.total(None, self.ring.place, self.ring.length - 1)

    def finish(self):
        for copy in self.sent:
            copy.wait_send()


def lanes_at(start, width):
    if not isinstance(start, int):
        start = pl.multiple_of(start, 128)
    return pl.ds(start, width)


class Slice:
    def __init__(self, grid):
        self.grid = grid
        nz, nx, nc = grid
        d = lax.axis_index("dp")
        self.d, self.z, self.x, self.core = d, d // (nx * nc), lax.rem(d // nc, nx), lax.rem(d, nc)
        self.row, self.col = lax.axis_index("row"), lax.axis_index("col")
        self.half = nz * nx * nc // 2
        self.place = group_place()
        self.zls = nz // 2
        self.partner = self.dp(self.z, self.x, 1 - self.core)
        self.z_ring = Ring(nz, self.z, lambda z: self.dp(z, self.x, self.core))
        self.x_ring = Ring(nx, self.x, lambda x: self.dp(self.z, x, self.core))
        self.y_ring = Ring(4, self.place, lambda q: {"row": q // 2, "col": lax.rem(q, 2)})

    def dp(self, z, x, core):
        _, nx, nc = self.grid
        return {"dp": (z * nx + x) * nc + core}

    def greet_rings(self, rings, whole=False):
        count = 0
        for ring in rings:
            steps = range(1, ring.length) if whole else [step for _, step in ring.ways]
            for step in steps:
                greet(ring.device(step))
                count += 1
        return count


class WeightGather:
    def __init__(self, here, cut, copies, local, own, full, spread):
        self.here, self.copies, self.core_copies = here, copies, []
        rows, lanes = own.shape
        pair = full.shape[-1] != lanes
        first = cut if pair else rows // 2
        cuts = (pl.ds(0, first), pl.ds(first, rows - first))
        z, x, core, zls = here.z, here.x, here.core, here.zls

        def part(width, half):
            return (0, width) if half is None else (half * (width // 2), width // 2)

        def chunk(order, along, half):
            zz, xx = (along, x) if order == 0 else (z, along)
            start, width = part(lanes, half)
            if pair:
                at = lanes_at((zz // zls) * lanes + start, width)
                return full.at[lax.rem(zz, zls), xx, core, cuts[order], at]
            return full.at[zz, xx, core, cuts[order], pl.ds(start, width)]

        def line(order, along, half):
            if order == 0:
                at = pl.ds(*part(full.shape[-1], half))
                return full.at[:, along, core, cuts[0], at]
            start, width = part(lanes, half)
            if pair:
                at = lanes_at((along // zls) * lanes + start, width)
                return full.at[lax.rem(along, zls), :, core, cuts[1], at]
            return full.at[along, :, core, cuts[1], pl.ds(start, width)]

        def small(order, along, half):
            return None if half == 1 else spread[1].at[along, x, core]

        def small_line(order, along, half):
            return None if half == 1 else spread[1].at[:, along, core]

        rings = ((here.z_ring, here.x_ring), (here.x_ring, here.z_ring))
        self.first, self.second, self.lines, self.own = [], [], [], []
        for order in range(2):
            sources = [own.at[cuts[order]]]
            chunks, lines = [partial(chunk, order)], [partial(line, order)]
            if order == 0 and spread:
                sources.append(spread[0])
                chunks.append(partial(small, order))
                lines.append(partial(small_line, order))
            for k, view in enumerate(chunks):
                self.own.append(
                    pltpu.make_async_copy(
                        sources[k], view(rings[order][0].place, None), local.at[order * 2 + k]
                    )
                )
            self.first.append(DirectGather(copies, rings[order][0], chunks, sources))
            self.second.append(
                RingGather(copies, rings[order][1], lines, None, partial(self.forward, order))
            )
            self.lines.append(lines)

    def forward(self, order, along):
        for view in self.lines[order]:
            ref = view(along, None)
            copy = self.copies.to(ref, ref, self.here.partner)
            copy.start()
            self.core_copies.append(copy)

    def start(self):
        for ring in self.first:
            ring.start()
        for copy in self.own:
            copy.start()

    def turn(self):
        for copy in self.own:
            copy.wait()
        for order in range(2):
            self.first[order].end()
            self.second[order].start()
            self.forward(order, self.second[order].ring.place)

    def second_middle(self):
        for ring in self.second:
            ring.middle()

    def end(self):
        for ring in self.second:
            ring.end()

    def arrive(self):
        for copy in self.core_copies:
            copy.wait_recv()

    def finish(self):
        for ring in self.first + self.second:
            ring.finish()
        for copy in self.core_copies:
            copy.wait_send()


def dot(left, right):
    return jnp.dot(left, right, preferred_element_type=F32)


def dot_rows(left, right):
    return lax.dot_general(left, right, CONTRACT_ROWS, preferred_element_type=F32)


def dot_cols(left, right):
    return lax.dot_general(left, right, CONTRACT_COLS, preferred_element_type=F32)


def norm_stats(state):
    width = state.shape[1]
    average = jnp.sum(state, 1, keepdims=True) / width
    spread = jnp.sum(state * state, 1, keepdims=True) / width - average * average
    inv_std = lax.rsqrt(spread + EPS_NORM)
    return ((state - average) * inv_std, inv_std)


def norm_back(grad_hat, hat):
    width = hat.shape[1]
    first = jnp.sum(grad_hat, 1, keepdims=True) / width
    second = jnp.sum(grad_hat * hat, 1, keepdims=True) / width
    return grad_hat - first - hat * second


class Layer:
    def __init__(self, layer, vec, tables, mask, bias, full_q, full_u, full_b, sizes):
        self.vec, self.tables, self.mask, self.bias = vec, tables, mask, bias
        self.layer, self.full_q, self.full_u, self.full_b = layer, full_q, full_u, full_b
        self.qkv_width, self.up_width, self.out_rows = sizes
        self.heads_here = self.qkv_width // (3 * HEAD)

    def vector(self, k):
        at = self.layer * VEC_ROWS + k
        return self.vec[at : at + 1, :]

    def q_matrix(self, start, width):
        return self.full_q[:, :, :, :, start : start + width].reshape(-1, width)

    def u_matrix(self, start, width):
        return self.full_u[:, :, :, :, start : start + width].reshape(-1, width)

    def b_matrix(self, low, high, start, width):
        value = self.full_b[:, :, :, low:high, start : start + width]
        return value.reshape(-1, width)

    def out_matrix(self, start, width):
        return self.b_matrix(0, self.out_rows, start, width)

    def down_matrix(self, start, width):
        return self.b_matrix(self.out_rows, self.full_b.shape[3], start, width)

    def inputs(self, hat, attn_in, mlp_in):
        attn_in[...] = (hat * self.vector(0) + self.vector(1)).astype(BF)
        mlp_in[...] = (hat * self.vector(2) + self.vector(3)).astype(BF)

    def project(self, attn_in, joined):
        pair = 6 * HEAD
        cosine, left, right = self.tables
        for start in range(0, self.qkv_width, pair):
            value = dot(attn_in[...], self.q_matrix(start, pair))
            value = value + self.bias[0:1, start : start + pair]
            value = (
                value * cosine[...]
                + pltpu.roll(value, pair - ROT // 2, 1) * left[...]
                + pltpu.roll(value, ROT // 2, 1) * right[...]
            )
            joined[:, start : start + pair] = value.astype(BF)

    def head(self, joined, h):
        start = h * 3 * HEAD
        return [joined[:, start + k * HEAD : start + (k + 1) * HEAD] for k in range(3)]

    def attend(self, joined, probs, heads):
        for h in range(self.heads_here):
            query, key_rows, value_rows = self.head(joined, h)
            scores = dot_cols(query, key_rows) * HEAD**-0.5 + self.mask[...]
            expo = jnp.exp(scores - jnp.max(scores, 1, keepdims=True))
            low = (expo / jnp.sum(expo, 1, keepdims=True)).astype(BF)
            probs[h] = low
            heads[:, h * HEAD : (h + 1) * HEAD] = dot(low, value_rows).astype(BF)

    def units(self, mlp_in, slope, units):
        width = 256
        for start in range(0, self.up_width, width):
            at = slice(start, start + width)
            value = dot(mlp_in[...], self.u_matrix(start, width))
            value = value + self.bias[1:2, at]
            below = 0.5 * (1.0 + lax.erf(value * 0.5**0.5))
            density = jnp.exp(value * value * -0.5) * ((2.0 * math.pi) ** -0.5)
            units[:, at] = (value * below).astype(BF)
            slope[:, at] = (below + value * density).astype(BF)

    def outputs(self, heads, units, start, width):
        return dot(heads[...], self.out_matrix(start, width)) + dot(
            units[...], self.down_matrix(start, width)
        )

    def branch_back(self, grad, slope, grad_heads, grad_pre):
        grad_heads[...] = dot_cols(grad[...], self.out_matrix(0, D)).astype(BF)
        zls = self.full_b.shape[0]
        width = self.up_width // zls
        step = min(width, 256)
        for zl in range(zls):
            matrix = self.full_b[zl, :, :, self.out_rows :, :].reshape(-1, D)
            for start in range(0, width, step):
                at = slice(zl * width + start, zl * width + start + step)
                pull = dot_cols(grad[...], matrix[start : start + step])
                grad_pre[:, at] = (pull * slope[:, at].astype(F32)).astype(BF)

    def attend_back(self, joined, probs, grad_heads, raw, grad_joined):
        for h in range(self.heads_here):
            query, key_rows, value_rows = self.head(joined, h)
            grad = grad_heads[:, h * HEAD : (h + 1) * HEAD]
            low = probs[h]
            high = low.astype(F32)
            grad_probs = dot_cols(grad, value_rows)
            inner = jnp.sum(grad_probs * high, 1, keepdims=True)
            grad_raw = (high * (grad_probs - inner) * HEAD**-0.5).astype(BF)
            start = h * 3 * HEAD
            raw[:, start : start + HEAD] = dot(grad_raw, key_rows)
            raw[:, start + HEAD : start + 2 * HEAD] = dot_rows(grad_raw, query)
            raw[:, start + 2 * HEAD : start + 3 * HEAD] = dot_rows(low, grad)
        pair = 6 * HEAD
        cosine, left, right = self.tables
        for start in range(0, self.qkv_width, pair):
            value = raw[:, start : start + pair]
            value = (
                value * cosine[...]
                + pltpu.roll(value * left[...], ROT // 2, 1)
                + pltpu.roll(value * right[...], pair - ROT // 2, 1)
            )
            grad_joined[:, start : start + pair] = value.astype(BF)

    def inputs_back(self, grad_joined, grad_pre, hat, grad, sums):
        grad_attn_in = dot_cols(grad_joined[...], self.q_matrix(0, self.qkv_width))
        rows = [
            jnp.sum(grad_attn_in * hat, 0, keepdims=True),
            jnp.sum(grad_attn_in, 0, keepdims=True),
        ]
        grad_hat = grad_attn_in * self.vector(0)
        grad_mlp_in = dot_cols(grad_pre[...], self.u_matrix(0, self.up_width))
        rows += [
            jnp.sum(grad_mlp_in * hat, 0, keepdims=True),
            jnp.sum(grad_mlp_in, 0, keepdims=True),
            jnp.sum(grad[...].astype(F32), 0, keepdims=True) * 0.25,
        ]
        for k, row in enumerate(rows):
            sums[k : k + 1, :] = row
        for k, (ref, width) in enumerate(
            ((grad_joined, self.qkv_width), (grad_pre, self.up_width))
        ):
            sums[5 + k : 6 + k, :] = jnp.zeros((1, D), F32)
            sums[5 + k : 6 + k, :width] = jnp.sum(ref[...].astype(F32), 0, keepdims=True)
        sums[7:8, :] = jnp.zeros((1, D), F32)
        return norm_back(grad_hat + grad_mlp_in * self.vector(2), hat)


def grads_a(left, right, out):
    width = right.shape[1]
    nz = out.shape[0]
    block = left.shape[1] // nz
    for k in range(nz):
        value = dot_rows(left[:, k * block : (k + 1) * block], right[...]).astype(BF)
        out[k] = value.reshape(*out.shape[1:4], width)


def grads_b(left, right, out, low, high):
    zls = out.shape[0]
    block = left.shape[1] // zls
    for k in range(zls):
        value = dot_rows(left[:, k * block : (k + 1) * block], right[...]).astype(BF)
        out[k, :, :, low:high, :] = value.reshape(*out.shape[1:3], high - low, D)


def rows_index(rows):
    def index(lead, target, start, width):
        return (
            pl.ds(pl.multiple_of(target * rows, rows), rows),
            lanes_at(start, width),
        )

    return index


def blocks_index(rows, lanes):
    def index(lead, target, start, width):
        return (
            pl.ds(pl.multiple_of(lax.rem(target, 2) * rows, rows), rows),
            lanes_at((target // 2) * lanes + start, width),
        )

    return index


def group_sum(here, copies, part, index, width, near, far):
    summand = Summand(part, index, None, width, (near.at[0], near.at[1]), (far.at[0], far.at[1]))
    return RingSum(copies, here.y_ring, [summand])


def group_gather(here, copies, whole, rows):
    def view(target, half):
        width = whole.shape[1]
        start, width = (0, width) if half is None else (half * (width // 2), width // 2)
        return whole.at[pl.ds(pl.multiple_of(target * rows, rows), rows), pl.ds(start, width)]

    return RingGather(copies, here.y_ring, [view])


def own_rows(here, rows):
    return pl.ds(pl.multiple_of(here.place * rows, rows), rows)


def ring_scratch(rows, width):
    return [pltpu.VMEM((2, rows, width // 2), BF), pltpu.VMEM((2, rows, width), BF)]


class GradSum:
    def __init__(self, here, cut, copies, kind, g, s, buffers):
        self.here, self.copies, self.kind, self.g, self.s = here, copies, kind, g, s
        self.near, self.far, self.mid, self.top, self.fin = buffers
        rows = g.shape[3]
        first = rows // 2 if kind == "a" else cut
        self.cuts = (pl.ds(0, first), pl.ds(first, rows - first))
        self.full = g.shape[4]
        self.lanes = self.full // 2
        self.lines, self.turns = [None, None], [None, None]

    def start(self):
        self.core = []
        for order in range(2):
            copy = self.copies.to(
                self.g.at[:, :, 1 - self.here.core, self.cuts[order]],
                self.s.at[:, :, self.cuts[order]],
                self.here.partner,
            )
            copy.start()
            self.core.append(copy)

    def line(self, order):
        here, at, zls = self.here, self.cuts[order], self.here.zls
        self.core[order].wait_recv()

        for zz in range(self.s.shape[0]):
            self.s[zz, :, at] = self.s[zz, :, at] + self.g[zz, :, here.core, at]
        nx = self.s.shape[1]
        if order == 0:
            ring, count, width = here.x_ring, self.s.shape[0], self.full

            def index(lead, target, start, width):
                return (lead, target, at, lanes_at(start, width))

        elif self.kind == "a":
            ring, count, width = here.z_ring, nx, self.full

            def index(lead, target, start, width):
                return (target, lead, at, lanes_at(start, width))

        else:
            ring, count, width = here.z_ring, nx, self.lanes

            def index(lead, target, start, width):
                return (
                    lax.rem(target, zls),
                    lead,
                    at,
                    lanes_at((target // zls) * self.lanes + start, width),
                )

        summand = Summand(
            self.s,
            index,
            count,
            width,
            (self.near[order].at[0], self.near[order].at[1]),
            (self.far[order].at[0], self.far[order].at[1]),
        )
        self.lines[order] = RingSum(self.copies, ring, [summand])
        self.lines[order].start()

    def line_middle(self, order):
        self.lines[order].middle()

    def turn(self, order):
        here, zls, mid = self.here, self.here.zls, self.mid[order]
        line = self.lines[order]
        line.end()

        def put(lead):
            mid[lead] = line.total(0, lead).astype(BF)

        over(mid.shape[:1], put)
        ring = here.z_ring if order == 0 else here.x_ring
        if self.kind == "b" and order == 0:

            def index(lead, target, start, width):
                return (
                    lax.rem(target, zls),
                    slice(None),
                    lanes_at((target // zls) * self.lanes + start, width),
                )

        else:

            def index(lead, target, start, width):
                return (target, slice(None), lanes_at(start, width))

        summand = Summand(
            mid,
            index,
            None,
            self.full if self.kind == "a" else self.lanes,
            None,
            [self.top[order].at[k] for k in range(ring.length - 1)],
        )
        self.turns[order] = DirectSum(self.copies, ring, summand)
        self.turns[order].start()

    def end(self, order):
        self.turns[order].end()
        value = self.turns[order].total().astype(BF)
        if self.kind == "a":
            self.fin[order] = value
        else:
            self.fin[self.cuts[order]] = value

    def finish(self):
        for copy in self.core:
            copy.wait_send()
        for order in range(2):
            self.lines[order].finish()
            self.turns[order].finish()


def grad_buffers(grid, cut, g_shape, kind):
    nz, nx, _ = grid
    rows, full = g_shape[3:]
    zls = g_shape[0]
    first = rows // 2 if kind == "a" else cut
    lanes = full if kind == "a" else full // 2
    cuts = (first, rows - first)

    def low(*dims):
        return pltpu.VMEM(dims, BF)

    counts = (zls, nx)
    widths = (full, lanes)
    fin = low(2, first, full) if kind == "a" else low(rows, lanes)
    return [
        low(zls, nx, rows, full),
        *[low(2, counts[o], cuts[o], widths[o] // 2) for o in range(2)],
        *[low(2, counts[o], cuts[o], widths[o]) for o in range(2)],
        *[low(counts[o], cuts[o], widths[o]) for o in range(2)],
        *[low((nz, nx)[o] - 1, cuts[o], lanes) for o in range(2)],
        fin,
    ]


def grad_sum(here, cut, copies, kind, g, refs):
    s, near0, near1, far0, far1, mid0, mid1, top0, top1, fin = refs
    return GradSum(
        here,
        cut,
        copies,
        kind,
        g,
        s,
        ((near0, near1), (far0, far1), (mid0, mid1), (top0, top1), fin),
    )


def lane_iota(rows, lanes):
    return lax.broadcasted_iota(jnp.int32, (rows, lanes), 1)


def make_tables(ids, live, cosine, left, right, mask):
    length = ids.shape[1]
    other = ids[...]
    row = lax.broadcasted_iota(jnp.int32, (length, length), 0)
    column = lax.broadcasted_iota(jnp.int32, (length, length), 1)
    other = jnp.broadcast_to(other.astype(F32), (length, length))
    own = jnp.sum(jnp.where(row == column, other, 0.0), 1, keepdims=True)
    live[...] = jnp.broadcast_to(jnp.where(own < SEQS, 1.0, 0.0), live.shape)
    earlier = jnp.sum((other < own).astype(F32), 1, keepdims=True)
    mask[...] = jnp.where((other == own) & (column <= row), 0.0, MASK_VALUE)
    place = lax.broadcasted_iota(jnp.int32, (length, 1), 0).astype(F32) - earlier
    lane = lane_iota(1, 128)
    at = lax.rem(lane, HEAD)
    turned = at < ROT
    power = lax.rem(at, ROT // 2).astype(F32)
    frequency = jnp.exp(power * (-2.0 / ROT * math.log(ROPE_BASE)))
    angles = place * frequency
    cos_part = jnp.where(turned, jnp.cos(angles), 1.0)
    sin_part = jnp.sin(angles)
    left_part = jnp.where(at < ROT // 2, -sin_part, 0.0)
    right_part = jnp.where(turned & (at >= ROT // 2), sin_part, 0.0)
    low_half = lane < HEAD
    for ref, value, rest in ((cosine, cos_part, 1.0), (left, left_part, 0.0), (right, right_part, 0.0)):
        ref[:, 0:128] = value
        ref[:, 128:256] = jnp.where(low_half, rest, value)
        ref[:, 256:384] = jnp.where(low_half, value, rest)


def make_biases(full_c, bias, widths):
    n_dp = math.prod(full_c.shape[:3])
    table = full_c[...].reshape(n_dp, *full_c.shape[3:])
    lanes = full_c.shape[4]
    for layer in range(LAYERS):
        values = table[:, layer, :].astype(BF)
        first = 0
        for k, width in enumerate(widths):
            total = n_dp * width
            lane = lax.broadcasted_iota(jnp.int32, (lanes, total), 0)
            column = lax.broadcasted_iota(jnp.int32, (lanes, total), 1)
            pick = jnp.where(lane == lax.rem(column, width) + first, 1.0, 0.0).astype(BF)
            spread = dot(values, pick)
            device = lax.broadcasted_iota(jnp.int32, (n_dp, total), 0)
            column = lax.broadcasted_iota(jnp.int32, (n_dp, total), 1)
            mine = jnp.where(column // width == device, spread, 0.0)
            bias[layer * 2 + k : layer * 2 + k + 1, :total] = jnp.sum(mine, 0, keepdims=True)
            first += width


def whole_kernel(grid, cut, sizes, widths, tree, *refs):
    at = SimpleNamespace(**jax.tree.unflatten(tree, refs))
    sends, recvs, local = at.sends, at.recvs, at.local
    here = Slice(grid)
    nz, nx, _ = grid
    copies = Copies(sends, recvs)
    copies.count = 48
    d, r, c, half = here.d, here.row, here.col, here.half
    hid, cot = at.hid, at.cot
    hid_all, cot_all, vec = at.hid_all, at.cot_all, at.vec
    rows, lanes = hid.shape
    quarter = rows // 2
    dh, dl = d // half, lax.rem(d, half)
    swap_needed = dh != r
    swap_to = {"dp": r * half + dl, "row": dh}
    slot_rows = at.qkv_weight.shape[1]
    forth = [{"dp": r * half + d // 2, "row": k} for k in range(2)]
    back_to = [{"dp": 2 * dl + k, "row": dh} for k in range(2)]
    forth_self = [(r == k) & (r * half + d // 2 == d) for k in range(2)]
    back_self = [(dh == r) & (2 * dl + k == d) for k in range(2)]
    slot = lax.rem(d, 2)

    count = here.greet_rings([here.z_ring, here.x_ring, here.y_ring], whole=True)
    greet(here.partner)
    for k in range(2):
        for device, itself in ((forth[k], forth_self[k]), (back_to[k], back_self[k])):

            @pl.when(jnp.logical_not(itself))
            def _():
                greet(device)

    @pl.when(swap_needed)
    def _():
        greet(swap_to)

    qkv_width, up_width, out_rows = sizes
    wa, wb = (at.wq, at.wu), at.wb

    def cast(layer):
        for ref, given, width in ((wa[0], at.qkv_weight, qkv_width), (wa[1], at.up_weight, up_width)):
            for k in range(2):
                ref[layer, k] = given[layer, :, k * width : (k + 1) * width].astype(BF)
        wb[layer, :out_rows] = at.out_weight[layer].astype(BF)
        wb[layer, out_rows:] = at.down_weight[layer].astype(BF)

    cast(0)
    vec_own, wc = at.vec_own, at.wc
    vec_own[...] = jnp.zeros(vec_own.shape, F32)
    for layer in range(LAYERS):
        for k in range(6):
            row = layer * VEC_ROWS + k
            vec_own[row : row + 1] = at.row_vectors[k, layer : layer + 1]
    wc[...] = jnp.zeros(wc.shape, F32)
    wc[:LAYERS, : widths[0]] = at.qkv_bias[...]
    wc[:LAYERS, widths[0] : sum(widths)] = at.up_bias[...]
    greeted(
        count
        + 5
        + swap_needed.astype(jnp.int32)
        - sum(k.astype(jnp.int32) for k in forth_self + back_self)
    )

    def when_else(condition, there, here_do):
        pl.when(condition)(there)
        pl.when(jnp.logical_not(condition))(here_do)

    def pair(src, dst, send, recv, device):
        return pltpu.make_async_remote_copy(
            src_ref=src,
            dst_ref=dst,
            send_sem=sends.at[send],
            recv_sem=recvs.at[recv],
            device_id=device,
            device_id_type=MESH,
        )

    a_own, b_own = (at.q_own, at.u_own), at.b_own
    slot_at = pl.ds(pl.multiple_of(slot * slot_rows, slot_rows), slot_rows)

    def a_copy(layer, kind, k):
        base = layer * 8 + kind * 2
        return pair(
            wa[kind].at[layer, k], a_own[kind].at[layer, slot_at], base + k, base + slot, forth[k]
        )

    def a_arrival(layer, kind, k):
        base = layer * 8 + kind * 2
        into = a_own[kind].at[layer, pl.ds(k * slot_rows, slot_rows)]
        return pair(wa[kind].at[layer, 0], into, base, base + k, back_to[k])

    def a_local(layer, kind, k):
        return pltpu.make_async_copy(
            wa[kind].at[layer, k], a_own[kind].at[layer, slot_at], local.at[24 + layer * 2 + kind]
        )

    def swap_copy(layer):
        return pair(wb.at[layer], b_own.at[layer], layer * 8 + 4, layer * 8 + 4, swap_to)

    def swap_local(layer):
        return pltpu.make_async_copy(wb.at[layer], b_own.at[layer], local.at[28 + layer])

    def begin(layer):
        for kind in range(2):
            for k in range(2):
                when_else(
                    forth_self[k],
                    lambda: a_local(layer, kind, k).start(),
                    lambda: a_copy(layer, kind, k).start(),
                )
        when_else(
            swap_needed, lambda: swap_copy(layer).start(), lambda: swap_local(layer).start()
        )

    def complete_a(layer, kind):
        for k in range(2):
            when_else(
                forth_self[k],
                lambda: a_local(layer, kind, k).wait(),
                lambda: a_copy(layer, kind, k).wait_send(),
            )

            @pl.when(jnp.logical_not(back_self[k]))
            def _():
                a_arrival(layer, kind, k).wait_recv()

    def complete_b(layer):
        when_else(swap_needed, lambda: swap_copy(layer).wait(), lambda: swap_local(layer).wait())

    begin(0)
    tokens = pl.ds(pl.multiple_of(c * rows, rows), rows)
    features = pl.ds(pl.multiple_of(r * lanes, lanes), lanes)
    hid_copies = [
        copies.to(hid, hid_all.at[tokens, features], here.y_ring.device(k)) for k in range(1, 4)
    ]
    cot_copies = [
        copies.to(cot, cot_all.at[tokens, features], here.y_ring.device(k)) for k in range(1, 4)
    ]
    hid_copies.append(copies.to(vec_own, vec.at[:, features], {"row": 1 - r}))
    own = [
        pltpu.make_async_copy(hid, hid_all.at[tokens, features], local.at[36]),
        pltpu.make_async_copy(cot, cot_all.at[tokens, features], local.at[37]),
        pltpu.make_async_copy(vec_own, vec.at[:, features], local.at[38]),
    ]
    for copy in hid_copies + own:
        copy.start()
    tables, mask, bias = (at.cosine, at.left, at.right), at.mask, at.bias
    complete_a(0, 0)

    full = ((at.q_zero, at.u_zero, at.b_zero), (at.q_one, at.u_one, at.b_one))
    full_c = at.full_c
    gathers = []
    for k in range(LAYERS):
        for kind in range(3):
            source = (a_own + (b_own,))[kind].at[k]
            spread = (wc, full_c) if k == 0 and kind == 0 else None
            count = 4 * (3 * k + kind)
            gathers.append(
                WeightGather(
                    here, cut, copies, local.at[pl.ds(count, 4)], source, full[k][kind], spread
                )
            )
    near, late = gathers[:3], gathers[3:]
    near[0].start()
    complete_a(0, 1)
    near[1].start()
    complete_b(0)
    near[2].start()
    make_tables(at.ids, at.live, *tables, mask)
    layers = [
        Layer(k, vec, tables, mask, bias.at[pl.ds(2 * k, 2)], *full[k], sizes)
        for k in range(LAYERS)
    ]
    attn_in, mlp_in, joined, probs = at.attn_in, at.mlp_in, at.joined, at.probs
    heads, slope, units = at.heads, at.slope, at.units
    for one in near:
        one.turn()
    for copy in hid_copies + own:
        copy.wait()
    near[0].second_middle()
    hat, _ = norm_stats(hid_all[...].astype(F32))
    layers[0].inputs(hat, attn_in[0], mlp_in[0])
    near[1].second_middle()
    near[2].second_middle()
    cast(1)
    begin(1)
    for one in near:
        one.end()
    near[0].arrive()
    make_biases(full_c, bias, widths)
    layers[0].project(attn_in[0], joined[0])
    complete_a(1, 0)
    late[0].start()
    complete_a(1, 1)
    late[1].start()
    complete_b(1)
    late[2].start()
    for copy in cot_copies:
        copy.start()
    mine = own_rows(here, quarter)
    layers[0].attend(joined[0], probs[0], heads[0])
    for one in late:
        one.turn()
    near[1].arrive()
    layers[0].units(mlp_in[0], slope[0], units[0])
    near[2].arrive()
    part = at.part[0]
    for start in (0, D // 2):
        part[:, start : start + D // 2] = (
            layers[0].outputs(heads[0], units[0], start, D // 2).astype(BF)
        )
    summed = group_sum(here, copies, part, rows_index(quarter), D, at.near[0], at.far[0])
    summed.start()
    late[0].second_middle()
    summed.middle()
    late[1].second_middle()
    state = hid_all[mine, :].astype(F32) + layers[0].vector(4) + layers[0].vector(5)
    summed.end()
    state = state + summed.total(0)
    at.state[...] = state
    hat, inverse = norm_stats(state)
    inv_std, hat_all = at.inv_std, at.hat_all
    inv_std[...] = jnp.broadcast_to(inverse, inv_std.shape)
    hat_all[mine, :] = hat.astype(BF)
    spread = group_gather(here, copies, hat_all, quarter)
    spread.start()
    grad = (at.grad[0], at.grad[1])
    for copy in cot_copies:
        copy.wait()
    grad[1][...] = (
        cot_all[...].astype(F32) * at.live[:, :1]
    ).astype(BF)
    late[2].second_middle()
    spread.middle()
    for one in late:
        one.end()
    spread.end()
    late[0].arrive()
    rings = [summed, spread]

    grads = [
        full[1],
        (at.gq, at.gu, at.gb),
    ]
    sum_q, sum_u, sum_b = [
        [
            grad_sum(
                here,
                cut,
                copies,
                "aab"[kind],
                grads[k][kind],
                at.sum_buffers[k][kind],
            )
            for k in range(LAYERS)
        ]
        for kind in range(3)
    ]
    out_q, out_u, out_b = at.out_q, at.out_u, at.out_b

    def owner_copy(layer, kind, order):
        out, one = ((out_q, sum_q), (out_u, sum_u))[kind]
        base = 16 + layer * 8 + kind * 2
        return pair(
            one[layer].fin.at[order], out.at[layer, r], base + order, base + r, back_to[order]
        )

    def owner_arrival(layer, kind, k):
        out, one = ((out_q, sum_q), (out_u, sum_u))[kind]
        base = 16 + layer * 8 + kind * 2
        return pair(one[layer].fin.at[0], out.at[layer, k], base, base + k, forth[k])

    def owner_local(layer, kind, order):
        out, one = ((out_q, sum_q), (out_u, sum_u))[kind]
        return pltpu.make_async_copy(
            one[layer].fin.at[order], out.at[layer, r], local.at[30 + layer * 2 + kind]
        )

    def out_swap(layer):
        return pair(sum_b[layer].fin, out_b.at[layer], 20 + layer * 8, 20 + layer * 8, swap_to)

    def out_local(layer):
        return pltpu.make_async_copy(sum_b[layer].fin, out_b.at[layer], local.at[34 + layer])

    def hand_a(layer, kind):
        for order in range(2):
            when_else(
                back_self[order],
                lambda: owner_local(layer, kind, order).start(),
                lambda: owner_copy(layer, kind, order).start(),
            )

    def hand_b(layer):
        when_else(swap_needed, lambda: out_swap(layer).start(), lambda: out_local(layer).start())

    def handed(layer):
        for kind in range(2):
            for k in range(2):
                when_else(
                    back_self[k],
                    lambda: owner_local(layer, kind, k).wait(),
                    lambda: owner_copy(layer, kind, k).wait_send(),
                )

                @pl.when(jnp.logical_not(forth_self[k]))
                def _():
                    owner_arrival(layer, kind, k).wait_recv()

        when_else(swap_needed, lambda: out_swap(layer).wait(), lambda: out_local(layer).wait())

    def phase(step, which):
        for order in range(2):
            for one in which:
                step(one, order)

    layer = layers[1]
    layer.inputs(hat_all[...].astype(F32), attn_in[1], mlp_in[1])
    layer.project(attn_in[1], joined[1])
    layer.attend(joined[1], probs[1], heads[1])
    late[1].arrive()
    layer.units(mlp_in[1], slope[1], units[1])
    late[2].arrive()
    for one in gathers:
        one.finish()
    b_high = at.gb.shape[3]
    grads_b(heads[1], grad[1], grads[1][2], 0, out_rows)
    grads_b(units[1], grad[1], grads[1][2], out_rows, b_high)
    sum_b[1].start()
    part = at.part[1]
    for start in (0, D // 2):
        part[:, start : start + D // 2] = (
            layer.outputs(heads[1], units[1], start, D // 2).astype(BF)
        )
    part[mine, :] = (part[mine, :].astype(F32) + at.state[...]).astype(BF)
    out_sum = group_sum(
        here, copies, part, blocks_index(rows, lanes), lanes, at.near[1], at.far[1]
    )
    out_sum.start()
    grad_heads, grad_pre, raw, grad_joined = at.grad_heads, at.grad_pre, at.raw, at.grad_joined
    sums = at.sums
    layer.branch_back(grad[1], slope[1], grad_heads, grad_pre)
    phase(GradSum.line, [sum_b[1]])
    layer.attend_back(joined[1], probs[1], grad_heads, raw, grad_joined)
    phase(GradSum.line_middle, [sum_b[1]])
    out_sum.middle()
    back = at.back[1]
    back[...] = layer.inputs_back(
        grad_joined, grad_pre, hat_all[...].astype(F32), grad[1], sums[1]
    ).astype(BF)
    summed = group_sum(here, copies, back, rows_index(quarter), D, at.near[2], at.far[2])
    summed.start()
    grads_a(mlp_in[1], grad_pre, grads[1][1])
    sum_u[1].start()
    summed.middle()
    grads_a(attn_in[1], grad_joined, grads[1][0])
    sum_q[1].start()
    summed.end()
    grad_one = at.grad_one
    total = grad[1][mine, :].astype(F32) + inv_std[:, :1] * summed.total(0)
    grad_one[...] = total
    grad[0][mine, :] = total.astype(BF)
    spread = group_gather(here, copies, grad[0], quarter)
    spread.start()
    phase(GradSum.line, [sum_u[1]])
    spread.middle()
    phase(GradSum.turn, [sum_b[1]])
    phase(GradSum.line, [sum_q[1]])
    out_sum.end()
    first_bias = vec[VEC_ROWS + 4 : VEC_ROWS + 5, features]
    bias_sum = first_bias + vec[VEC_ROWS + 5 : VEC_ROWS + 6, features]
    at.hidden[...] = (out_sum.total(0) + bias_sum).astype(BF)
    phase(GradSum.line_middle, [sum_u[1]])
    spread.end()
    rings += [out_sum, summed, spread]

    def conclude(layer_index, one, kind):
        for order in range(2):
            one.end(order)
        if kind == 2:
            hand_b(layer_index)
        else:
            hand_a(layer_index, kind)

    layer = layers[0]
    grads_b(heads[0], grad[0], grads[0][2], 0, out_rows)
    grads_b(units[0], grad[0], grads[0][2], out_rows, b_high)
    sum_b[0].start()
    phase(GradSum.line_middle, [sum_q[1]])
    layer.branch_back(grad[0], slope[0], grad_heads, grad_pre)
    conclude(1, sum_b[1], 2)
    phase(GradSum.turn, [sum_u[1]])
    phase(GradSum.line, [sum_b[0]])
    grads_a(mlp_in[0], grad_pre, grads[0][1])
    sum_u[0].start()
    phase(GradSum.turn, [sum_q[1]])
    layer.attend_back(joined[0], probs[0], grad_heads, raw, grad_joined)
    phase(GradSum.line_middle, [sum_b[0]])
    grads_a(attn_in[0], grad_joined, grads[0][0])
    sum_q[0].start()
    phase(GradSum.line, [sum_u[0]])
    hat, inverse = norm_stats(hid_all[...].astype(F32))
    value = layer.inputs_back(grad_joined, grad_pre, hat, grad[0], sums[0])
    back = at.back[0]
    back[...] = (inverse * value).astype(BF)
    back[mine, :] = (back[mine, :].astype(F32) + grad_one[...]).astype(BF)
    summed = group_sum(
        here, copies, back, blocks_index(rows, lanes), lanes, at.near[3], at.far[3]
    )
    summed.start()
    phase(GradSum.line, [sum_q[0]])
    v_core, v_line, v_last, v_group = at.v_core, at.v_line, at.v_last, at.v_group
    v_lanes = D // 2
    v_mine = pl.ds(pl.multiple_of(here.core * v_lanes, v_lanes), v_lanes)
    v_other = pl.ds(pl.multiple_of((1 - here.core) * v_lanes, v_lanes), v_lanes)
    v_copies = [copies.to(sums[k].at[:, v_other], v_core.at[k], here.partner) for k in range(2)]
    for copy in v_copies:
        copy.start()
    phase(GradSum.line_middle, [sum_u[0]])
    summed.middle()
    conclude(1, sum_u[1], 1)
    conclude(1, sum_q[1], 0)
    phase(GradSum.turn, [sum_b[0]])
    for copy in v_copies:
        copy.wait()
    for k in range(LAYERS):
        v_line[here.x, k * VEC_ROWS : (k + 1) * VEC_ROWS] = v_core[k] + sums[k][:, v_mine]
    v_x = [
        copies.to(v_line.at[here.x], v_line.at[here.x], here.x_ring.device(k))
        for k in range(1, nx)
    ]
    for copy in v_x:
        copy.start()
    phase(GradSum.line_middle, [sum_q[0]])
    phase(GradSum.turn, [sum_u[0]])
    summed.end()
    at.grad_out[...] = summed.total(0)
    rings.append(summed)
    for copy in v_x:
        copy.wait()
    total = v_line[0]
    for k in range(1, nx):
        total = total + v_line[k]
    v_last[here.z] = total
    v_z = [
        copies.to(v_last.at[here.z], v_last.at[here.z], here.z_ring.device(k))
        for k in range(1, nz)
    ]
    for copy in v_z:
        copy.start()
    phase(GradSum.turn, [sum_q[0]])
    conclude(0, sum_b[0], 2)
    for copy in v_z:
        copy.wait()
    total = v_last[0]
    for k in range(1, nz):
        total = total + v_last[k]
    v_group[here.place] = total
    v_y = [
        copies.to(v_group.at[here.place], v_group.at[here.place], here.y_ring.device(k))
        for k in range(1, 4)
    ]
    for copy in v_y:
        copy.start()
    conclude(0, sum_u[0], 1)
    for copy in v_y:
        copy.wait()
    total = v_group[0]
    for k in range(1, 4):
        total = total + v_group[k]
    out_v = at.out_v
    out_v[0, :, v_mine] = total
    out_v[1, :, v_mine] = v_group[here.place]
    v_swap = copies.to(out_v.at[:, :, v_mine], out_v.at[:, :, v_mine], here.partner)
    v_swap.start()
    conclude(0, sum_q[0], 0)
    v_swap.wait()
    handed(1)
    handed(0)
    assert copies.count <= sends.shape[0], copies.count
    for ring in rings:
        ring.finish()
    for one in sum_q + sum_u + sum_b:
        one.finish()


def whole(grid, cut, sizes, widths, ins):
    nz, nx, nc = grid
    qkv_width, up_width, out_rows = sizes
    rows, lanes = ins["hid"].shape
    group, quarter = 2 * rows, rows // 2
    slot_rows, down_rows = ins["qkv_weight"].shape[1], ins["down_weight"].shape[1]
    b_rows = out_rows + down_rows
    heads_here = qkv_width // (3 * HEAD)

    def low(*dims):
        return pltpu.VMEM(dims, BF)

    def high(*dims):
        return pltpu.VMEM(dims, F32)

    def twice(make, *dims):
        return [make(*dims) for _ in range(LAYERS)]

    shape = jax.ShapeDtypeStruct
    outs = dict(
        hidden=shape((rows, lanes), BF),
        grad_out=shape((rows, lanes), F32),
        out_q=shape((LAYERS, 2, slot_rows, qkv_width), BF),
        out_u=shape((LAYERS, 2, slot_rows, up_width), BF),
        out_b=shape((LAYERS, b_rows, lanes), BF),
        out_v=shape((2, LAYERS * VEC_ROWS, D), F32),
    )
    q_shape = (nz, nx, nc, 2 * slot_rows, qkv_width)
    u_shape = (nz, nx, nc, 2 * slot_rows, up_width)
    b_shape = (nz // 2, nx, nc, b_rows, 2 * lanes)
    c_shape = (8, -(-sum(widths) // 128) * 128)
    kinds = ((q_shape, "a"), (u_shape, "a"), (b_shape, "b"))
    blocks = [ring_scratch(quarter, D), ring_scratch(rows, lanes)] * 2
    scratch = dict(
        hid_all=low(group, D),
        cot_all=low(group, D),
        vec=high(LAYERS * VEC_ROWS, D),
        vec_own=high(LAYERS * VEC_ROWS, lanes),
        wq=low(LAYERS, 2, slot_rows, qkv_width),
        wu=low(LAYERS, 2, slot_rows, up_width),
        wb=low(LAYERS, b_rows, lanes),
        wc=high(*c_shape),
        q_own=low(LAYERS, 2 * slot_rows, qkv_width),
        u_own=low(LAYERS, 2 * slot_rows, up_width),
        b_own=low(LAYERS, b_rows, lanes),
        q_zero=low(*q_shape),
        q_one=low(*q_shape),
        u_zero=low(*u_shape),
        u_one=low(*u_shape),
        b_zero=low(*b_shape),
        b_one=low(*b_shape),
        full_c=high(nz, nx, nc, *c_shape),
        cosine=high(group, 6 * HEAD),
        left=high(group, 6 * HEAD),
        right=high(group, 6 * HEAD),
        mask=high(group, group),
        live=high(group, 128),
        bias=high(2 * LAYERS, D),
        state=high(quarter, D),
        inv_std=high(quarter, 128),
        hat_all=low(group, D),
        grad_one=high(quarter, D),
        grad_heads=low(group, heads_here * HEAD),
        grad_pre=low(group, up_width),
        raw=high(group, qkv_width),
        grad_joined=low(group, qkv_width),
        gq=low(*q_shape),
        gu=low(*u_shape),
        gb=low(*b_shape),
        v_core=high(2, VEC_ROWS, D // 2),
        v_line=high(nx, LAYERS * VEC_ROWS, D // 2),
        v_last=high(nz, LAYERS * VEC_ROWS, D // 2),
        v_group=high(4, LAYERS * VEC_ROWS, D // 2),
        attn_in=twice(low, group, D),
        mlp_in=twice(low, group, D),
        joined=twice(low, group, qkv_width),
        probs=twice(low, heads_here, group, group),
        heads=twice(low, group, heads_here * HEAD),
        slope=twice(low, group, up_width),
        units=twice(low, group, up_width),
        part=twice(low, group, D),
        back=twice(low, group, D),
        grad=twice(low, group, D),
        sums=twice(high, VEC_ROWS, D),
        sum_buffers=[
            [grad_buffers(grid, cut, dims, kind) for dims, kind in kinds] for _ in range(LAYERS)
        ],
        near=[block[0] for block in blocks],
        far=[block[1] for block in blocks],
        sends=pltpu.SemaphoreType.DMA((480,)),
        recvs=pltpu.SemaphoreType.DMA((480,)),
        local=pltpu.SemaphoreType.DMA((40,)),
    )
    flat = jax.tree.leaves(scratch)
    tree = jax.tree.structure(dict(**ins, **outs, **scratch))
    order = [*ins.values(), *outs.values(), *scratch.values()]
    names = [*ins, *outs, *scratch]
    ranks = jax.tree.unflatten(
        jax.tree.structure(dict(zip(names, order))), range(tree.num_leaves)
    )
    given = jax.tree.leaves([ranks[name] for name in names])

    def kernel(*refs):
        placed = [None] * len(refs)
        for rank, ref in zip(given, refs):
            placed[rank] = ref
        whole_kernel(grid, cut, sizes, widths, tree, *placed)

    flat = jax.tree.leaves(list(scratch.values()))
    return pl.pallas_call(
        kernel,
        out_shape=tuple(outs.values()),
        in_specs=[VMEM_SPEC] * len(ins),
        out_specs=(VMEM_SPEC,) * len(outs),
        scratch_shapes=flat,
        compiler_params=params(0, 63),
        name="whole_step",
    )(*ins.values())


def update_kernel(n_dp, bias_widths, out_rows, *refs):
    given, refs = refs[:27], refs[27:]
    results, refs = refs[:23], refs[23:]
    held, made, in_sems, out_sems = refs[:27], refs[27:48], refs[48], refs[49]
    d, r = lax.axis_index("dp"), lax.axis_index("row")
    loads = [
        pltpu.make_async_copy(src, dst, in_sems.at[k])
        for k, (src, dst) in enumerate(zip(given, held))
    ]
    stores = [
        pltpu.make_async_copy(src, dst, out_sems.at[k])
        for k, (src, dst) in enumerate(zip((*made, *held[25:]), results))
    ]
    for copy in loads:
        copy.start()
    own_q, own_u, own_b, all_v = held[:4]
    old = held[4:25]
    for copy in loads[:4]:
        copy.wait()

    def update(k, at, gradient, rate, decay):
        values = adamw(*[ref[at] for ref in old[3 * k : 3 * k + 3]], gradient, rate, decay)
        for ref, value in zip(made[3 * k : 3 * k + 3], values):
            ref[at] = value

    def begin(k):
        for copy in loads[4 + 3 * k : 7 + 3 * k]:
            copy.wait()

    def finish(k):
        for copy in stores[3 * k : 3 * k + 3]:
            copy.start()

    for k, own in ((0, own_q), (2, own_u)):
        begin(k)
        width = own.shape[3]
        for layer in range(LAYERS):
            for side in range(2):
                at = (layer, slice(None), slice(side * width, (side + 1) * width))
                update(k, at, own[layer, side].astype(F32), RATE_MATRIX, DECAY_MATRIX)
        finish(k)
    for k, rows in ((1, slice(0, out_rows)), (3, slice(out_rows, None))):
        begin(k)
        update(k, ..., own_b[:, rows].astype(F32), RATE_MATRIX, DECAY_MATRIX)
        finish(k)
    for k, width in enumerate(bias_widths):
        begin(4 + k)
        for layer in range(LAYERS):
            rows = all_v[1, layer * VEC_ROWS : (layer + 1) * VEC_ROWS, :]
            moved = pltpu.roll(rows, lax.rem(D - d * width, D), 1)
            at = (slice(layer, layer + 1), slice(None))
            update(4 + k, at, moved[5 + k : 6 + k, :width], RATE_MATRIX, 0.0)
        finish(4 + k)
    lanes = old[18].shape[2]
    features = pl.ds(pl.multiple_of(r * lanes, lanes), lanes)
    begin(6)
    for layer in range(LAYERS):
        for k in range(6):
            row = layer * VEC_ROWS + min(k, 4)
            at = (k, slice(layer, layer + 1), slice(None))
            update(6, at, all_v[0, row : row + 1, features], RATE_VECTOR, 0.0)
    finish(6)
    for load, store in zip(loads[25:], stores[21:]):
        load.wait()
        store.start()
    for copy in stores:
        copy.wait()


def update_all(n_dp, bias_widths, out_rows, passed, gradients, old):
    anywhere = pl.BlockSpec(memory_space=pl.ANY)
    given = (*gradients, *old, *passed)
    return pl.pallas_call(
        partial(update_kernel, n_dp, bias_widths, out_rows),
        out_shape=tuple(jax.ShapeDtypeStruct(a.shape, a.dtype) for a in (*old, *passed)),
        in_specs=[anywhere] * len(given),
        out_specs=(anywhere,) * (len(old) + len(passed)),
        scratch_shapes=[
            *[pltpu.VMEM(a.shape, a.dtype) for a in given],
            *[pltpu.VMEM(a.shape, F32) for a in old],
            pltpu.SemaphoreType.DMA((len(given),)),
            pltpu.SemaphoreType.DMA((len(old) + len(passed),)),
        ],
        compiler_params=pltpu.CompilerParams(vmem_limit_bytes=60 << 20),
        name="update_all",
    )(*given)


def on_device(
    hidden_in,
    cotangent,
    seq_ids,
    qkv_weight,
    qkv_first,
    qkv_second,
    out_weight,
    out_first,
    out_second,
    up_weight,
    up_first,
    up_second,
    down_weight,
    down_first,
    down_second,
    qkv_bias,
    qkv_bias_first,
    qkv_bias_second,
    up_bias,
    up_bias_first,
    up_bias_second,
    row_vectors,
    row_first,
    row_second,
):
    n_dp = lax.axis_size("dp")
    grid = GRIDS[n_dp]
    group_len = seq_ids.shape[0]
    qkv_width, up_width = qkv_weight.shape[2] // 2, up_weight.shape[2] // 2
    out_rows, down_rows = out_weight.shape[1], down_weight.shape[1]
    bias_widths = qkv_bias.shape[1], up_bias.shape[1]
    cut = out_rows + down_rows // 2
    sizes = (qkv_width, up_width, out_rows)

    ins = dict(
        hid=hidden_in,
        cot=cotangent,
        ids=seq_ids.reshape(1, group_len),
        row_vectors=row_vectors.transpose(1, 0, 2),
        qkv_bias=qkv_bias,
        up_bias=up_bias,
        qkv_weight=qkv_weight,
        out_weight=out_weight,
        up_weight=up_weight,
        down_weight=down_weight,
    )
    *passed, own_q, own_u, own_b, all_v = whole(grid, cut, sizes, bias_widths, ins)
    gradients = (own_q, own_u, own_b, all_v)
    old = (
        qkv_weight,
        qkv_first,
        qkv_second,
        out_weight,
        out_first,
        out_second,
        up_weight,
        up_first,
        up_second,
        down_weight,
        down_first,
        down_second,
        qkv_bias,
        qkv_bias_first,
        qkv_bias_second,
        up_bias,
        up_bias_first,
        up_bias_second,
        row_vectors.transpose(1, 0, 2),
        row_first.transpose(1, 0, 2),
        row_second.transpose(1, 0, 2),
    )
    *new, row_new, row_one, row_two, hidden_out, grad_state = update_all(
        n_dp, bias_widths, out_rows, passed, gradients, old
    )
    rows = [a.transpose(1, 0, 2) for a in (row_new, row_one, row_two)]
    return hidden_out, grad_state, *new, *rows


def solution(mesh):
    placed = (
        P(("dp", "col"), "row"),
        P(("dp", "col"), "row"),
        P("dp"),
        P(None, ("row", "dp"), "col"),
        P(None, ("row", "dp"), "col"),
        P(None, ("row", "dp"), "col"),
        P(None, ("col", "dp"), "row"),
        P(None, ("col", "dp"), "row"),
        P(None, ("col", "dp"), "row"),
        P(None, ("row", "dp"), "col"),
        P(None, ("row", "dp"), "col"),
        P(None, ("row", "dp"), "col"),
        P(None, ("col", "dp"), "row"),
        P(None, ("col", "dp"), "row"),
        P(None, ("col", "dp"), "row"),
        P(None, ("col", "row", "dp")),
        P(None, ("col", "row", "dp")),
        P(None, ("col", "row", "dp")),
        P(None, ("col", "row", "dp")),
        P(None, ("col", "row", "dp")),
        P(None, ("col", "row", "dp")),
        P(None, None, "row"),
        P(None, None, "row"),
        P(None, None, "row"),
    )
    return jax.shard_map(
        on_device,
        mesh=mesh,
        in_specs=placed,
        out_specs=(
            P(("dp", "col"), "row"),
            P(("dp", "col"), "row"),
            P(None, ("row", "dp"), "col"),
            P(None, ("row", "dp"), "col"),
            P(None, ("row", "dp"), "col"),
            P(None, ("col", "dp"), "row"),
            P(None, ("col", "dp"), "row"),
            P(None, ("col", "dp"), "row"),
            P(None, ("row", "dp"), "col"),
            P(None, ("row", "dp"), "col"),
            P(None, ("row", "dp"), "col"),
            P(None, ("col", "dp"), "row"),
            P(None, ("col", "dp"), "row"),
            P(None, ("col", "dp"), "row"),
            P(None, ("col", "row", "dp")),
            P(None, ("col", "row", "dp")),
            P(None, ("col", "row", "dp")),
            P(None, ("col", "row", "dp")),
            P(None, ("col", "row", "dp")),
            P(None, ("col", "row", "dp")),
            P(None, None, "row"),
            P(None, None, "row"),
            P(None, None, "row"),
        ),
        check_vma=False,
    )
```
